32 devices in a mesh: dp: 16 (over z, x, core), own: 2 (over y).
Axes of the slice: x: 2, y: 2, z: 4, core: 2. Of those that a mesh axis runs over, the one named last changes fastest.
Arguments:
- latents: bfloat16 [64, 1024, 384], P(('dp', 'own')), may hold values from -6 to 6
- condition: bfloat16 [64, 384], P(('dp', 'own')), may hold values from -6 to 6
- cotangent: bfloat16 [64, 1024, 384], P(('dp', 'own')), may hold values from -6 to 6
- owner: int32 [18], replicated, may hold values from 0 to 1, as said below
- master: float32 [20, 384, 384], P('own')
- stat_left: float32 [20, 384, 384], P('own'), as said below
- stat_right: float32 [20, 384, 384], P('own'), as said below
- root_left: float32 [20, 384, 384], P('own'), as said below
- root_right: float32 [20, 384, 384], P('own'), as said below
- bias: float32 [5760], replicated, may hold values from -1.2 to 1.2
- moment_one: float32 [5760], replicated, may hold values from -51.2 to 51.2
- moment_two: float32 [5760], replicated, may hold values from 308.0192 to 1245.184
Outputs:
- block_out: bfloat16 [64, 1024, 384], P(('dp', 'own'))
- latents_grad: float32 [64, 1024, 384], P(('dp', 'own'))
- condition_grad: float32 [64, 384], P(('dp', 'own'))
- weight_grads: float32 [20, 384, 384], P('own')
- stat_left_new: float32 [20, 384, 384], P('own')
- stat_right_new: float32 [20, 384, 384], P('own')
- master_new: float32 [20, 384, 384], P('own')
- bias_grad: float32 [5760], replicated
- moment_one_new: float32 [5760], replicated
- moment_two_new: float32 [5760], replicated
- bias_new: float32 [5760], replicated
The draws below stay inside these ranges and needn't reach their ends.
Inputs may be any that keep to these rules, and one draw needn't show every extreme that they name: owner[b] is the device along own that keeps block b; no device keeps more than 10 blocks, and some device keeps exactly 10. `stat_left`: each matrix is symmetric. `stat_right`: each matrix is symmetric. `root_left`: each matrix is symmetric. `root_right`: each matrix is symmetric.
All inputs are finite; a program needn't handle non-finite values.
Results may differ from the reference program's by a relative error of at most 0.015.
The reference program's roundings to bfloat16 on the way count: a program that leaves them out, or rounds other values in their place, can miss the bound.
Values may be sent and summed in bfloat16 or wider, within the bound.
No kernel may reach another device: no remote copies, remote signals or barrier semaphores. Data moves between devices by JAX's collectives and lax.ppermute only.
A program may use at most 256 MiB of HBM per device.

```python
import math
import jax
import jax.numpy as jnp
from jax import lax

D = 384
H = 6
HD = 64
FF = 1536
LEN = 1024
STEP = 10
SEQS = 64
NBLK = 18
SLOTS = 10
N_OWN = 2


def owner_table(key):
    base = jax.random.fold_in(key, 7)
    first_key, second_key, third_key = jax.random.split(base, 3)
    total = N_OWN * SLOTS
    busiest = jax.random.randint(first_key, (), 0, N_OWN)
    scores = jax.random.permutation(second_key, total).astype(jnp.int32)
    places = jnp.arange(total, dtype=jnp.int32)
    scores = scores + jnp.where(places // SLOTS == busiest, total, 0).astype(jnp.int32)
    chosen = jnp.argsort(-scores, stable=True)[:NBLK]
    shuffle = jax.random.permutation(third_key, NBLK)
    return (chosen[shuffle] // SLOTS).astype(jnp.int32)


def slot_places_drawn(owner):
    order = jnp.arange(NBLK, dtype=jnp.int32)
    before = (order[None, :] < order[:, None]) & (owner[None, :] == owner[:, None])
    return (owner * SLOTS + jnp.sum(before.astype(jnp.int32), axis=1)).astype(jnp.int32)


def block_scales():
    ffn_blocks = FF // D
    return jnp.concatenate([jnp.full((3,), D ** (-0.5), jnp.float32), jnp.full((1,), 10.0 * D ** (-0.5), jnp.float32), jnp.full((ffn_blocks,), D ** (-0.5), jnp.float32), jnp.full((ffn_blocks,), FF ** (-0.5), jnp.float32), jnp.full((6,), D ** (-0.5), jnp.float32)])


def draw_owner(key, part):
    table = owner_table(key)
    return table


def draw_master(key, part):
    table = owner_table(key)
    key = jax.random.fold_in(key, 2)
    places = slot_places_drawn(table)
    spread = jnp.full((N_OWN * SLOTS,), D ** (-0.5), jnp.float32).at[places].set(block_scales())
    return jax.random.normal(key, (N_OWN * SLOTS, D, D), jnp.float32) * spread[:, None, None]


def statistic_draw(key, level):
    first_key, second_key = jax.random.split(key)
    diagonal = level * jnp.exp(jax.random.uniform(first_key, (N_OWN * SLOTS, D), jnp.float32, 0.0, math.log(4.0)))
    noise = jax.random.normal(second_key, (N_OWN * SLOTS, D, D), jnp.float32)
    symmetric = (noise + jnp.transpose(noise, (0, 2, 1))) * (0.35 * level * D ** (-0.5))
    return symmetric + diagonal[:, :, None] * jnp.eye(D, dtype=jnp.float32)[None]


def root_draw(key, level):
    first_key, second_key = jax.random.split(key)
    factor = level ** (-0.25)
    diagonal = factor * jnp.exp(jax.random.uniform(first_key, (N_OWN * SLOTS, D), jnp.float32, math.log(0.4), math.log(4.0)))
    noise = jax.random.normal(second_key, (N_OWN * SLOTS, D, D), jnp.float32)
    symmetric = (noise + jnp.transpose(noise, (0, 2, 1))) * (0.03 * factor)
    return symmetric + diagonal[:, :, None] * jnp.eye(D, dtype=jnp.float32)[None]


def draw_stat_left(key, part):
    key = jax.random.fold_in(key, 3)
    return statistic_draw(key, D * 0.75 * SEQS * LEN)


def draw_stat_right(key, part):
    key = jax.random.fold_in(key, 4)
    return statistic_draw(key, D * 0.75 * SEQS * LEN)


def draw_root_left(key, part):
    key = jax.random.fold_in(key, 5)
    return root_draw(key, D * 0.75 * SEQS * LEN)


def draw_root_right(key, part):
    key = jax.random.fold_in(key, 6)
    return root_draw(key, D * 0.75 * SEQS * LEN)


def level_of(rng, shape, cuts, low, top_value):
    gain = 1.0
    for axis_at, parts in cuts:
        steps = jax.random.uniform(jax.random.fold_in(jax.random.fold_in(rng, 6), axis_at), (parts,), jnp.float32, low / len(cuts), top_value / len(cuts))
        gain = gain * jnp.repeat(jnp.exp(steps), shape[axis_at] // parts).reshape((-1,) + (1,) * (len(shape) - 1 - axis_at))
    return gain


def normal_values(rng, dims, width, limit, cuts=(), held_as=jnp.bfloat16):
    values = jax.random.normal(rng, dims, jnp.float32) * width
    if len(cuts) > 0:
        values = level_of(rng, dims, cuts, -0.22, 0.18) * values
    return jnp.clip(values, min=-limit, max=limit).astype(held_as)


def setup_inputs(seed: int = 0) -> dict:
    key_list = jax.random.split(jax.random.key(seed), 13)
    latents = normal_values(key_list[0], (SEQS, LEN, D), 1.0, 6.0, ((0, 32),))
    condition = normal_values(key_list[1], (SEQS, D), 1.0, 6.0, ((0, 32),))
    cotangent = normal_values(key_list[2], (SEQS, LEN, D), 1.0, 6.0, ((0, 32),))
    owner = draw_owner(jax.random.fold_in(key_list[12], 71), 0)
    master = draw_master(jax.random.fold_in(key_list[12], 71), 0)
    stat_left = draw_stat_left(jax.random.fold_in(key_list[12], 71), 0)
    stat_right = draw_stat_right(jax.random.fold_in(key_list[12], 71), 0)
    root_left = draw_root_left(jax.random.fold_in(key_list[12], 71), 0)
    root_right = draw_root_right(jax.random.fold_in(key_list[12], 71), 0)
    bias = normal_values(key_list[9], (11 * D + FF,), 0.2, 1.2, (), jnp.float32)
    moment_one = normal_values(key_list[10], (11 * D + FF,), (0.033 * (SEQS * LEN) ** 0.5), 51.2, (), jnp.float32)
    moment_two = jnp.clip(jnp.exp(jax.random.uniform(key_list[11], (11 * D + FF,), jnp.float32, math.log(308.0192), math.log(1245.184))), 308.0192, 1245.184)
    return dict(latents=latents, condition=condition, cotangent=cotangent, owner=owner, master=master, stat_left=stat_left, stat_right=stat_right, root_left=root_left, root_right=root_right, bias=bias, moment_one=moment_one, moment_two=moment_two)


highest = lax.Precision.HIGHEST
norm_eps = 1e-06
shampoo_rate = 1.0
shampoo_decay = 0.01
adam_rate = 0.2
adam_decay = 0.01

@jax.custom_vjp
def low(v):
    return lax.optimization_barrier(v.astype(jnp.bfloat16)).astype(jnp.float32)

@jax.custom_vjp
def low_back(v):
    return v

def low_keep(v):
    return (low(v), None)

def low_pass(kept, grad):
    return (grad,)

def back_keep(v):
    return (v, None)

def back_low(kept, grad):
    return (low(grad),)
low.defvjp(low_keep, low_pass)
low_back.defvjp(back_keep, back_low)

def slot_places(owner):
    order = jnp.arange(NBLK, dtype=jnp.int32)
    before = (order[None, :] < order[:, None]) & (owner[None, :] == owner[:, None])
    return (owner * SLOTS + lax.optimization_barrier(jnp.sum(before.astype(jnp.int32), axis=1))).astype(jnp.int32)

def column_blocks(blocks):
    return jnp.transpose(blocks, (1, 0, 2)).reshape(blocks.shape[1], blocks.shape[0] * blocks.shape[2])

def layer_norm(value):
    centered = value - lax.optimization_barrier(jnp.mean(value, axis=-1, keepdims=True))
    return centered * lax.rsqrt(lax.optimization_barrier(jnp.mean(centered * centered, axis=-1, keepdims=True)) + norm_eps)

def forward(blocks, bias, latents, condition):
    weights = low(blocks)
    ffn_blocks = FF // D
    weight_qkv = column_blocks(weights[0:3])
    weight_proj = weights[3]
    weight_up = column_blocks(weights[4:4 + ffn_blocks])
    weight_down = weights[4 + ffn_blocks:4 + 2 * ffn_blocks].reshape(FF, D)
    weight_ada = column_blocks(weights[4 + 2 * ffn_blocks:])
    bias_qkv = bias[0:3 * D]
    bias_proj = bias[3 * D:4 * D]
    bias_up = bias[4 * D:4 * D + FF]
    bias_down = bias[4 * D + FF:5 * D + FF]
    bias_ada = bias[5 * D + FF:]
    silu_cond = low(jax.nn.silu(condition))
    modulation = low_back(jnp.dot(silu_cond, weight_ada, precision=highest) + bias_ada)
    pieces = [modulation[:, None, j * D:(j + 1) * D] for j in range(6)]
    shift_one, scale_one, gate_one, shift_two, scale_two, gate_two = pieces
    bundle = latents.shape[0]
    first_in = low(layer_norm(latents) * (1.0 + scale_one) + shift_one)
    qkv_low = low(low_back(jnp.einsum('gld,de->gle', first_in, weight_qkv, precision=highest) + bias_qkv))
    columns = qkv_low.reshape(bundle, LEN, 3, H, HD)
    query, keys, values = (columns[:, :, 0], columns[:, :, 1], columns[:, :, 2])
    scores = low_back(jnp.einsum('gqhd,gkhd->ghqk', query, keys, precision=highest)) * HD ** (-0.5)
    expo_scores = jnp.exp(scores - lax.optimization_barrier(jnp.max(scores, axis=-1, keepdims=True)))
    probabilities = expo_scores / lax.optimization_barrier(jnp.sum(expo_scores, axis=-1, keepdims=True))
    attn_mixed = low(low_back(jnp.einsum('ghqk,gkhd->gqhd', low(probabilities), values, precision=highest)))
    attn_mixed = attn_mixed.reshape(bundle, LEN, D)
    attn_out = low_back(jnp.einsum('gld,de->gle', attn_mixed, weight_proj, precision=highest) + bias_proj)
    residual = latents + gate_one * attn_out
    second_in = low(layer_norm(residual) * (1.0 + scale_two) + shift_two)
    hidden_pre = low_back(jnp.einsum('gld,df->glf', second_in, weight_up, precision=highest) + bias_up)
    hidden_act = low(jax.nn.gelu(hidden_pre, approximate=True))
    ffn_out = low_back(jnp.einsum('glf,fd->gld', hidden_act, weight_down, precision=highest) + bias_down)
    return residual + gate_two * ffn_out

def reference(latents, condition, cotangent, owner, master, stat_left, stat_right, root_left, root_right, bias, moment_one, moment_two):
    places = slot_places(owner)
    blocks = master[places]
    bundle = 4
    rounds = SEQS // bundle
    batch_latents = latents.astype(jnp.float32).reshape(rounds, bundle, LEN, D)
    batch_cond = condition.astype(jnp.float32).reshape(rounds, bundle, D)
    batch_back = cotangent.astype(jnp.float32).reshape(rounds, bundle, LEN, D)

    def accumulate(carry, entries):
        these_latents, these_cond, these_back = entries
        outputs, pullback = jax.vjp(forward, blocks, bias, these_latents, these_cond)
        grad_blocks, grad_bias, grad_latents, grad_cond = pullback(these_back)
        return ((carry[0] + grad_blocks, carry[1] + grad_bias), (outputs.astype(jnp.bfloat16), grad_latents, grad_cond))
    start = (jnp.zeros(blocks.shape, jnp.float32), jnp.zeros(bias.shape, jnp.float32))
    sums, stacked = lax.scan(accumulate, start, (batch_latents, batch_cond, batch_back))
    block_grads, bias_grad = sums
    block_out = stacked[0].reshape(SEQS, LEN, D)
    latents_grad = stacked[1].reshape(SEQS, LEN, D)
    condition_grad = stacked[2].reshape(SEQS, D)
    weight_grads = jnp.zeros((N_OWN * SLOTS, D, D), jnp.float32).at[places].set(block_grads)

    def renew(entries):
        gradient, left_stat, right_stat, left_root, right_root, weight = entries
        left_new = 0.5 * left_stat + 0.5 * jnp.dot(gradient, gradient.T, precision=highest)
        right_new = 0.5 * right_stat + 0.5 * jnp.dot(gradient.T, gradient, precision=highest)
        direction = jnp.dot(jnp.dot(left_root, gradient, precision=highest), right_root, precision=highest)
        scaled = jnp.sqrt(jnp.mean(weight * weight) + norm_eps) * direction * lax.rsqrt(jnp.mean(direction * direction) + norm_eps)
        return (left_new, right_new, weight - shampoo_rate * (scaled + shampoo_decay * weight))
    stat_left_new, stat_right_new, master_new = lax.map(renew, (weight_grads, stat_left, stat_right, root_left, root_right, master))
    moment_one_new = 0.9 * moment_one + 0.1 * bias_grad
    moment_two_new = 0.95 * moment_two + 0.05 * bias_grad * bias_grad
    corrected = moment_one_new / (1.0 - 0.9 ** STEP) / (jnp.sqrt(moment_two_new / (1.0 - 0.95 ** STEP)) + 1e-08)
    bias_new = bias - adam_rate * (corrected + adam_decay * bias)
    return (block_out, latents_grad, condition_grad, weight_grads, stat_left_new, stat_right_new, master_new, bias_grad, moment_one_new, moment_two_new, bias_new)
```

```python
import functools

import jax
import jax.numpy as jnp
from jax import lax
from jax.experimental import pallas as pl
from jax.experimental.pallas import tpu as pltpu
from jax.sharding import PartitionSpec as P

D = 384
H = 6
HD = 64
FF = 1536
FB = FF // D
STEP = 10
HALF = D // 2
LATE = 4
EARLY = 2 * FB

norm_eps = 1e-06
shampoo_rate = 1.0
shampoo_decay = 0.01
adam_rate = 0.2
adam_decay = 0.01
f32 = jnp.float32
bf16 = jnp.bfloat16
VMEM = 56 * 1024 * 1024

NN = (((1,), (0,)), ((), ()))
NT = (((1,), (1,)), ((), ()))
TN = (((0,), (0,)), ((), ()))


def dot(left, right, dims=NN):
    return lax.dot_general(left, right, dims, preferred_element_type=f32)


def cost(flops, moved, trans=0):
    return pl.CostEstimate(flops=int(flops), bytes_accessed=int(moved), transcendentals=int(trans))


def params(**more):
    return pltpu.CompilerParams(vmem_limit_bytes=VMEM, **more)


def shape(dims, dtype=f32):
    return jax.ShapeDtypeStruct(dims, dtype)


class Net:
    def __init__(self, n_dp, n_own):
        self.n_dp, self.n_own = n_dp, n_own
        self.dp_bits = [1 << i for i in range(n_dp.bit_length() - 1)]
        self.own_bits = [1 << i for i in range(n_own.bit_length() - 1)]
        core = [("dp", self.dp_bits[0])]
        plane = [("dp", self.dp_bits[1]), ("own", self.own_bits[0])]
        line = [("dp", self.dp_bits[2]), ("dp", self.dp_bits[3])]
        self.stages = [core, plane, line]
        self.rest = [[("dp", b)] for b in self.dp_bits[4:]] + [
            [("own", b)] for b in self.own_bits[1:]
        ]

    def place(self, bits):
        at = {"dp": lax.axis_index("dp"), "own": lax.axis_index("own")}
        total = 0
        for i, (axis, bit) in enumerate(bits):
            total = total + jnp.where((at[axis] & bit) != 0, 1 << i, 0)
        return total.astype(jnp.int32)

    def swap(self, value, bits, which):
        dp_mask = own_mask = 0
        for i, (axis, bit) in enumerate(bits):
            if which >> i & 1:
                if axis == "dp":
                    dp_mask |= bit
                else:
                    own_mask |= bit
        pairs = []
        for d in range(self.n_dp):
            for o in range(self.n_own):
                source = d * self.n_own + o
                pairs.append((source, (d ^ dp_mask) * self.n_own + (o ^ own_mask)))
        return lax.ppermute(value, ("dp", "own"), pairs)

    def scatter_sum(self, parts, bits, link):
        me = self.place(bits)
        got = []
        for g in range(1 << len(bits)):
            piece = lax.dynamic_index_in_dim(parts, me ^ g, 0, keepdims=False)
            if g > 0:
                piece = self.swap(piece.astype(link), bits, g).astype(parts.dtype)
            got.append(piece)
        while len(got) > 1:
            got = [got[i] + got[i + 1] for i in range(0, len(got), 2)]
        return got[0]

    def gather(self, value, bits):
        return jnp.stack([value] + [self.swap(value, bits, g) for g in range(1, 1 << len(bits))])

    def add_up(self, value, bits):
        got = [value] + [self.swap(value, bits, g) for g in range(1, 1 << len(bits))]
        while len(got) > 1:
            got = [got[i] + got[i + 1] for i in range(0, len(got), 2)]
        return got[0]

    def own_list(self):
        return [("own", b) for b in self.own_bits]


def pick_kernel(table, master, out):
    kept = table[1, pl.program_id(0)] > 0

    @pl.when(kept)
    def _():
        out[...] = master[...].astype(bf16)

    @pl.when(jnp.logical_not(kept))
    def _():
        out[...] = jnp.zeros_like(out)


def pick_blocks(table, master, halves):
    count = table.shape[1]
    rows = HALF if halves else D
    return pl.pallas_call(
        pick_kernel,
        grid_spec=pltpu.PrefetchScalarGridSpec(
            num_scalar_prefetch=1,
            grid=(count,),
            in_specs=[
                pl.BlockSpec((1, rows, D), lambda i, t: (t[0, i], t[2, i] if halves else 0, 0))
            ],
            out_specs=pl.BlockSpec((1, rows, D), lambda i, t: (i, 0, 0)),
        ),
        out_shape=shape((count, rows, D), bf16),
        compiler_params=params(),
        cost_estimate=cost(0, count * rows * D * 6),
        name="pick_blocks",
    )(table, master)


def join_halves(core, near, far, out):
    out[:, pl.ds(pl.multiple_of(core * HALF, HALF), HALF), :] = near[...]
    out[:, pl.ds(pl.multiple_of((1 - core) * HALF, HALF), HALF), :] = far[...]


def normed(value):
    centered = value - jnp.mean(value, axis=-1, keepdims=True)
    inverse = lax.rsqrt(jnp.mean(centered * centered, axis=-1, keepdims=True) + norm_eps)
    return centered * inverse, inverse


def norm_back(gradient, norm, inverse):
    return inverse * (
        gradient
        - jnp.mean(gradient, axis=-1, keepdims=True)
        - norm * jnp.mean(gradient * norm, axis=-1, keepdims=True)
    )


def attend_kernel(core, latents, mod, near, far, bias, qkv, mixed, total, weight):
    @pl.when(pl.program_id(0) == 0)
    def _():
        join_halves(core[0], near, far, weight)

    norm, _ = normed(latents[0].astype(f32))
    first = (norm * (1.0 + mod[0, 1:2]) + mod[0, 0:1]).astype(bf16)
    for b in range(3):
        qkv[0, :, b * D : (b + 1) * D] = (dot(first, weight[b]) + bias[b : b + 1]).astype(bf16)
    lane = lax.broadcasted_iota(jnp.int32, (1, 2 * HD), 1)
    values_t = qkv[0, :, 2 * D : 3 * D].T
    total[0] = jnp.zeros_like(total[0])
    for p in range(H // 2):
        keys = qkv[0, :, D + 2 * HD * p : D + 2 * HD * (p + 1)]
        pair = qkv[0, :, 2 * HD * p : 2 * HD * (p + 1)]
        for h in range(2):
            j = 2 * p + h
            mask = jnp.where((lane < HD) == (h == 0), HD**-0.5, 0.0).astype(bf16)
            scores = dot(keys, pair * mask, NT)
            peak = jnp.max(scores, axis=0, keepdims=True)
            expo = jnp.exp(scores - peak)
            sums = jnp.sum(expo, axis=0, keepdims=True)
            out = dot(values_t[HD * j : HD * (j + 1)], expo.astype(bf16))
            mixed[0, HD * j : HD * (j + 1), :] = (out * (1.0 / sums)).astype(bf16)
            total[0, j : j + 1, :] = peak + jnp.log(sums)


def middle_kernel(
    rows,
    core,
    latents,
    upstream,
    mixed,
    mod,
    near,
    far,
    bias,
    block_out,
    residual_back,
    mixed_back,
    delta,
    sums,
    grad_early,
    grad_proj,
    bias_sums,
    weight,
    second_s,
    act_s,
    pre_s,
    attn_s,
    ffn_s,
):
    step = pl.program_id(0)

    @pl.when(step == 0)
    def _():
        join_halves(core[0], near, far, weight)

    gate_one, shift_two, scale_two, gate_two = (mod[0, i : i + 1] for i in (2, 3, 4, 5))
    length = latents.shape[1]
    back_gate_two = back_gate_one = back_scale = back_shift = 0.0
    low_ffn = low_attn = 0.0
    low_pre = [0.0] * FB

    def column(value):
        return jnp.sum(value, axis=0, keepdims=True)

    for start in range(0, length, rows):
        part = slice(start, start + rows)
        attn_out = dot(mixed[0, :, part], weight[0], TN) + bias[3:4]
        residual = latents[0, part].astype(f32) + gate_one * attn_out
        norm, inverse = normed(residual)
        second = (norm * (1.0 + scale_two) + shift_two).astype(bf16)
        second_s[part] = second
        ct = upstream[0, part].astype(f32)
        ffn_back = (ct * gate_two).astype(bf16)
        ffn_s[part] = ffn_back
        ffn_out = bias[8:9]
        second_back = 0.0
        for n in range(FB):
            cols = slice(n * D, (n + 1) * D)
            pre = dot(second, weight[1 + n]) + bias[4 + n : 5 + n]
            square = pre * pre
            k0 = 0.7978845608028654
            tanh = jnp.tanh(pre * (k0 + (k0 * 0.044715) * square))
            half = 0.5 + 0.5 * tanh
            act = (pre * half).astype(bf16)
            slope = half + pre * (0.5 - 0.5 * tanh * tanh) * (
                k0 + (3.0 * k0 * 0.044715) * square
            )
            act_s[part, cols] = act
            ffn_out = ffn_out + dot(act, weight[1 + FB + n])
            act_back = dot(ffn_back, weight[1 + FB + n], NT)
            pre_back_f = act_back * slope
            pre_back = pre_back_f.astype(bf16)
            pre_s[part, cols] = pre_back
            low_pre[n] = low_pre[n] + column(pre_back.astype(f32))
            second_back = second_back + dot(pre_back, weight[1 + n], NT)
        block_out[0, part] = (residual + gate_two * ffn_out).astype(bf16)
        back_gate_two = back_gate_two + column(ct * ffn_out)
        back_scale = back_scale + column(second_back * norm)
        back_shift = back_shift + column(second_back)
        res_back = ct + norm_back(second_back * (1.0 + scale_two), norm, inverse)
        residual_back[0, part] = res_back
        back_gate_one = back_gate_one + column(res_back * attn_out)
        attn_back = (res_back * gate_one).astype(bf16)
        attn_s[part] = attn_back
        low_ffn = low_ffn + column(ffn_back.astype(f32))
        low_attn = low_attn + column(attn_back.astype(f32))
        mix_back = dot(attn_back, weight[0], NT).astype(bf16)
        mixed_back[0, part] = mix_back
        turned = mix_back.astype(f32).T * mixed[0, :, part].astype(f32)
        for j in range(H):
            delta[0, j : j + 1, part] = jnp.sum(
                turned[HD * j : HD * (j + 1)], axis=0, keepdims=True
            )
        delta[0, H:8, part] = jnp.zeros((8 - H, rows), f32)

    sums[0] = jnp.concatenate(
        [back_gate_one, back_shift, back_scale, back_gate_two, jnp.zeros((4, D), f32)], axis=0
    )
    biases = jnp.concatenate(
        [low_attn] + low_pre + [low_ffn, jnp.zeros((8 - FB - 2, D), f32)], axis=0
    )

    def store(first):
        def put(ref, index, value):
            ref[index] = value if first else ref[index] + value

        put(bias_sums, Ellipsis, biases)
        put(grad_proj, 0, dot(mixed[0], attn_s[...]))
        for n in range(FB):
            cols = slice(n * D, (n + 1) * D)
            put(grad_early, n, dot(second_s[...], pre_s[:, cols], TN))
            put(grad_early, FB + n, dot(act_s[:, cols], ffn_s[...], TN))

    @pl.when(step == 0)
    def _():
        store(True)

    @pl.when(step > 0)
    def _():
        store(False)


def attend_back_kernel(query, keys, values, back, total, delta, *rest):
    back_query, back_keys, back_values = rest[-3:]
    pair = rest[0]
    lane = lax.broadcasted_iota(jnp.int32, (1, 2 * HD), 1)
    keys_t = keys[0].T
    key_sum = value_sum = 0.0
    query_parts = []
    row = lax.broadcasted_iota(jnp.int32, (8, 1), 0)
    for h in range(2):
        one = jnp.where((lane < HD) == (h == 0), 1.0, 0.0).astype(bf16)
        pick = row == 2 * pair + h
        log_total = jnp.sum(jnp.where(pick, total[0], 0.0), axis=0, keepdims=True)
        row_delta = jnp.sum(jnp.where(pick, delta[0], 0.0), axis=0, keepdims=True)
        q = query[0] * (one * HD**-0.5)
        g = back[0] * one
        scores = dot(keys[0], q, NT)
        prob = jnp.exp(scores - log_total)
        prob_back = dot(values[0], g, NT)
        score_back = (prob * (prob_back - row_delta)).astype(bf16)
        value_sum = value_sum + dot(prob.astype(bf16), g)
        key_sum = key_sum + dot(score_back, q)
        query_parts.append(dot(keys_t[HD * h : HD * (h + 1)], score_back))
    back_keys[0] = key_sum.astype(bf16)
    back_values[0] = value_sum.astype(bf16)
    back_query[0] = (jnp.concatenate(query_parts, axis=0) * HD**-0.5).T.astype(bf16)


def first_back_kernel(
    core,
    latents,
    residual_back,
    mod,
    back_query,
    back_keys,
    back_values,
    near,
    far,
    grad_proj,
    latents_grad,
    sums,
    grads,
    bias_sums,
    weight,
):
    step = pl.program_id(0)

    @pl.when(step == 0)
    def _():
        join_halves(core[0], near, far, weight)
        grads[3] = grad_proj[0]

    norm, inverse = normed(latents[0].astype(f32))
    first = (norm * (1.0 + mod[0, 1:2]) + mod[0, 0:1]).astype(bf16)
    backs = (back_query[0], back_keys[0], back_values[0])
    new = [dot(first, b, TN) for b in backs]
    lows = jnp.concatenate(
        [jnp.sum(b.astype(f32), axis=0, keepdims=True) for b in backs]
        + [jnp.zeros((5, D), f32)],
        axis=0,
    )

    @pl.when(step == 0)
    def _():
        for i in range(3):
            grads[i] = new[i]
        bias_sums[...] = lows

    @pl.when(step > 0)
    def _():
        for i in range(3):
            grads[i] += new[i]
        bias_sums[...] += lows

    first_back = sum(dot(b, weight[i], NT) for i, b in enumerate(backs))
    sums[0] = jnp.concatenate(
        [
            jnp.sum(first_back, axis=0, keepdims=True),
            jnp.sum(first_back * norm, axis=0, keepdims=True),
            jnp.zeros((6, D), f32),
        ],
        axis=0,
    )
    latents_grad[0] = residual_back[0] + norm_back(
        first_back * (1.0 + mod[0, 1:2]), norm, inverse
    )


def split_two(value):
    high = value.astype(bf16)
    return high, (value - high.astype(f32)).astype(bf16)


def renew(gradient, state, outs):
    left, right, root_left, root_right, master = state
    grads_out, left_out, right_out, master_out = outs
    low = gradient.astype(bf16)
    grads_out[0] = gradient
    left_out[0] = 0.5 * left[0] + 0.5 * dot(low, low, NT)
    right_out[0] = 0.5 * right[0] + 0.5 * dot(low, low, TN)
    left_high, left_low = split_two(root_left[0])
    right_high, right_low = split_two(root_right[0])
    inner = dot(left_high, low) + dot(left_low, low)
    inner_high, inner_low = split_two(inner)
    direction = dot(inner_high, right_high) + dot(inner_low, right_high) + dot(inner_high, right_low)
    weight = master[0]
    scale = jnp.sqrt(jnp.mean(weight * weight) + norm_eps) * lax.rsqrt(
        jnp.mean(direction * direction) + norm_eps
    )
    master_out[0] = weight - shampoo_rate * (scale * direction + shampoo_decay * weight)


def keep_slot(table, given, outs):
    @pl.when((table[1, 0] == 0) & (pl.program_id(0) == 0))
    def _():
        for before, out in zip(given, outs):
            pltpu.sync_copy(before.at[pl.ds(table[0, 0], 1)], out)


def summed_slots_kernel(pieces, table, *refs):
    parts, state, outs = refs[:pieces], refs[pieces : pieces + 5], refs[-4:]
    keep_slot(table, refs[pieces + 5 : -4], outs)

    @pl.when(table[1, pl.program_id(0)] > 0)
    def _():
        gradient = jnp.concatenate([p[0, 0, 0] for p in parts], axis=0).astype(f32)
        renew(gradient, state, outs)


def cond_slots_kernel(table, cond, mods, *refs):
    state, outs = refs[:5], refs[-4:]
    keep_slot(table, refs[5:-4], outs)
    kind = table[1, pl.program_id(0)]

    @pl.when(kind == 1)
    def _():
        renew(dot(cond[...], mods[...], TN), state, outs)

    @pl.when(kind == 2)
    def _():
        left, right, _, _, master = state
        outs[0][0] = jnp.zeros_like(outs[0][0])
        outs[1][0] = 0.5 * left[0]
        outs[2][0] = 0.5 * right[0]
        outs[3][0] = master[0] - shampoo_rate * (shampoo_decay * master[0])


def slot_call(kernel, table, lead, lead_specs, state, outs, name):
    slots = state[0].shape[0]
    slot_spec = pl.BlockSpec((1, D, D), lambda i, t: (t[0, i], 0, 0))
    given = [] if outs is None else list(outs)
    steps = table.shape[1]
    first = 1 + len(lead) + 5
    return pl.pallas_call(
        kernel,
        grid_spec=pltpu.PrefetchScalarGridSpec(
            num_scalar_prefetch=1,
            grid=(steps,),
            in_specs=lead_specs
            + [slot_spec] * 5
            + [pl.BlockSpec(memory_space=pl.ANY)] * len(given),
            out_specs=[slot_spec] * 4,
        ),
        out_shape=[shape((slots, D, D))] * 4,
        input_output_aliases={first + i: i for i in range(len(given))},
        compiler_params=params(),
        cost_estimate=cost(steps * 7 * 2 * D**3, steps * 10 * D * D * 4),
        name=name,
    )(table, *lead, *state, *given)


def slot_places(owner, slot_count):
    order = jnp.arange(owner.shape[0], dtype=jnp.int32)
    before = (order[None, :] < order[:, None]) & (owner[None, :] == owner[:, None])
    return owner * slot_count + jnp.sum(before.astype(jnp.int32), axis=1)


def slot_table(blocks, mine, local, kinds, steps):
    work = kinds > 0
    rank = jnp.cumsum(work.astype(jnp.int32)) - 1
    count = rank[-1] + 1
    step = jnp.minimum(jnp.arange(steps, dtype=jnp.int32), jnp.maximum(count - 1, 0))
    hit = (rank[None, :] == step[:, None]) & work[None, :]
    live = (jnp.arange(steps, dtype=jnp.int32) < count).astype(jnp.int32)

    def choose(values):
        return jnp.sum(jnp.where(hit, values[None, :], 0), axis=1).astype(jnp.int32)

    return jnp.stack([choose(local), choose(kinds) * live, choose(blocks)])


def per_device(
    net,
    latents,
    condition,
    cotangent,
    owner,
    master,
    stat_left,
    stat_right,
    root_left,
    root_right,
    bias,
    moment_one,
    moment_two,
):
    slots = master.shape[0]
    seqs, length, _ = latents.shape
    tokens = seqs * length
    blocks = owner.shape[0]
    ada = blocks - 4 - EARLY
    member = lax.axis_index("own").astype(jnp.int32)
    core = net.place(net.stages[0])
    places = slot_places(owner, slots)
    mine = owner == member
    local = jnp.where(mine, places - member * slots, 0).astype(jnp.int32)
    table = jnp.stack(
        [local, mine.astype(jnp.int32), jnp.broadcast_to(core, (blocks,)).astype(jnp.int32)]
    )
    core_one = core.reshape(1)
    own_all = net.own_list()

    near_qkv = pick_blocks(table[:, 0:3], master, True)
    own_ada = pick_blocks(table[:, 4 + EARLY :], master, False)
    near_rest = pick_blocks(table[:, 3 : 4 + EARLY], master, True)
    for bit in own_all:
        near_qkv = near_qkv + net.swap(near_qkv, [bit], 1)
    far_qkv = net.swap(near_qkv, net.stages[0], 1)

    bias_rows = bias.reshape(-1, D)
    cond_float = condition.astype(f32)
    silu_cond, silu_pull = jax.vjp(jax.nn.silu, cond_float)
    cond_low = silu_cond.astype(bf16)
    cond_group = net.gather(cond_low, own_all)
    mod_parts = jnp.einsum("gld,bde->glbe", cond_group, own_ada, preferred_element_type=f32)
    modulation = mod_parts[0]
    for g in range(1, net.n_own):
        modulation = modulation + net.swap(mod_parts[g], own_all, g)
    modulation = modulation + bias_rows[9:]

    for bit in own_all:
        near_rest = near_rest + net.swap(near_rest, [bit], 1)
    far_rest = net.swap(near_rest, net.stages[0], 1)

    def whole(*dims):
        return pl.BlockSpec(dims, lambda i, *_: (0,) * len(dims))

    def each(*dims):
        return pl.BlockSpec((1,) + dims, lambda i, *_: (i,) + (0,) * len(dims))

    smem = pl.BlockSpec(memory_space=pltpu.SMEM)
    tok = each(length, D)
    qkv, mixed, totals = pl.pallas_call(
        attend_kernel,
        grid=(seqs,),
        in_specs=[
            smem,
            tok,
            each(6, D),
            whole(3, HALF, D),
            whole(3, HALF, D),
            whole(*bias_rows.shape),
        ],
        out_specs=[each(length, 3 * D), each(D, length), each(8, length)],
        out_shape=[
            shape((seqs, length, 3 * D), bf16),
            shape((seqs, D, length), bf16),
            shape((seqs, 8, length)),
        ],
        scratch_shapes=[pltpu.VMEM((3, D, D), bf16)],
        compiler_params=params(),
        cost_estimate=cost(16e9, 12e6, 12e6),
        name="attend",
    )(core_one, latents, modulation, near_qkv, far_qkv, bias_rows)

    (
        block_out,
        residual_back,
        mixed_back,
        delta,
        mid_sums,
        grad_early,
        grad_proj,
        mid_bias,
    ) = pl.pallas_call(
        functools.partial(middle_kernel, 256),
        grid=(seqs,),
        in_specs=[
            smem,
            tok,
            tok,
            each(D, length),
            each(6, D),
            whole(1 + EARLY, HALF, D),
            whole(1 + EARLY, HALF, D),
            whole(*bias_rows.shape),
        ],
        out_specs=[
            tok,
            tok,
            tok,
            each(8, length),
            each(8, D),
            whole(EARLY, D, D),
            whole(1, D, D),
            whole(8, D),
        ],
        out_shape=[
            shape((seqs, length, D), bf16),
            shape((seqs, length, D)),
            shape((seqs, length, D), bf16),
            shape((seqs, 8, length)),
            shape((seqs, 8, D)),
            shape((EARLY, D, D)),
            shape((1, D, D)),
            shape((8, D)),
        ],
        scratch_shapes=[
            pltpu.VMEM((1 + EARLY, D, D), bf16),
            pltpu.VMEM((length, D), bf16),
            pltpu.VMEM((length, FF), bf16),
            pltpu.VMEM((length, FF), bf16),
            pltpu.VMEM((length, D), bf16),
            pltpu.VMEM((length, D), bf16),
        ],
        compiler_params=params(),
        cost_estimate=cost(22e9, 25e6, 3e6),
        name="middle",
    )(core_one, latents, cotangent, mixed, modulation, near_rest, far_rest, bias_rows)

    def reduce_scatter(grads):
        rows = grads.shape[0] * D
        value = grads.reshape(2, rows // 2, D)
        value = net.scatter_sum(value, net.stages[0], f32)
        value = net.scatter_sum(value.reshape(4, rows // 8, D), net.stages[1], bf16)
        value = net.scatter_sum(value.reshape(4, rows // 32, D), net.stages[2], f32)
        for bits in net.rest:
            value = net.add_up(value, bits)
        return value.astype(bf16)

    def all_gather(value):
        for bits in net.stages[::-1]:
            value = net.gather(value, bits)
        return value

    early = all_gather(reduce_scatter(grad_early))

    backs = None
    for s in range(seqs):
        for p in range(H // 2):
            def head(offset, s=s, p=p):
                return pl.BlockSpec((1, length, 2 * HD), lambda i: (s, 0, offset + p))

            stat = pl.BlockSpec((1, 8, length), lambda i, s=s: (s, 0, 0))
            given = [] if backs is None else list(backs)

            def kernel(*refs, p=p):
                attend_back_kernel(*refs[:6], p, *refs[6:])

            backs = pl.pallas_call(
                kernel,
                grid=(1,),
                in_specs=[head(0), head(3), head(6), head(0), stat, stat]
                + [pl.BlockSpec(memory_space=pl.ANY)] * len(given),
                out_specs=[head(0)] * 3,
                out_shape=[shape((seqs, length, D), bf16)] * 3,
                input_output_aliases={6 + i: i for i in range(len(given))},
                compiler_params=params(),
                cost_estimate=cost(5e9, 2e6, 2e6),
                name="attend_back",
            )(qkv, qkv, qkv, mixed_back, totals, delta, *given)

    latents_grad, first_sums, grad_late, first_bias = pl.pallas_call(
        first_back_kernel,
        grid=(seqs,),
        in_specs=[
            smem,
            tok,
            tok,
            each(6, D),
            tok,
            tok,
            tok,
            whole(3, HALF, D),
            whole(3, HALF, D),
            whole(1, D, D),
        ],
        out_specs=[tok, each(8, D), whole(LATE, D, D), whole(8, D)],
        out_shape=[
            shape((seqs, length, D)),
            shape((seqs, 8, D)),
            shape((LATE, D, D)),
            shape((8, D)),
        ],
        scratch_shapes=[pltpu.VMEM((3, D, D), bf16)],
        compiler_params=params(),
        cost_estimate=cost(5e9, 18e6),
        name="first_back",
    )(core_one, latents, residual_back, modulation, *backs, near_qkv, far_qkv, grad_proj)

    late = all_gather(reduce_scatter(grad_late))

    back_mod = jnp.concatenate(
        [first_sums[:, 0:2].reshape(seqs, 2 * D), mid_sums[:, 0:4].reshape(seqs, 4 * D)], axis=1
    ).astype(bf16)
    rows = jnp.concatenate([back_mod, cond_low], axis=1)
    every = net.stages + net.rest
    for bits in every[::-1]:
        rows = net.gather(rows, bits)
    order = []
    for bits in every:
        order = order + bits[::-1]
    digits = len(order)
    group_rows = []
    flat = rows.reshape(1 << digits, seqs, (ada + 1) * D)
    for g in range(net.n_own):
        at = 0
        for k, (axis, bit) in enumerate(order):
            if axis == "own" and g & bit:
                at |= 1 << (digits - 1 - k)
        group_rows.append(flat[at])
    me = net.place(order[::-1])
    devices = 1 << digits
    number = jnp.arange(devices * seqs, dtype=jnp.int32)
    turn = (
        (number[:, None] // seqs ^ me) == number[None, :] // seqs
    ) & (number[:, None] % seqs == number[None, :] % seqs)
    sorted_rows = dot(
        turn.astype(bf16), rows.reshape(devices * seqs, (ada + 1) * D)
    ).astype(bf16)
    all_mods, all_cond = sorted_rows[:, : ada * D], sorted_rows[:, ada * D :]
    group = jnp.stack(group_rows)[:, :, : ada * D].reshape(net.n_own, seqs, ada, D)
    cond_parts = jnp.einsum("glbe,bde->gld", group, own_ada, preferred_element_type=f32)
    back_cond = cond_parts[0]
    for g in range(1, net.n_own):
        back_cond = back_cond + net.swap(cond_parts[g], own_all, g)
    condition_grad = silu_pull(back_cond)[0]

    bias_part = jnp.concatenate([first_bias[0:3], mid_bias[0 : FB + 2]], axis=0)
    for bits in every:
        bias_part = net.add_up(bias_part, bits)
    bias_grad = jnp.concatenate(
        [bias_part.reshape(-1), jnp.sum(all_mods.astype(f32), axis=0)]
    )

    state = (stat_left, stat_right, root_left, root_right, master)
    number = jnp.arange(blocks, dtype=jnp.int32)
    is_early = (number >= 4) & (number < 4 + EARLY)
    is_ada = number >= 4 + EARLY
    seat = [net.place(bits) for bits in net.stages]

    def gather_specs(value, count):
        per = 32 // count
        specs = []
        for i in range(per):
            def where(s, t, i=i):
                shard = t[2, s] * per + i
                return (
                    (shard // 16) ^ t[3, 0],
                    (shard // 4 % 4) ^ t[3, 1],
                    (shard % 4) ^ t[3, 2],
                    0,
                    0,
                )

            specs.append(pl.BlockSpec((1, 1, 1) + value.shape[3:], where))
        return [value] * per, specs

    def with_seat(given):
        row = jnp.zeros((1, given.shape[1]), jnp.int32)
        for i in range(3):
            row = row.at[0, i].set(seat[i])
        return jnp.concatenate([given, row], axis=0)

    def steps_of(count):
        return max(3, min(slots, count))

    early_table = with_seat(
        slot_table(number - 4, mine, local, (mine & is_early).astype(jnp.int32), steps_of(EARLY))
    )
    lead, specs = gather_specs(early, EARLY)
    outs = slot_call(
        functools.partial(summed_slots_kernel, len(lead)),
        early_table,
        lead,
        specs,
        state,
        None,
        "early_slots",
    )

    filled = jnp.sum(mine.astype(jnp.int32))
    empty = jnp.arange(slots, dtype=jnp.int32)
    cond_table = slot_table(
        jnp.concatenate([jnp.maximum(number - 4 - EARLY, 0), jnp.zeros_like(empty)]),
        None,
        jnp.concatenate([local, empty]),
        jnp.concatenate(
            [(mine & is_ada).astype(jnp.int32), jnp.where(empty >= filled, 2, 0)]
        ).astype(jnp.int32),
        slots,
    )
    count_rows = devices * seqs
    outs = slot_call(
        cond_slots_kernel,
        cond_table,
        [all_cond, all_mods],
        [
            pl.BlockSpec((count_rows, D), lambda i, t: (0, 0)),
            pl.BlockSpec((count_rows, D), lambda i, t: (0, t[2, i])),
        ],
        state,
        outs,
        "cond_slots",
    )

    late_table = with_seat(
        slot_table(number, mine, local, (mine & (number < 4)).astype(jnp.int32), steps_of(LATE))
    )
    lead, specs = gather_specs(late, LATE)
    weight_grads, left_new, right_new, master_new = slot_call(
        functools.partial(summed_slots_kernel, len(lead)),
        late_table,
        lead,
        specs,
        state,
        outs,
        "late_slots",
    )

    moment_one_new = 0.9 * moment_one + 0.1 * bias_grad
    moment_two_new = 0.95 * moment_two + 0.05 * bias_grad * bias_grad
    corrected = (
        moment_one_new / (1.0 - 0.9**STEP) / (jnp.sqrt(moment_two_new / (1.0 - 0.95**STEP)) + 1e-08)
    )
    bias_new = bias - adam_rate * (corrected + adam_decay * bias)
    return (
        block_out,
        latents_grad,
        condition_grad,
        weight_grads,
        left_new,
        right_new,
        master_new,
        bias_grad,
        moment_one_new,
        moment_two_new,
        bias_new,
    )


def solution(mesh):
    net = Net(mesh.shape["dp"], mesh.shape["own"])
    token = P(("dp", "own"), None, None)
    slot = P("own", None, None)
    return jax.shard_map(
        functools.partial(per_device, net),
        mesh=mesh,
        in_specs=(token, P(("dp", "own"), None), token, P()) + (slot,) * 5 + (P(),) * 3,
        out_specs=(token, token, P(("dp", "own"), None)) + (slot,) * 4 + (P(),) * 4,
        check_vma=False,
    )
```

```python
import functools

import jax
import jax.numpy as jnp
from jax import lax
from jax.experimental import pallas as pl
from jax.experimental.pallas import tpu as pltpu
from jax.sharding import PartitionSpec as P

D = 384
H = 6
HD = 64
FF = 1536
FB = FF // D
STEP = 10
HALF = D // 2
LATE = 4
EARLY = 2 * FB

SHRINK = 2.5

norm_eps = 1e-06
shampoo_rate = 1.0
shampoo_decay = 0.01
adam_rate = 0.2
adam_decay = 0.01
f32 = jnp.float32
bf16 = jnp.bfloat16
VMEM = 56 * 1024 * 1024
LIMIT = 60.0

NN = (((1,), (0,)), ((), ()))
NT = (((1,), (1,)), ((), ()))
TN = (((0,), (0,)), ((), ()))


def dot(left, right, dims=NN):
    return lax.dot_general(left, right, dims, preferred_element_type=f32)


def cost(flops, moved, trans=0):
    return pl.CostEstimate(
        flops=int(flops / SHRINK),
        bytes_accessed=int(moved / SHRINK),
        transcendentals=int(trans / SHRINK),
    )


def params(**more):
    return pltpu.CompilerParams(vmem_limit_bytes=VMEM, **more)


def shape(dims, dtype=f32):
    return jax.ShapeDtypeStruct(dims, dtype)


def tie(value, *others):
    return lax.optimization_barrier((value,) + others)[0] if others else value


class Net:
    def __init__(self, n_dp, n_own):
        self.n_dp, self.n_own = n_dp, n_own
        self.dp_bits = [1 << i for i in range(n_dp.bit_length() - 1)]
        self.own_bits = [1 << i for i in range(n_own.bit_length() - 1)]
        core = [("dp", self.dp_bits[0])]
        plane = [("dp", self.dp_bits[1]), ("own", self.own_bits[0])]
        line = [("dp", self.dp_bits[2]), ("dp", self.dp_bits[3])]
        self.stages = [core, plane, line]
        self.rest = [[("dp", b)] for b in self.dp_bits[4:]] + [
            [("own", b)] for b in self.own_bits[1:]
        ]

    def place(self, bits):
        at = {"dp": lax.axis_index("dp"), "own": lax.axis_index("own")}
        total = 0
        for i, (axis, bit) in enumerate(bits):
            total = total + jnp.where((at[axis] & bit) != 0, 1 << i, 0)
        return total.astype(jnp.int32)

    def swap(self, value, bits, which):
        dp_mask = own_mask = 0
        for i, (axis, bit) in enumerate(bits):
            if which >> i & 1:
                if axis == "dp":
                    dp_mask |= bit
                else:
                    own_mask |= bit
        pairs = []
        for d in range(self.n_dp):
            for o in range(self.n_own):
                source = d * self.n_own + o
                pairs.append((source, (d ^ dp_mask) * self.n_own + (o ^ own_mask)))
        return lax.ppermute(value, ("dp", "own"), pairs)

    def scatter_sum(self, parts, bits, link, *others):
        me = self.place(bits)
        got = []
        for g in range(1 << len(bits)):
            piece = lax.dynamic_index_in_dim(parts, me ^ g, 0, keepdims=False)
            if g > 0:
                piece = tie(self.swap(piece.astype(link), bits, g), *others).astype(parts.dtype)
            got.append(piece)
        while len(got) > 1:
            got = [got[i] + got[i + 1] for i in range(0, len(got), 2)]
        return got[0]

    def gather(self, value, bits, *others):
        got = [self.swap(value, bits, g) for g in range(1, 1 << len(bits))]
        return jnp.stack([value] + tie(got, *others))

    def add_up(self, value, bits):
        got = [value] + [self.swap(value, bits, g) for g in range(1, 1 << len(bits))]
        while len(got) > 1:
            got = [got[i] + got[i + 1] for i in range(0, len(got), 2)]
        return got[0]

    def digits(self):
        found = []
        for bits in (self.stages + self.rest)[::-1]:
            found = found + bits
        return found

    def own_list(self):
        return [("own", b) for b in self.own_bits]


def plan_kernel(steps_soon, steps_last, slots, owner, seat, table):
    blocks = owner.shape[0]
    for i in range(4):
        table[2, i] = seat[i]
    count = jnp.int32(0)
    mine = []
    for b in range(blocks):
        here = (owner[b] == seat[4]).astype(jnp.int32)
        table[0, b] = count * here
        table[1, b] = here
        mine.append((here, count))
        count = count + here

    def fill(row, steps, entries):
        at = jnp.int32(0)
        for i in range(steps):
            for k in range(3):
                table[row + k, i] = 0
        for here, slot, kind, block in entries:
            @pl.when(here > 0)
            def _(at=at, slot=slot, kind=kind, block=block):
                table[row, at] = slot
                table[row + 1, at] = kind
                table[row + 2, at] = block

            at = at + here
        for i in range(1, steps):
            @pl.when(i >= at)
            def _(i=i):
                table[row, i] = table[row, i - 1]
                table[row + 2, i] = table[row + 2, i - 1]

    first_ada = LATE + EARLY
    soon = [(*mine[LATE + n], 1, n) for n in range(EARLY)]
    soon += [(*mine[first_ada + n], 2, n - 2) for n in range(2, blocks - first_ada)]
    for i in range(slots):
        soon.append(((i >= count).astype(jnp.int32), i, 3, 0))
    fill(3, steps_soon, soon)
    last = [(*mine[first_ada + n], 2, n) for n in range(2)]
    last += [(*mine[n], 1, n) for n in range(LATE)]
    fill(6, steps_last, last)


def make_plan(owner, seat, slots, steps_soon, steps_last):
    smem = pl.BlockSpec(memory_space=pltpu.SMEM)
    return pl.pallas_call(
        functools.partial(plan_kernel, steps_soon, steps_last, slots),
        in_specs=[smem, smem],
        out_specs=smem,
        out_shape=shape((9, max(32, slots)), jnp.int32),
        name="plan",
    )(owner, seat)


def pick_kernel(blocks, table, *refs):
    for i, b in enumerate(blocks):
        kept = jnp.where(table[1, b] > 0, 1.0, 0.0)
        refs[-1][i] = (refs[i][0] * kept).astype(bf16)


def pick_blocks(table, master, blocks, rows):
    dims = (len(blocks), rows, D)
    specs = [
        pl.BlockSpec((1, rows, D), lambda i, t, b=b: (t[0, b], t[2, 0] if rows < D else 0, 0))
        for b in blocks
    ]
    return pl.pallas_call(
        functools.partial(pick_kernel, blocks),
        grid_spec=pltpu.PrefetchScalarGridSpec(
            num_scalar_prefetch=1,
            grid=(1,),
            in_specs=specs,
            out_specs=pl.BlockSpec(dims, lambda i, t: (0, 0, 0)),
        ),
        out_shape=shape(dims, bf16),
        compiler_params=params(),
        cost_estimate=cost(0, 6 * dims[0] * rows * D),
        name="pick_blocks",
    )(table, *([master] * len(blocks)))


def join_halves(core, near, far, out):
    out[:, pl.ds(pl.multiple_of(core * HALF, HALF), HALF), :] = near[...]
    out[:, pl.ds(pl.multiple_of((1 - core) * HALF, HALF), HALF), :] = far[...]


def normed(value):
    centered = value - jnp.mean(value, axis=-1, keepdims=True)
    inverse = lax.rsqrt(jnp.mean(centered * centered, axis=-1, keepdims=True) + norm_eps)
    return centered * inverse, inverse


def norm_back(gradient, norm, inverse):
    return inverse * (
        gradient
        - jnp.mean(gradient, axis=-1, keepdims=True)
        - norm * jnp.mean(gradient * norm, axis=-1, keepdims=True)
    )


def attend_kernel(core, latents, mod, near, far, bias, qkv, mixed, total, first_in, weight):
    @pl.when(pl.program_id(0) == 0)
    def _():
        join_halves(core[2, 0], near, far, weight)

    norm, _ = normed(latents[0].astype(f32))
    first = (norm * (1.0 + mod[0, 1:2]) + mod[0, 0:1]).astype(bf16)
    first_in[0] = first
    for b in range(3):
        qkv[0, :, b * D : (b + 1) * D] = (dot(first, weight[b]) + bias[b : b + 1]).astype(bf16)
    total[0] = jnp.zeros_like(total[0])

    head_of = lax.broadcasted_iota(jnp.int32, (D, 2 * HD), 0) // HD
    marks = jnp.where(
        head_of == lax.broadcasted_iota(jnp.int32, (D, 2 * HD), 1), 1.0, 0.0
    ).astype(bf16)

    def longest(block):
        value = qkv[0, :, block * D : (block + 1) * D].astype(f32)
        return jnp.max(dot((value * value).astype(bf16), marks), axis=0, keepdims=True)

    bound = jnp.max(longest(0) * longest(1)) * (1.05 / HD)
    small = bound < LIMIT * LIMIT

    def heads(shifted):
        lane = lax.broadcasted_iota(jnp.int32, (1, 2 * HD), 1)
        values_t = qkv[0, :, 2 * D : 3 * D].T
        for p in range(H // 2):
            keys = qkv[0, :, D + 2 * HD * p : D + 2 * HD * (p + 1)]
            pair = qkv[0, :, 2 * HD * p : 2 * HD * (p + 1)]
            for h in range(2):
                j = 2 * p + h
                mask = jnp.where((lane < HD) == (h == 0), HD**-0.5, 0.0).astype(bf16)
                scores = dot(keys, pair * mask, NT)
                peak = 0.0
                if shifted:
                    peak = jnp.max(scores, axis=0, keepdims=True)
                    scores = scores - peak
                expo = jnp.exp(scores)
                sums = jnp.sum(expo, axis=0, keepdims=True)
                prob = (expo * (1.0 / sums)).astype(bf16)
                out = dot(values_t[HD * j : HD * (j + 1)], prob)
                mixed[0, HD * j : HD * (j + 1), :] = out.astype(bf16)
                total[0, j : j + 1, :] = peak + jnp.log(sums)

    @pl.when(small)
    def _():
        heads(False)

    @pl.when(jnp.logical_not(small))
    def _():
        heads(True)


def middle_kernel(
    rows,
    core,
    latents,
    upstream,
    mixed,
    mod,
    near,
    far,
    bias,
    block_out,
    residual_back,
    mixed_back,
    sums,
    grad_early,
    grad_late,
    bias_sums,
    proj,
    up,
    down,
    second_s,
    act_s,
    pre_s,
    attn_s,
    ffn_s,
):
    step = pl.program_id(0)

    @pl.when(step == 0)
    def _():
        for half, ref in ((core[2, 0], near), (1 - core[2, 0], far)):
            at = pl.multiple_of(half * HALF, HALF)
            proj[pl.ds(at, HALF), :] = ref[0]
            for n in range(FB):
                up[pl.ds(at, HALF), n * D : (n + 1) * D] = ref[1 + n]
                down[pl.ds(n * D + at, HALF), :] = ref[1 + FB + n]

    gate_one, shift_two, scale_two, gate_two = (mod[0, i : i + 1] for i in (2, 3, 4, 5))
    length = latents.shape[1]
    back_gate_two = back_gate_one = back_scale = back_shift = 0.0
    low_ffn = low_attn = low_pre = 0.0
    bias_up = jnp.concatenate([bias[4 + n : 5 + n] for n in range(FB)], axis=1)

    def column(value):
        return jnp.sum(value, axis=0, keepdims=True)

    for start in range(0, length, rows):
        part = slice(start, start + rows)
        attn_out = dot(mixed[0, :, part], proj[...], TN) + bias[3:4]
        residual = latents[0, part].astype(f32) + gate_one * attn_out
        norm, inverse = normed(residual)
        second = (norm * (1.0 + scale_two) + shift_two).astype(bf16)
        second_s[part] = second
        ct = upstream[0, part].astype(f32)
        ffn_back = (ct * gate_two).astype(bf16)
        ffn_s[part] = ffn_back
        pre = dot(second, up[...]) + bias_up
        square = pre * pre
        k0 = 0.7978845608028654
        tanh = jnp.tanh(pre * (k0 + (k0 * 0.044715) * square))
        half = 0.5 + 0.5 * tanh
        act_s[part] = (pre * half).astype(bf16)
        slope = half + pre * (0.5 - 0.5 * tanh * tanh) * (k0 + (3.0 * k0 * 0.044715) * square)
        ffn_out = dot(act_s[part], down[...]) + bias[8:9]
        pre_back = (dot(ffn_back, down[...], NT) * slope).astype(bf16)
        pre_s[part] = pre_back
        low_pre = low_pre + column(pre_back.astype(f32))
        second_back = dot(pre_back, up[...], NT)
        block_out[0, part] = (residual + gate_two * ffn_out).astype(bf16)
        back_gate_two = back_gate_two + column(ct * ffn_out)
        back_scale = back_scale + column(second_back * norm)
        back_shift = back_shift + column(second_back)
        res_back = ct + norm_back(second_back * (1.0 + scale_two), norm, inverse)
        residual_back[0, part] = res_back
        back_gate_one = back_gate_one + column(res_back * attn_out)
        attn_back = (res_back * gate_one).astype(bf16)
        attn_s[part] = attn_back
        low_ffn = low_ffn + column(ffn_back.astype(f32))
        low_attn = low_attn + column(attn_back.astype(f32))
        mixed_back[0, part] = dot(attn_back, proj[...], NT).astype(bf16)

    sums[0] = jnp.concatenate(
        [back_gate_one, back_shift, back_scale, back_gate_two, jnp.zeros((4, D), f32)], axis=0
    )
    biases = jnp.concatenate(
        [low_attn]
        + [low_pre[:, n * D : (n + 1) * D] for n in range(FB)]
        + [low_ffn, jnp.zeros((8 - FB - 2, D), f32)],
        axis=0,
    )

    def store(first):
        def put(ref, index, value):
            ref[index] = value if first else ref[index] + value

        put(bias_sums, Ellipsis, biases)
        put(grad_late, 0, dot(mixed[0], attn_s[...]))
        grad_up = dot(second_s[...], pre_s[...], TN)
        for n in range(FB):
            cols = slice(n * D, (n + 1) * D)
            put(grad_early, n, grad_up[:, cols])
            put(grad_early, FB + n, dot(act_s[:, cols], ffn_s[...], TN))

    @pl.when(step == 0)
    def _():
        store(True)

    @pl.when(step > 0)
    def _():
        store(False)


def attend_back_kernel(begin, first_pair, query, keys, values, back, total, first, *rest):
    grads_in, biases_in = rest[:2]
    back_query, back_keys, back_values, grads, biases = rest[-5:]
    pair = first_pair + pl.program_id(0)
    lane = lax.broadcasted_iota(jnp.int32, (1, 2 * HD), 1)
    keys_t = keys[0].T
    key_sum = value_sum = 0.0
    query_parts = []
    for h in range(2):
        one = jnp.where((lane < HD) == (h == 0), 1.0, 0.0).astype(bf16)
        q = query[0] * (one * HD**-0.5)
        g = back[0] * one
        prob = jnp.exp(dot(keys[0], q, NT) - total[0, pl.ds(2 * pair + h, 1)])
        prob_back = dot(values[0], g, NT)
        row_delta = jnp.sum(prob * prob_back, axis=0, keepdims=True)
        score_back = (prob * (prob_back - row_delta)).astype(bf16)
        value_sum = value_sum + dot(prob.astype(bf16), g)
        key_sum = key_sum + dot(score_back, q)
        query_parts.append(dot(keys_t[HD * h : HD * (h + 1)], score_back))
    low = (
        (jnp.concatenate(query_parts, axis=0) * HD**-0.5).T.astype(bf16),
        key_sum.astype(bf16),
        value_sum.astype(bf16),
    )
    lows = []
    for i, (out, value) in enumerate(zip((back_query, back_keys, back_values), low)):
        out[0] = value
        new = dot(first[0], value, TN)
        grads[i] = new if begin else grads_in[i] + new
        lows.append(jnp.sum(value.astype(f32), axis=0, keepdims=True))
    lows = jnp.concatenate(lows + [jnp.zeros((5, 2 * HD), f32)], axis=0)
    biases[...] = lows if begin else biases_in[...] + lows


def first_back_kernel(table, latents, residual_back, mod, back_query, back_keys, back_values, near, far, *rest):
    latents_grad, sums, weight = rest[-3:]

    @pl.when(pl.program_id(0) == 0)
    def _():
        join_halves(table[2, 0], near, far, weight)

    norm, inverse = normed(latents[0].astype(f32))
    first_back = (
        dot(back_query[0], weight[0], NT)
        + dot(back_keys[0], weight[1], NT)
        + dot(back_values[0], weight[2], NT)
    )
    both = jnp.concatenate(
        [
            jnp.sum(first_back, axis=0, keepdims=True),
            jnp.sum(first_back * norm, axis=0, keepdims=True),
            jnp.zeros((6, D), f32),
        ],
        axis=0,
    )

    @pl.when(pl.program_id(0) == 0)
    def _():
        sums[0] = both

    @pl.when(pl.program_id(0) > 0)
    def _():
        sums[0] += both

    latents_grad[0] = residual_back[0] + norm_back(
        first_back * (1.0 + mod[0, 1:2]), norm, inverse
    )


def split_two(value):
    high = value.astype(bf16)
    return high, (value - high.astype(f32)).astype(bf16)


def renew(gradient, state, outs):
    left, right, root_left, root_right, master = state
    grads_out, left_out, right_out, master_out = outs
    low = gradient.astype(bf16)
    grads_out[0] = gradient
    left_out[0] = 0.5 * left[0] + 0.5 * dot(low, low, NT)
    right_out[0] = 0.5 * right[0] + 0.5 * dot(low, low, TN)
    left_high, left_low = split_two(root_left[0])
    right_high, right_low = split_two(root_right[0])
    inner = dot(left_high, low) + dot(left_low, low)
    inner_high, inner_low = split_two(inner)
    direction = dot(inner_high, right_high) + dot(inner_low, right_high) + dot(inner_high, right_low)
    weight = master[0]
    scale = jnp.sqrt(jnp.mean(weight * weight) + norm_eps) * lax.rsqrt(
        jnp.mean(direction * direction) + norm_eps
    )
    master_out[0] = weight - shampoo_rate * (scale * direction + shampoo_decay * weight)


def slots_kernel(row, begin, pieces, table, cond, mods, *refs):
    halves = refs[:pieces], refs[pieces : 2 * pieces]
    state, outs = refs[2 * pieces : 2 * pieces + 5], refs[-4:]
    given = refs[2 * pieces + 5 : -4][:4]
    step = pl.program_id(0)
    kind = table[row + 1, begin + step]
    far = shard_half(table, row, begin + step, pieces)

    if given:
        @pl.when((table[row + 1, begin] == 0) & (step == 0))
        def _():
            for before, out in zip(given, outs):
                pltpu.sync_copy(before.at[pl.ds(table[row, begin], 1)], out)

    for half, parts in enumerate(halves):
        @pl.when((kind == 1) & (far == half))
        def _(parts=parts):
            outs[0][0] = jnp.concatenate([p[0, 0] for p in parts], axis=0).astype(f32)

    @pl.when(kind == 2)
    def _():
        outs[0][0] = dot(cond[...], mods[...], TN)

    @pl.when((kind == 1) | (kind == 2))
    def _():
        renew(outs[0][0], state, outs)

    @pl.when(kind == 3)
    def _():
        left, right, _, _, master = state
        outs[0][0] = jnp.zeros_like(outs[0][0])
        outs[1][0] = 0.5 * left[0]
        outs[2][0] = 0.5 * right[0]
        outs[3][0] = master[0] - shampoo_rate * (shampoo_decay * master[0])


def shard_half(table, row, step, pieces):
    return ((table[row + 2, step] * pieces) >> 4) ^ table[2, 0]


def slots_call(row, begin, steps, table, cond, mods, gathered, rows, state, outs, ties, name):
    slots = state[0].shape[0]
    pieces = D // rows
    slot_spec = pl.BlockSpec((1, D, D), lambda s, t: (t[row, begin + s], 0, 0))

    def if_kind(t, s, kind, value):
        return jnp.where(t[row + 1, begin + s] == kind, value, 0)

    specs = [
        pl.BlockSpec(cond.shape, lambda s, t: (0, 0)),
        pl.BlockSpec(
            (cond.shape[0], D), lambda s, t: (0, if_kind(t, s, 2, t[row + 2, begin + s]))
        ),
    ]
    for half in range(2):
        for i in range(pieces):
            def where(s, t, i=i, half=half):
                shard = if_kind(t, s, 1, t[row + 2, begin + s]) * pieces + i
                used = shard_half(t, row, begin + s, pieces) == half
                return (
                    jnp.where(used, ((shard >> 2) & 3) ^ t[2, 1], 0),
                    jnp.where(used, (shard & 3) ^ t[2, 2], 0),
                    0,
                    0,
                )

            specs.append(pl.BlockSpec((1, 1, rows, D), where))
    more = ([] if outs is None else list(outs)) + list(ties)
    first = 3 + 2 * pieces + 5
    return pl.pallas_call(
        functools.partial(slots_kernel if outs is not None else slots_first, row, begin, pieces),
        grid_spec=pltpu.PrefetchScalarGridSpec(
            num_scalar_prefetch=1,
            grid=(steps,),
            in_specs=specs + [slot_spec] * 5 + [pl.BlockSpec(memory_space=pl.ANY)] * len(more),
            out_specs=[slot_spec] * 4,
        ),
        out_shape=[shape((slots, D, D))] * 4,
        input_output_aliases={} if outs is None else {first + i: i for i in range(4)},
        compiler_params=params(),
        cost_estimate=cost(steps * 7 * 2 * D**3, steps * 10 * D * D * 4),
        name=name,
    )(table, cond, mods, *([gathered[0]] * pieces), *([gathered[1]] * pieces), *state, *more)


def slots_first(row, begin, pieces, table, cond, mods, *refs):
    slots_kernel(row, begin, pieces, table, cond, mods, *refs[: 2 * pieces + 5], *refs[-4:])


def whole(*dims):
    return pl.BlockSpec(dims, lambda *_: (0,) * len(dims))


def each(*dims):
    return pl.BlockSpec((1,) + dims, lambda i, *_: (i,) + (0,) * len(dims))


def per_device(
    net,
    latents,
    condition,
    cotangent,
    owner,
    master,
    stat_left,
    stat_right,
    root_left,
    root_right,
    bias,
    moment_one,
    moment_two,
):
    slots = master.shape[0]
    seqs, length, _ = latents.shape
    blocks = owner.shape[0]
    first_ada = LATE + EARLY
    ada = blocks - first_ada
    own_all = net.own_list()
    steps_last = min(slots, 2 + LATE)
    anyplace = pl.BlockSpec(memory_space=pl.ANY)
    smem = pl.BlockSpec(memory_space=pltpu.SMEM)
    tok = each(length, D)

    seat = jnp.stack(
        [net.place(bits) for bits in net.stages]
        + [jnp.int32(0), lax.axis_index("own").astype(jnp.int32)]
    )
    table = make_plan(owner, seat, slots, slots, steps_last)

    near_qkv = pick_blocks(table, master, list(range(3)), HALF)
    own_ada = pick_blocks(table, master, list(range(first_ada, blocks)), D)
    near_rest = pick_blocks(table, master, list(range(3, first_ada)), HALF)
    for bit in own_all:
        near_qkv = near_qkv + tie(net.swap(near_qkv, [bit], 1), near_rest)
    far_qkv = net.swap(near_qkv, net.stages[0], 1)

    bias_rows = bias.reshape(-1, D)
    cond_float = condition.astype(f32)
    silu_cond, silu_pull = jax.vjp(jax.nn.silu, cond_float)
    cond_low = silu_cond.astype(bf16)
    cond_group = net.gather(cond_low, own_all)
    mod_parts = jnp.einsum("gld,bde->glbe", cond_group, own_ada, preferred_element_type=f32)
    modulation = mod_parts[0]
    for g in range(1, net.n_own):
        modulation = modulation + net.swap(mod_parts[g], own_all, g)
    modulation = modulation + bias_rows[9:]

    near_rest = tie(near_rest, near_qkv, modulation)

    qkv, mixed, totals, first_in = pl.pallas_call(
        attend_kernel,
        grid=(seqs,),
        in_specs=[
            smem,
            tok,
            each(6, D),
            whole(3, HALF, D),
            whole(3, HALF, D),
            whole(*bias_rows.shape),
        ],
        out_specs=[each(length, 3 * D), each(D, length), each(8, length), tok],
        out_shape=[
            shape((seqs, length, 3 * D), bf16),
            shape((seqs, D, length), bf16),
            shape((seqs, 8, length)),
            shape((seqs, length, D), bf16),
        ],
        scratch_shapes=[pltpu.VMEM((3, D, D), bf16)],
        compiler_params=params(),
        cost_estimate=cost(16e9, 12e6, 12e6),
        name="attend",
    )(table, latents, modulation, near_qkv, far_qkv, bias_rows)

    for bit in own_all:
        near_rest = near_rest + tie(net.swap(near_rest, [bit], 1), qkv)
    far_rest = net.swap(near_rest, net.stages[0], 1)

    (
        block_out,
        residual_back,
        mixed_back,
        mid_sums,
        grad_early,
        grad_late,
        mid_bias,
    ) = pl.pallas_call(
        functools.partial(middle_kernel, length // 2),
        grid=(seqs,),
        in_specs=[
            smem,
            tok,
            tok,
            each(D, length),
            each(6, D),
            whole(1 + EARLY, HALF, D),
            whole(1 + EARLY, HALF, D),
            whole(*bias_rows.shape),
        ],
        out_specs=[
            tok,
            tok,
            tok,
            each(8, D),
            whole(EARLY, D, D),
            pl.BlockSpec((1, D, D), lambda i: (LATE - 1, 0, 0)),
            whole(8, D),
        ],
        out_shape=[
            shape((seqs, length, D), bf16),
            shape((seqs, length, D)),
            shape((seqs, length, D), bf16),
            shape((seqs, 8, D)),
            shape((EARLY, D, D)),
            shape((LATE, D, D)),
            shape((8, D)),
        ],
        scratch_shapes=[
            pltpu.VMEM((D, D), bf16),
            pltpu.VMEM((D, FF), bf16),
            pltpu.VMEM((FF, D), bf16),
            pltpu.VMEM((length, D), bf16),
            pltpu.VMEM((length, FF), bf16),
            pltpu.VMEM((length, FF), bf16),
            pltpu.VMEM((length, D), bf16),
            pltpu.VMEM((length, D), bf16),
        ],
        compiler_params=params(),
        cost_estimate=cost(22e9, 25e6, 3e6),
        name="middle",
    )(table, latents, cotangent, mixed, modulation, near_rest, far_rest, bias_rows)

    def core_stage(grads, *others):
        return net.scatter_sum(grads.reshape(2, -1, D), net.stages[0], f32, *others)

    def plane_stage(value, *others):
        return net.scatter_sum(value.reshape(4, -1, D), net.stages[1], bf16, *others)

    def line_stage(value, *others):
        value = net.scatter_sum(value.reshape(4, -1, D), net.stages[2], bf16, *others)
        for bits in net.rest:
            value = net.add_up(value, bits)
        return value.astype(bf16)

    def with_small(value, small):
        for bits in net.rest[::-1]:
            small = net.gather(small, bits)
        return jnp.concatenate([value, small.reshape(-1, D)], axis=0)

    digits = net.digits()
    devices = 1 << len(digits)
    number = jnp.arange(devices, dtype=jnp.int32)
    turn = ((number[:, None] ^ net.place(digits)) == number[None, :]).astype(bf16)
    group = []
    for g in range(net.n_own):
        group.append(sum(1 << k for k, (axis, bit) in enumerate(digits) if axis == "own" and g & bit))

    def small_rows(gathered, rows, count):
        flat = jnp.stack([half[:, :, rows:] for half in gathered]).reshape(devices, count, D)
        ordered = dot(turn, flat.reshape(devices, count * D)).reshape(devices, count, D)
        return ordered, jnp.stack([flat[i] for i in group])

    def two_parts(value):
        high, low = split_two(value)
        return [high, low]

    def padded(rows, count):
        rows = jnp.concatenate(rows, axis=0)
        return jnp.pad(rows, ((0, count - rows.shape[0]), (0, 0)))

    mid_low = mid_sums[:, 0:4].astype(bf16)
    soon_rows = -(-(seqs * 5 + FB + 2) // 16) * 16
    last_rows = -(-(seqs * 2 + 2 * 3) // 16) * 16
    small_soon = padded(
        [jnp.concatenate([mid_low, cond_low[:, None]], axis=1).reshape(seqs * 5, D)]
        + [mid_bias[0 : FB + 2].astype(bf16)],
        soon_rows,
    )

    def back_pairs(n, first_pair, count, carried, ties):
        def head(offset):
            return pl.BlockSpec((1, length, 2 * HD), lambda i: (n, 0, offset + first_pair + i))

        def latent(*dims):
            return pl.BlockSpec((1,) + dims, lambda i: (n, 0, 0))

        begin = n == 0
        grad_spec = pl.BlockSpec((3, D, 2 * HD), lambda i: (0, 0, first_pair + i))
        bias_spec = pl.BlockSpec((8, 2 * HD), lambda i: (0, first_pair + i))
        return pl.pallas_call(
            functools.partial(attend_back_kernel, begin, first_pair),
            grid=(count,),
            in_specs=[head(0), head(3), head(6), head(0), latent(8, length), latent(length, D)]
            + ([anyplace] * 2 if begin else [grad_spec, bias_spec])
            + [anyplace] * (len(carried) - 2 + len(ties)),
            out_specs=[head(0)] * 3 + [grad_spec, bias_spec],
            out_shape=[shape((seqs, length, D), bf16)] * 3 + [shape((LATE, D, D)), shape((8, D))],
            input_output_aliases={6: 3, 7: 4} | {8 + i: i for i in range(len(carried) - 2)},
            compiler_params=params(),
            cost_estimate=cost(count * 7e9, count * 3e6, count * 2e6),
            name="attend_back",
        )(qkv, qkv, qkv, mixed_back, totals, first_in, *carried, *ties)

    def first_back(n, backs, carried, ties):
        rows = length // 2
        part = pl.BlockSpec((1, rows, D), lambda i: (n, i, 0))
        return pl.pallas_call(
            first_back_kernel,
            grid=(2,),
            in_specs=[smem, part, part, pl.BlockSpec((1, 6, D), lambda i: (n, 0, 0))]
            + [part] * 3
            + [whole(3, HALF, D)] * 2
            + [anyplace] * (len(carried) + len(ties)),
            out_specs=[part, pl.BlockSpec((1, 8, D), lambda i: (n, 0, 0))],
            out_shape=[shape((seqs, length, D)), shape((seqs, 8, D))],
            input_output_aliases={9 + i: i for i in range(len(carried))},
            scratch_shapes=[pltpu.VMEM((3, D, D), bf16)],
            compiler_params=params(),
            cost_estimate=cost(3.5e9, 9e6),
            name="first_back",
        )(table, latents, residual_back, modulation, *backs, near_qkv, far_qkv, *carried, *ties)

    def swapped(backs):
        return [backs[3], backs[4], *backs[:3]]

    early = grad_early
    stages = [
        core_stage,
        plane_stage,
        lambda value: with_small(line_stage(value), small_soon),
        lambda value: net.gather(value, net.stages[2]),
    ]
    def after_stage(*others):
        nonlocal early
        if stages:
            early = stages.pop(0)(early)
            return [early, *others]
        return list(others)

    backs = [None] * 3 + [grad_late, jnp.zeros((8, D), f32)]
    firsts = []
    for n in range(seqs):
        for first_pair, count in ((0, 1), (1, 2)) if n == 0 else ((0, 1), (1, 1), (2, 1)):
            if n + first_pair == 0:
                carried, ties = backs[3:], []
            else:
                carried = swapped(backs)
                last = n > 0 and first_pair == 2
                ties = [] if last else after_stage(*(firsts[:1] if first_pair == 0 else []))
            backs = back_pairs(n, first_pair, count, carried, ties)
        if n < seqs - 1:
            firsts = first_back(n, backs[:3], firsts, after_stage())
    for stage in stages:
        early = stage(early)
    early = net.gather(early, net.stages[1], backs[0])
    grad_late, first_bias = backs[3:]
    latents_grad, first_sums = first_back(seqs - 1, backs[:3], firsts, [])
    late = core_stage(tie(grad_late, early), latents_grad)
    early = (early, net.swap(early, net.stages[0], 1))
    small_last = padded(
        [first_sums[:, 0:2].astype(bf16).reshape(seqs * 2, D)] + two_parts(first_bias[0:3]),
        last_rows,
    )

    early_rows = EARLY * D // 32
    late_rows = LATE * D // 32
    ordered_soon, group_soon = small_rows(early, early_rows, soon_rows)
    latent_rows = ordered_soon[:, : seqs * 5].reshape(devices * seqs, 5, D).astype(bf16)
    all_cond = latent_rows[:, 4]
    mods_soon = latent_rows[:, :4].reshape(devices * seqs, 4 * D)
    state = (stat_left, stat_right, root_left, root_right, master)
    cuts = [0, max(1, slots // 5), max(2, slots // 2), slots]

    def soon_slots(i, outs, ties):
        return slots_call(
            3,
            cuts[i],
            cuts[i + 1] - cuts[i],
            table,
            all_cond,
            mods_soon,
            early,
            early_rows,
            state,
            outs,
            ties,
            "soon_slots",
        )

    outs = soon_slots(0, None, [late])
    late = plane_stage(late, *outs)
    outs = soon_slots(1, outs, [late])
    late = with_small(line_stage(late, *outs), small_last)
    outs = soon_slots(2, outs, [late])
    late = net.gather(late, net.stages[2], *outs)
    late = net.gather(late, net.stages[1])
    late = (late, net.swap(late, net.stages[0], 1))
    ordered_last, group_last = small_rows(late, late_rows, last_rows)
    mods_last = ordered_last[:, : seqs * 2].reshape(devices * seqs, 2 * D).astype(bf16)
    weight_grads, left_new, right_new, master_new = slots_call(
        6, 0, steps_last, table, all_cond, mods_last, late, late_rows, state, outs, [], "last_slots"
    )

    group_mods = jnp.concatenate(
        [
            group_last[:, : seqs * 2].reshape(net.n_own, seqs, 2, D),
            group_soon[:, : seqs * 5].reshape(net.n_own, seqs, 5, D)[:, :, :4],
        ],
        axis=2,
    )
    cond_parts = jnp.einsum("glbe,bde->gld", group_mods, own_ada, preferred_element_type=f32)
    cond_parts = tie(cond_parts, weight_grads)
    back_cond = cond_parts[0]
    for g in range(1, net.n_own):
        back_cond = back_cond + net.swap(cond_parts[g], own_all, g)
    condition_grad = silu_pull(back_cond)[0]

    bias_last = jnp.sum(ordered_last[:, seqs * 2 : seqs * 2 + 6], axis=0)
    bias_soon = jnp.sum(ordered_soon[:, seqs * 5 : seqs * 5 + FB + 2], axis=0)

    bias_grad = jnp.concatenate(
        [
            (bias_last[:3] + bias_last[3:]).reshape(-1),
            bias_soon.reshape(-1),
            jnp.sum(mods_last.astype(f32), axis=0),
            jnp.sum(mods_soon.astype(f32), axis=0),
        ]
    )
    moment_one_new = 0.9 * moment_one + 0.1 * bias_grad
    moment_two_new = 0.95 * moment_two + 0.05 * bias_grad * bias_grad
    corrected = (
        moment_one_new / (1.0 - 0.9**STEP) / (jnp.sqrt(moment_two_new / (1.0 - 0.95**STEP)) + 1e-08)
    )
    bias_new = bias - adam_rate * (corrected + adam_decay * bias)
    return (
        block_out,
        latents_grad,
        condition_grad,
        weight_grads,
        left_new,
        right_new,
        master_new,
        bias_grad,
        moment_one_new,
        moment_two_new,
        bias_new,
    )


def solution(mesh):
    net = Net(mesh.shape["dp"], mesh.shape["own"])
    token = P(("dp", "own"), None, None)
    slot = P("own", None, None)
    return jax.shard_map(
        functools.partial(per_device, net),
        mesh=mesh,
        in_specs=(token, P(("dp", "own"), None), token, P()) + (slot,) * 5 + (P(),) * 3,
        out_specs=(token, token, P(("dp", "own"), None)) + (slot,) * 4 + (P(),) * 4,
        check_vma=False,
    )
```

```python
import functools

import jax
import jax.numpy as jnp
from jax import lax
from jax.experimental import pallas as pl
from jax.experimental.pallas import tpu as pltpu
from jax.sharding import PartitionSpec as P

D = 384
H = 6
HD = 64
FF = 1536
FB = FF // D
STEP = 10
HALF = D // 2
LATE = 4
EARLY = 2 * FB

SHRINK = 2.5

norm_eps = 1e-06
shampoo_rate = 1.0
shampoo_decay = 0.01
adam_rate = 0.2
adam_decay = 0.01
f32 = jnp.float32
bf16 = jnp.bfloat16
VMEM = 60 * 1024 * 1024
LIMIT = 60.0

NN = (((1,), (0,)), ((), ()))
NT = (((1,), (1,)), ((), ()))
TN = (((0,), (0,)), ((), ()))


def dot(left, right, dims=NN):
    return lax.dot_general(left, right, dims, preferred_element_type=f32)


def cost(flops, moved, trans=0):
    return pl.CostEstimate(
        flops=int(flops / SHRINK),
        bytes_accessed=int(moved / SHRINK),
        transcendentals=int(trans / SHRINK),
    )


def params(**more):
    return pltpu.CompilerParams(vmem_limit_bytes=VMEM, **more)


def shape(dims, dtype=f32):
    return jax.ShapeDtypeStruct(dims, dtype)


def tie(value, *others):
    return lax.optimization_barrier((value,) + others)[0] if others else value


class Net:
    def __init__(self, n_dp, n_own):
        self.n_dp, self.n_own = n_dp, n_own
        self.dp_bits = [1 << i for i in range(n_dp.bit_length() - 1)]
        self.own_bits = [1 << i for i in range(n_own.bit_length() - 1)]
        core = [("dp", self.dp_bits[0])]
        plane = [("dp", self.dp_bits[1]), ("own", self.own_bits[0])]
        line = [("dp", self.dp_bits[2]), ("dp", self.dp_bits[3])]
        self.stages = [core, plane, line]
        self.rest = [[("dp", b)] for b in self.dp_bits[4:]] + [
            [("own", b)] for b in self.own_bits[1:]
        ]

    def place(self, bits):
        at = {"dp": lax.axis_index("dp"), "own": lax.axis_index("own")}
        total = 0
        for i, (axis, bit) in enumerate(bits):
            total = total + jnp.where((at[axis] & bit) != 0, 1 << i, 0)
        return total.astype(jnp.int32)

    def swap(self, value, bits, which):
        dp_mask = own_mask = 0
        for i, (axis, bit) in enumerate(bits):
            if which >> i & 1:
                if axis == "dp":
                    dp_mask |= bit
                else:
                    own_mask |= bit
        pairs = []
        for d in range(self.n_dp):
            for o in range(self.n_own):
                source = d * self.n_own + o
                pairs.append((source, (d ^ dp_mask) * self.n_own + (o ^ own_mask)))
        return lax.ppermute(value, ("dp", "own"), pairs)

    def scatter_sum(self, parts, bits, link, *others):
        me = self.place(bits)
        got = []
        for g in range(1 << len(bits)):
            piece = lax.dynamic_index_in_dim(parts, me ^ g, 0, keepdims=False)
            if g > 0:
                piece = tie(self.swap(piece.astype(link), bits, g), *others).astype(parts.dtype)
            got.append(piece)
        while len(got) > 1:
            got = [got[i] + got[i + 1] for i in range(0, len(got), 2)]
        return got[0]

    def gather(self, value, bits, *others):
        got = [self.swap(value, bits, g) for g in range(1, 1 << len(bits))]
        return jnp.stack([value] + tie(got, *others))

    def add_up(self, value, bits):
        got = [value] + [self.swap(value, bits, g) for g in range(1, 1 << len(bits))]
        while len(got) > 1:
            got = [got[i] + got[i + 1] for i in range(0, len(got), 2)]
        return got[0]

    def digits(self):
        found = []
        for bits in (self.stages + self.rest)[::-1]:
            found = found + bits
        return found

    def own_list(self):
        return [("own", b) for b in self.own_bits]


def plan_kernel(cuts_soon, steps_last, slots, owner, seat, table):
    blocks = owner.shape[0]
    for i in range(4):
        table[2, i] = seat[i]
    count = jnp.int32(0)
    mine = []
    for b in range(blocks):
        here = (owner[b] == seat[4]).astype(jnp.int32)
        table[0, b] = count * here
        table[1, b] = here
        mine.append((here, count))
        count = count + here

    def fill(row, cuts, entries):
        left = jnp.int32(0)
        for here, *_ in entries:
            left = left + here
        steps = cuts[-1]
        for i in range(steps):
            for k in range(3):
                table[row + k, i] = 0
        ends = []
        for c in range(len(cuts) - 1):
            room, calls = cuts[c + 1] - cuts[c], len(cuts) - 1 - c
            part = jnp.minimum(room, (left + calls - 1) // calls)
            part = jnp.maximum(part, left - (steps - cuts[c + 1]))
            ends.append(cuts[c] + part)
            left = left - part
        at = jnp.int32(0)
        for c in range(len(ends) - 1):
            at = jnp.where(at == ends[c], cuts[c + 1], at)
        for here, slot, kind, block in entries:
            @pl.when(here > 0)
            def _(at=at, slot=slot, kind=kind, block=block):
                table[row, at] = slot
                table[row + 1, at] = kind
                table[row + 2, at] = block

            at = at + here
            for c in range(len(ends) - 1):
                at = jnp.where(at == ends[c], cuts[c + 1], at)
        for i in range(1, steps):
            @pl.when(table[row + 1, i] == 0)
            def _(i=i):
                table[row, i] = table[row, i - 1]
                table[row + 2, i] = table[row + 2, i - 1]

    first_ada = LATE + EARLY
    soon = [(*mine[LATE + n], 1, n) for n in range(EARLY)]
    soon += [(*mine[first_ada + n], 2, n - 2) for n in range(2, blocks - first_ada)]
    for i in range(slots):
        soon.append(((i >= count).astype(jnp.int32), i, 3, 0))
    fill(3, cuts_soon, soon)
    last = [(*mine[first_ada + n], 2, n) for n in range(2)]
    last += [(*mine[n], 1, n) for n in range(LATE)]
    fill(6, [0, steps_last], last)


def make_plan(owner, seat, slots, cuts_soon, steps_last):
    smem = pl.BlockSpec(memory_space=pltpu.SMEM)
    return pl.pallas_call(
        functools.partial(plan_kernel, cuts_soon, steps_last, slots),
        in_specs=[smem, smem],
        out_specs=smem,
        out_shape=shape((9, max(32, slots)), jnp.int32),
        name="plan",
    )(owner, seat)


def pick_kernel(blocks, table, *refs):
    for i, b in enumerate(blocks):
        kept = jnp.where(table[1, b] > 0, 1.0, 0.0)
        refs[-1][i] = (refs[i][0] * kept).astype(bf16)


def pick_blocks(table, master, blocks, rows):
    dims = (len(blocks), rows, D)
    specs = [
        pl.BlockSpec((1, rows, D), lambda i, t, b=b: (t[0, b], t[2, 0] if rows < D else 0, 0))
        for b in blocks
    ]
    return pl.pallas_call(
        functools.partial(pick_kernel, blocks),
        grid_spec=pltpu.PrefetchScalarGridSpec(
            num_scalar_prefetch=1,
            grid=(1,),
            in_specs=specs,
            out_specs=pl.BlockSpec(dims, lambda i, t: (0, 0, 0)),
        ),
        out_shape=shape(dims, bf16),
        compiler_params=params(),
        cost_estimate=cost(0, 6 * dims[0] * rows * D),
        name="pick_blocks",
    )(table, *([master] * len(blocks)))


def join_halves(core, near, far, out):
    out[:, pl.ds(pl.multiple_of(core * HALF, HALF), HALF), :] = near[...]
    out[:, pl.ds(pl.multiple_of((1 - core) * HALF, HALF), HALF), :] = far[...]


def normed(value):
    centered = value - jnp.mean(value, axis=-1, keepdims=True)
    inverse = lax.rsqrt(jnp.mean(centered * centered, axis=-1, keepdims=True) + norm_eps)
    return centered * inverse, inverse


def norm_back(gradient, norm, inverse):
    return inverse * (
        gradient
        - jnp.mean(gradient, axis=-1, keepdims=True)
        - norm * jnp.mean(gradient * norm, axis=-1, keepdims=True)
    )


def attend_kernel(core, latents, mod, near, far, bias, qkv, mixed, total, first_in, weight):
    @pl.when(pl.program_id(0) == 0)
    def _():
        join_halves(core[2, 0], near, far, weight)

    norm, _ = normed(latents[0].astype(f32))
    first = (norm * (1.0 + mod[0, 1:2]) + mod[0, 0:1]).astype(bf16)
    first_in[0] = first.T
    for b in range(3):
        qkv[0, :, b * D : (b + 1) * D] = (dot(first, weight[b]) + bias[:, b * D : (b + 1) * D]).astype(bf16)
    total[0] = jnp.zeros_like(total[0])

    head_of = lax.broadcasted_iota(jnp.int32, (D, 2 * HD), 0) // HD
    marks = jnp.where(
        head_of == lax.broadcasted_iota(jnp.int32, (D, 2 * HD), 1), 1.0, 0.0
    ).astype(bf16)

    def longest(block):
        value = qkv[0, :, block * D : (block + 1) * D].astype(f32)
        return jnp.max(dot((value * value).astype(bf16), marks), axis=0, keepdims=True)

    bound = jnp.max(longest(0) * longest(1)) * (1.05 / HD)
    small = bound < LIMIT * LIMIT

    def heads(shifted):
        lane = lax.broadcasted_iota(jnp.int32, (1, 2 * HD), 1)
        values_t = qkv[0, :, 2 * D : 3 * D].T
        for p in range(H // 2):
            keys = qkv[0, :, D + 2 * HD * p : D + 2 * HD * (p + 1)]
            pair = qkv[0, :, 2 * HD * p : 2 * HD * (p + 1)]
            for h in range(2):
                j = 2 * p + h
                mask = jnp.where((lane < HD) == (h == 0), HD**-0.5, 0.0).astype(bf16)
                scores = dot(keys, pair * mask, NT)
                peak = 0.0
                if shifted:
                    peak = jnp.max(scores, axis=0, keepdims=True)
                    scores = scores - peak
                expo = jnp.exp(scores)
                sums = jnp.sum(expo, axis=0, keepdims=True)
                prob = (expo * (1.0 / sums)).astype(bf16)
                out = dot(values_t[HD * j : HD * (j + 1)], prob)
                mixed[0, HD * j : HD * (j + 1), :] = out.astype(bf16)
                total[0, j : j + 1, :] = peak + jnp.log(sums)

    @pl.when(small)
    def _():
        heads(False)

    @pl.when(jnp.logical_not(small))
    def _():
        heads(True)


def middle_kernel(
    seqs,
    core,
    latents,
    upstream,
    mixed,
    mod,
    near,
    far,
    bias,
    cond,
    block_out,
    residual_back,
    mixed_back,
    keep,
    send,
    grad_late,
    small,
    proj,
    up,
    down,
    total,
    sums,
    bias_sums,
    second_s,
    act_s,
    pre_s,
    sems,
):
    seq, step = pl.program_id(0), pl.program_id(1)

    @pl.when((seq == 0) & (step == 0))
    def _():
        for half, ref in ((core[2, 0], near), (1 - core[2, 0], far)):
            at = pl.multiple_of(half * HALF, HALF)
            proj[pl.ds(at, HALF), :] = ref[0]
            for n in range(FB):
                up[pl.ds(at, HALF), n * D : (n + 1) * D] = ref[1 + n]
                down[pl.ds(n * D + at, HALF), :] = ref[1 + FB + n]
        total[...] = jnp.zeros_like(total)
        grad_late[...] = jnp.zeros_like(grad_late)
        bias_sums[...] = jnp.zeros_like(bias_sums)

    gate_one, shift_two, scale_two, gate_two = (mod[0, i : i + 1] for i in (2, 3, 4, 5))
    bias_up = bias[:, 4 * D : 4 * D + FF]

    def column(value):
        return jnp.sum(value, axis=0, keepdims=True)

    attn_out = dot(mixed[0], proj[...], TN) + bias[:, 3 * D : 4 * D]
    residual = latents[0].astype(f32) + gate_one * attn_out
    norm, inverse = normed(residual)
    second = (norm * (1.0 + scale_two) + shift_two).astype(bf16)
    second_s[...] = second
    ct = upstream[0].astype(f32)
    ffn_back = (ct * gate_two).astype(bf16)
    pre = dot(second, up[...]) + bias_up
    square = pre * pre
    k0 = 0.7978845608028654
    tanh = jnp.tanh(pre * (k0 + (k0 * 0.044715) * square))
    half = 0.5 + 0.5 * tanh
    act_s[...] = (pre * half).astype(bf16)
    slope = half + pre * (0.5 - 0.5 * tanh * tanh) * (k0 + (3.0 * k0 * 0.044715) * square)
    ffn_out = dot(act_s[...], down[...]) + bias[:, 4 * D + FF : 5 * D + FF]
    pre_back = (dot(ffn_back, down[...], NT) * slope).astype(bf16)
    pre_s[...] = pre_back
    low_pre = column(pre_back.astype(f32))
    second_back = dot(pre_back, up[...], NT)
    block_out[0] = (residual + gate_two * ffn_out).astype(bf16)
    res_back = ct + norm_back(second_back * (1.0 + scale_two), norm, inverse)
    residual_back[0] = res_back
    attn_back = (res_back * gate_one).astype(bf16)
    mixed_back[0] = dot(attn_back, proj[...], NT).astype(bf16)
    both = jnp.concatenate(
        [
            column(res_back * attn_out),
            column(second_back),
            column(second_back * norm),
            column(ct * ffn_out),
        ],
        axis=0,
    )
    bias_sums[...] += jnp.concatenate(
        [column(attn_back.astype(f32))]
        + [low_pre[:, n * D : (n + 1) * D] for n in range(FB)]
        + [column(ffn_back.astype(f32))],
        axis=0,
    )

    for n in range(seqs):
        @pl.when(seq == n)
        def _(n=n):
            sums[n] = jnp.where(step == 0, both, sums[n] + both)

    grad_late[0] += dot(mixed[0], attn_back)
    grad_up = dot(second_s[...], pre_s[...], TN)
    side = core[2, 0] * FB
    for n in range(FB):
        cols = slice(n * D, (n + 1) * D)
        total[side + n] += grad_up[:, cols]
        total[FB - side + n] += dot(act_s[:, cols], ffn_back, TN)

    @pl.when((seq == pl.num_programs(0) - 1) & (step == pl.num_programs(1) - 1))
    def _():
        copies = [
            pltpu.make_async_copy(total.at[pl.ds(i * FB, FB)], out, sems.at[i])
            for i, out in enumerate((keep, send))
        ]
        for copy in copies:
            copy.start()
        rows = [jnp.concatenate([sums[n], cond[n : n + 1]], axis=0) for n in range(seqs)]
        rows.append(bias_sums[...])
        filled = seqs * 5 + FB + 2
        if small.shape[0] > filled:
            rows.append(jnp.zeros((small.shape[0] - filled, D), f32))
        small[...] = jnp.concatenate(rows, axis=0).astype(bf16)
        for copy in copies:
            copy.wait()


def attend_back_kernel(begin, first_pair, query, keys, values, back, total, first, *rest):
    grads_in, biases_in = rest[:2]
    back_query, back_keys, back_values, grads, biases = rest[-5:]
    pair = first_pair + pl.program_id(0)
    lane = lax.broadcasted_iota(jnp.int32, (1, 2 * HD), 1)
    keys_t = keys[0].T
    key_sum = value_sum = 0.0
    query_parts = []
    for h in range(2):
        one = jnp.where((lane < HD) == (h == 0), 1.0, 0.0).astype(bf16)
        q = query[0] * (one * HD**-0.5)
        g = back[0] * one
        prob = jnp.exp(dot(keys[0], q, NT) - total[0, pl.ds(2 * pair + h, 1)])
        prob_back = dot(values[0], g, NT)
        row_delta = jnp.sum(prob * prob_back, axis=0, keepdims=True)
        score_back = (prob * (prob_back - row_delta)).astype(bf16)
        value_sum = value_sum + dot(prob.astype(bf16), g)
        key_sum = key_sum + dot(score_back, q)
        query_parts.append(dot(keys_t[HD * h : HD * (h + 1)], score_back))
    low = (
        (jnp.concatenate(query_parts, axis=0) * HD**-0.5).T.astype(bf16),
        key_sum.astype(bf16),
        value_sum.astype(bf16),
    )
    for out, value in zip((back_query, back_keys, back_values), low):
        out[0] = value
    joined = jnp.concatenate(low, axis=1)
    new = dot(first[0], joined)
    sums = jnp.sum(joined.astype(f32), axis=0, keepdims=True)
    width = 2 * HD
    for i in range(3):
        cols = slice(i * width, (i + 1) * width)
        grads[i] = new[:, cols] if begin else grads_in[i] + new[:, cols]
        biases[i : i + 1] = sums[:, cols] if begin else biases_in[i : i + 1] + sums[:, cols]


def first_back_kernel(table, latents, residual_back, mod, back_query, back_keys, back_values, near, far, *rest):
    latents_grad, sums, weight = rest[-3:]

    @pl.when(pl.program_id(0) == 0)
    def _():
        join_halves(table[2, 0], near, far, weight)

    norm, inverse = normed(latents[0].astype(f32))
    first_back = (
        dot(back_query[0], weight[0], NT)
        + dot(back_keys[0], weight[1], NT)
        + dot(back_values[0], weight[2], NT)
    )
    both = jnp.concatenate(
        [
            jnp.sum(first_back, axis=0, keepdims=True),
            jnp.sum(first_back * norm, axis=0, keepdims=True),
            jnp.zeros((6, D), f32),
        ],
        axis=0,
    )

    @pl.when(pl.program_id(0) == 0)
    def _():
        sums[0] = both

    @pl.when(pl.program_id(0) > 0)
    def _():
        sums[0] += both

    latents_grad[0] = residual_back[0] + norm_back(
        first_back * (1.0 + mod[0, 1:2]), norm, inverse
    )


def split_two(value):
    high = value.astype(bf16)
    return high, (value - high.astype(f32)).astype(bf16)


def chosen_rows(rows, count, seqs, me, group, per, kind):
    latent = lax.broadcasted_iota(jnp.int32, (count, rows.shape[0]), 0)
    wanted = (latent // seqs ^ me) * group + latent % seqs * per + kind
    hit = wanted == lax.broadcasted_iota(jnp.int32, (count, rows.shape[0]), 1)
    return dot(jnp.where(hit, 1.0, 0.0).astype(bf16), rows[...])


def slots_kernel(
    row, begin, room, pieces, stages, line, small, table, conds, mods, near, far, *refs
):
    state, outs = refs[:5], refs[-9:-5]
    held, gradient_in, made, in_sems, out_sems = refs[-5:]
    cond_group, mod_group, per, seqs = small
    rows = D // pieces
    count = jnp.int32(0)
    for i in range(room):
        count = count + (table[row + 1, begin + i] > 0).astype(jnp.int32)

    def piece(half, i, p, buf):
        shard = table[row + 2, begin + i] * pieces + p
        at = ((shard // line & 3) ^ table[2, 1], (shard & 3) ^ table[2, 2])[:stages]
        return pltpu.make_async_copy(
            half.at[(*at, pl.ds(0, rows))],
            gradient_in.at[buf, pl.ds(p * rows, rows)],
            in_sems.at[buf, 5 + p],
        )

    def arriving(i, k, buf):
        return pltpu.make_async_copy(
            state[k].at[table[row, begin + i]], held.at[buf, k], in_sems.at[buf, k]
        )

    def leaving(i, k, buf):
        return pltpu.make_async_copy(
            made.at[buf, k], outs[k].at[table[row, begin + i]], out_sems.at[buf, k]
        )

    def fetch(i, buf):
        side = (table[row + 2, begin + i] * pieces // (4 * line)) ^ table[2, 0]
        for number, half in enumerate((near, far)):
            @pl.when((table[row + 1, begin + i] == 1) & (side == number))
            def _(half=half):
                for p in range(pieces):
                    piece(half, i, p, buf).start()

        for k in (2, 3, 4, 0, 1):
            arriving(i, k, buf).start()

    @pl.when(count > 0)
    def _():
        fetch(0, 0)

    def one(i, carry):
        buf = i & 1
        kind = table[row + 1, begin + i]

        @pl.when(i + 1 < count)
        def _():
            fetch(i + 1, 1 - buf)

        @pl.when(i >= 2)
        def _():
            for k in range(4):
                leaving(i - 2, k, buf).wait()

        @pl.when(kind == 1)
        def _():
            for p in range(pieces):
                piece(near, i, p, buf).wait()
            made[buf, 0] = gradient_in[buf].astype(f32)

        @pl.when(kind == 2)
        def _():
            total = conds.shape[0] // cond_group * seqs
            me, block = table[2, 3], table[row + 2, begin + i]
            cond = chosen_rows(conds, total, seqs, me, cond_group, 5, 4).astype(bf16)
            mod = chosen_rows(mods, total, seqs, me, mod_group, per, block).astype(bf16)
            made[buf, 0] = dot(cond, mod, TN)

        @pl.when(kind == 3)
        def _():
            made[buf, 0] = jnp.zeros((D, D), f32)

        leaving(i, 0, buf).start()
        low = made[buf, 0].astype(bf16)
        arriving(i, 2, buf).wait()
        turned = low.T
        two = dot(jnp.concatenate([held[buf, 2].astype(bf16), turned], axis=0), low)
        arriving(i, 3, buf).wait()
        direction = dot(two[:D].astype(bf16), held[buf, 3].astype(bf16))
        arriving(i, 4, buf).wait()
        weight = held[buf, 4]
        scale = jnp.sqrt(jnp.mean(weight * weight) + norm_eps) * lax.rsqrt(
            jnp.mean(direction * direction) + norm_eps
        )
        made[buf, 3] = weight - shampoo_rate * (scale * direction + shampoo_decay * weight)
        leaving(i, 3, buf).start()
        arriving(i, 0, buf).wait()
        made[buf, 1] = 0.5 * held[buf, 0] + 0.5 * dot(low, turned)
        leaving(i, 1, buf).start()
        arriving(i, 1, buf).wait()
        made[buf, 2] = 0.5 * held[buf, 1] + 0.5 * two[D:]
        leaving(i, 2, buf).start()
        return carry

    lax.fori_loop(0, count, one, 0)
    for back in (2, 1):
        @pl.when(count >= back)
        def _(back=back):
            for k in range(4):
                leaving(count - back, k, (count - back) & 1).wait()


def slots_call(row, begin, steps, table, small, gathered, rows, state, outs, ties, name):
    slots = state[0].shape[0]
    pieces = D // rows
    stages = gathered[0].ndim - 2
    line = gathered[0].shape[1] if stages > 1 else 1
    conds, mods, *small = small
    given = [] if outs is None else list(outs)
    anyplace = pl.BlockSpec(memory_space=pl.ANY)
    more = given + list(ties)
    return pl.pallas_call(
        functools.partial(slots_kernel, row, begin, steps, pieces, stages, line, small),
        grid=(1,),
        in_specs=[pl.BlockSpec(memory_space=pltpu.SMEM), whole(*conds.shape), whole(*mods.shape)]
        + [anyplace] * (7 + len(more)),
        out_specs=[anyplace] * 4,
        out_shape=[shape((slots, D, D))] * 4,
        scratch_shapes=[
            pltpu.VMEM((2, 5, D, D), f32),
            pltpu.VMEM((2, D, D), bf16),
            pltpu.VMEM((2, 4, D, D), f32),
            pltpu.SemaphoreType.DMA((2, 5 + pieces)),
            pltpu.SemaphoreType.DMA((2, 4)),
        ],
        input_output_aliases={10 + i: i for i in range(len(given))},
        compiler_params=params(),
        cost_estimate=cost(steps * 7 * 2 * D**3, steps * 10 * D * D * 4),
        name=name,
    )(table, conds, mods, *gathered, *state, *more)


def finish_kernel(
    seqs,
    group,
    soon_group,
    last_group,
    table,
    soon,
    last,
    ada,
    bias,
    one,
    two,
    grad_out,
    one_out,
    two_out,
    bias_out,
    cond_out,
):
    me = table[2, 3]
    devices = soon.shape[0] // soon_group

    def totals(rows, each_group, kinds):
        count = len(kinds) * devices
        at = lax.broadcasted_iota(jnp.int32, (count, rows.shape[0]), 0)
        first = kinds[0]
        assert list(kinds) == list(range(first, first + len(kinds)))
        wanted = (at % devices ^ me) * each_group + at // devices + first
        hit = wanted == lax.broadcasted_iota(jnp.int32, (count, rows.shape[0]), 1)
        found = dot(jnp.where(hit, 1.0, 0.0).astype(bf16), rows[...])
        return [
            jnp.sum(found[k * devices : (k + 1) * devices], axis=0, keepdims=True)
            for k in range(len(kinds))
        ]

    of_soon = totals(soon, soon_group, range(0, seqs * 5 + FB + 2))
    of_last = totals(last, last_group, range(0, seqs * 2 + 6))
    qkv = [of_last[seqs * 2 + i] + of_last[seqs * 2 + 3 + i] for i in range(3)]
    mods = [sum(of_last[n * 2 + i] for n in range(seqs)) for i in range(2)]
    mods += [sum(of_soon[n * 5 + i] for n in range(seqs)) for i in range(4)]
    grad = jnp.concatenate(qkv + of_soon[seqs * 5 : seqs * 5 + FB + 2] + mods, axis=1)
    grad = grad.reshape(-1)
    grad_out[...] = grad
    one_new = 0.9 * one[...] + 0.1 * grad
    two_new = 0.95 * two[...] + 0.05 * grad * grad
    one_out[...] = one_new
    two_out[...] = two_new
    corrected = (
        one_new / (1.0 - 0.9**STEP) / (jnp.sqrt(two_new / (1.0 - 0.95**STEP)) + 1e-08)
    )
    bias_out[...] = bias[...] - adam_rate * (corrected + adam_decay * bias[...])
    for g, device in enumerate(group):
        total = 0.0
        for b in range(ada.shape[0]):
            rows, each_group, per, kind = (
                (last, last_group, 2, b) if b < 2 else (soon, soon_group, 5, b - 2)
            )
            base = device * each_group
            mine = jnp.concatenate(
                [rows[base + n * per + kind : base + n * per + kind + 1] for n in range(seqs)]
                + [jnp.zeros((8 - seqs, D), bf16)],
                axis=0,
            )
            total = total + dot(mine, ada[b], NT)
        cond_out[g * seqs : (g + 1) * seqs] = total[:seqs]


def finish(table, soon, last, ada, bias, one, two, seqs, group, soon_group, last_group):
    inputs = (soon, last, ada, bias, one, two)
    outs = [shape(bias.shape)] * 4 + [shape((len(group) * seqs, D))]
    return pl.pallas_call(
        functools.partial(finish_kernel, seqs, group, soon_group, last_group),
        grid=(1,),
        in_specs=[pl.BlockSpec(memory_space=pltpu.SMEM)] + [whole(*v.shape) for v in inputs],
        out_specs=[whole(*v.shape) for v in outs],
        out_shape=outs,
        compiler_params=params(),
        cost_estimate=cost(1e8, 2e6),
        name="finish",
    )(table, *inputs)


def whole(*dims):
    return pl.BlockSpec(dims, lambda *_: (0,) * len(dims))


def each(*dims):
    return pl.BlockSpec((1,) + dims, lambda i, *_: (i,) + (0,) * len(dims))


def middle(rows, table, latents, cotangent, mixed, modulation, near_rest, far_rest, bias_row, cond, small_rows):
    seqs, length, _ = latents.shape
    tok = pl.BlockSpec((1, rows, D), lambda i, j: (i, j, 0))
    anyplace = pl.BlockSpec(memory_space=pl.ANY)
    return pl.pallas_call(
        functools.partial(middle_kernel, seqs),
        grid=(seqs, length // rows),
        in_specs=[
            pl.BlockSpec(memory_space=pltpu.SMEM),
            tok,
            tok,
            pl.BlockSpec((1, D, rows), lambda i, j: (i, 0, j)),
            each(6, D),
            whole(1 + EARLY, HALF, D),
            whole(1 + EARLY, HALF, D),
            whole(*bias_row.shape),
            whole(*cond.shape),
        ],
        out_specs=[
            tok,
            tok,
            tok,
            anyplace,
            anyplace,
            pl.BlockSpec((1, D, D), lambda *_: (LATE - 1, 0, 0)),
            whole(small_rows, D),
        ],
        out_shape=[
            shape((seqs, length, D), bf16),
            shape((seqs, length, D)),
            shape((seqs, length, D), bf16),
            shape((FB, D, D)),
            shape((FB, D, D)),
            shape((LATE, D, D)),
            shape((small_rows, D), bf16),
        ],
        scratch_shapes=[
            pltpu.VMEM((D, D), bf16),
            pltpu.VMEM((D, FF), bf16),
            pltpu.VMEM((FF, D), bf16),
            pltpu.VMEM((2 * FB, D, D), f32),
            pltpu.VMEM((seqs, 4, D), f32),
            pltpu.VMEM((FB + 2, D), f32),
            pltpu.VMEM((rows, D), bf16),
            pltpu.VMEM((rows, FF), bf16),
            pltpu.VMEM((rows, FF), bf16),
            pltpu.SemaphoreType.DMA((2,)),
        ],
        compiler_params=params(),
        cost_estimate=cost(22e9, 25e6, 3e6),
        name="middle",
    )(table, latents, cotangent, mixed, modulation, near_rest, far_rest, bias_row, cond)


def per_device(
    net,
    latents,
    condition,
    cotangent,
    owner,
    master,
    stat_left,
    stat_right,
    root_left,
    root_right,
    bias,
    moment_one,
    moment_two,
):
    slots = master.shape[0]
    seqs, length, _ = latents.shape
    blocks = owner.shape[0]
    first_ada = LATE + EARLY
    ada = blocks - first_ada
    own_all = net.own_list()
    steps_last = min(slots, 2 + LATE)
    anyplace = pl.BlockSpec(memory_space=pl.ANY)
    smem = pl.BlockSpec(memory_space=pltpu.SMEM)
    tok = each(length, D)
    soon_rows = -(-(seqs * 5 + FB + 2) // 16) * 16
    last_rows = -(-(seqs * 2 + 2 * 3) // 16) * 16

    seat = jnp.stack(
        [net.place(bits) for bits in net.stages]
        + [net.place(net.digits()), lax.axis_index("own").astype(jnp.int32)]
    )
    cuts = [0, max(1, slots // 5), max(2, slots // 2), slots]
    table = make_plan(owner, seat, slots, cuts, steps_last)

    near_qkv = pick_blocks(table, master, list(range(3)), HALF)
    own_ada = pick_blocks(table, master, list(range(first_ada, blocks)), D)
    near_rest = pick_blocks(table, master, list(range(3, first_ada)), HALF)
    for bit in own_all:
        near_qkv = near_qkv + tie(net.swap(near_qkv, [bit], 1), near_rest)
    far_qkv = net.swap(near_qkv, net.stages[0], 1)

    bias_row = bias.reshape(1, -1)
    cond_float = condition.astype(f32)
    silu_cond, silu_pull = jax.vjp(jax.nn.silu, cond_float)
    cond_low = silu_cond.astype(bf16)
    cond_group = net.gather(cond_low, own_all)
    mod_parts = jnp.einsum("gld,bde->glbe", cond_group, own_ada, preferred_element_type=f32)
    modulation = mod_parts[0]
    for g in range(1, net.n_own):
        modulation = modulation + net.swap(mod_parts[g], own_all, g)
    modulation = modulation + bias[5 * D + FF :].reshape(ada, D)

    near_rest = tie(near_rest, near_qkv, modulation)

    qkv, mixed, totals, first_in = pl.pallas_call(
        attend_kernel,
        grid=(seqs,),
        in_specs=[
            smem,
            tok,
            each(6, D),
            whole(3, HALF, D),
            whole(3, HALF, D),
            whole(*bias_row.shape),
        ],
        out_specs=[each(length, 3 * D), each(D, length), each(8, length), each(D, length)],
        out_shape=[
            shape((seqs, length, 3 * D), bf16),
            shape((seqs, D, length), bf16),
            shape((seqs, 8, length)),
            shape((seqs, D, length), bf16),
        ],
        scratch_shapes=[pltpu.VMEM((3, D, D), bf16)],
        compiler_params=params(),
        cost_estimate=cost(16e9, 12e6, 12e6),
        name="attend",
    )(table, latents, modulation, near_qkv, far_qkv, bias_row)

    for bit in own_all:
        near_rest = near_rest + tie(net.swap(near_rest, [bit], 1), qkv)
    far_rest = net.swap(near_rest, net.stages[0], 1)

    (
        block_out,
        residual_back,
        mixed_back,
        early_keep,
        early_send,
        grad_late,
        small_soon,
    ) = middle(
        length,
        table,
        latents,
        cotangent,
        mixed,
        modulation,
        near_rest,
        far_rest,
        bias_row,
        cond_low.astype(f32),
        soon_rows,
    )

    def core_stage(grads, *others):
        return net.scatter_sum(grads.reshape(2, -1, D), net.stages[0], f32, *others)

    def plane_stage(value, *others):
        return net.scatter_sum(value.reshape(4, -1, D), net.stages[1], bf16, *others)

    def line_stage(value, *others):
        value = net.scatter_sum(value.reshape(4, -1, D), net.stages[2], bf16, *others)
        for bits in net.rest:
            value = net.add_up(value, bits)
        return value.astype(bf16)

    def with_small(value, small):
        for bits in net.rest[::-1]:
            small = net.gather(small, bits)
        return jnp.concatenate([value, small.reshape(-1, D)], axis=0)

    def line_exchange(value, small, others):
        rows = value.shape[0]
        got = net.gather(with_small(value.astype(bf16), small), net.stages[2], *others)
        value = (got[0, :rows].astype(f32) + got[1, :rows]) + (got[2, :rows].astype(f32) + got[3, :rows])
        for bits in net.rest:
            value = net.add_up(value, bits)
        return jnp.concatenate([value.astype(bf16), got[:, rows:].reshape(-1, D)], axis=0)

    def small_rows(gathered, rows):
        return jnp.stack([half[..., rows:, :] for half in gathered]).reshape(-1, D)

    def two_parts(value):
        high, low = split_two(value)
        return [high, low]

    def padded(rows, count):
        rows = jnp.concatenate(rows, axis=0)
        return jnp.pad(rows, ((0, count - rows.shape[0]), (0, 0)))

    def back_pairs(n, first_pair, count, carried, ties):
        def head(offset):
            return pl.BlockSpec((1, length, 2 * HD), lambda i: (n, 0, offset + first_pair + i))

        def latent(*dims):
            return pl.BlockSpec((1,) + dims, lambda i: (n, 0, 0))

        begin = n == 0
        grad_spec = pl.BlockSpec((3, D, 2 * HD), lambda i: (0, 0, first_pair + i))
        bias_spec = pl.BlockSpec((8, 2 * HD), lambda i: (0, first_pair + i))
        return pl.pallas_call(
            functools.partial(attend_back_kernel, begin, first_pair),
            grid=(count,),
            in_specs=[head(0), head(3), head(6), head(0), latent(8, length), latent(D, length)]
            + ([anyplace] * 2 if begin else [grad_spec, bias_spec])[: len(carried)]
            + [anyplace] * (len(carried[2:]) + len(ties)),
            out_specs=[head(0)] * 3 + [grad_spec, bias_spec],
            out_shape=[shape((seqs, length, D), bf16)] * 3 + [shape((LATE, D, D)), shape((8, D))],
            input_output_aliases={6 + i: at for i, at in enumerate((3, 4, 0, 1, 2)[: len(carried)])},
            compiler_params=params(),
            cost_estimate=cost(count * 7e9, count * 3e6, count * 2e6),
            name="attend_back",
        )(qkv, qkv, qkv, mixed_back, totals, first_in, *carried, *ties)

    def first_back(n, backs, carried, ties):
        rows = length // 2
        part = pl.BlockSpec((1, rows, D), lambda i: (n, i, 0))
        return pl.pallas_call(
            first_back_kernel,
            grid=(2,),
            in_specs=[smem, part, part, pl.BlockSpec((1, 6, D), lambda i: (n, 0, 0))]
            + [part] * 3
            + [whole(3, HALF, D)] * 2
            + [anyplace] * (len(carried) + len(ties)),
            out_specs=[part, pl.BlockSpec((1, 8, D), lambda i: (n, 0, 0))],
            out_shape=[shape((seqs, length, D)), shape((seqs, 8, D))],
            input_output_aliases={9 + i: i for i in range(len(carried))},
            scratch_shapes=[pltpu.VMEM((3, D, D), bf16)],
            compiler_params=params(),
            cost_estimate=cost(3.5e9, 9e6),
            name="first_back",
        )(table, latents, residual_back, modulation, *backs, near_qkv, far_qkv, *carried, *ties)

    def swapped(backs):
        return [backs[3], backs[4], *backs[:3]]

    early = early_keep
    stages = [
        lambda value: value + net.swap(early_send, net.stages[0], 1),
        plane_stage,
        lambda value: with_small(line_stage(value), small_soon),
        lambda value: net.gather(value, net.stages[2]),
    ]
    def after_stage(*others):
        nonlocal early
        if stages:
            early = stages.pop(0)(early)
            return [early, *others]
        return list(others)

    backs = [None] * 3 + [grad_late]
    firsts = []
    for n in range(seqs):
        for first_pair, count in ((0, 1), (1, 2)) if n == 0 else ((0, 1), (1, 1), (2, 1)):
            if n + first_pair == 0:
                carried, ties = [grad_late], []
            else:
                carried = swapped(backs)
                last = n > 0 and first_pair == 2
                ties = [] if last else after_stage(*(firsts[:1] if first_pair == 0 else []))
            backs = back_pairs(n, first_pair, count, carried, ties)
        if n < seqs - 1:
            firsts = first_back(n, backs[:3], firsts, after_stage())
    for stage in stages:
        early = stage(early)
    early = net.gather(early, net.stages[1], backs[0])
    grad_late, first_bias = backs[3:]
    latents_grad, first_sums = first_back(seqs - 1, backs[:3], firsts, [])
    late = core_stage(tie(grad_late, early), latents_grad)
    early = (early, net.swap(early, net.stages[0], 1))
    small_last = padded(
        [first_sums[:, 0:2].astype(bf16).reshape(seqs * 2, D)] + two_parts(first_bias[0:3]),
        last_rows,
    )

    early_rows = EARLY * D // 32
    late_rows = LATE * D // 8
    rows_soon = small_rows(early, early_rows)
    state = (stat_left, stat_right, root_left, root_right, master)
    def soon_slots(i, outs, ties):
        return slots_call(
            3,
            cuts[i],
            cuts[i + 1] - cuts[i],
            table,
            (rows_soon, rows_soon, soon_rows, soon_rows, 5, seqs),
            early,
            early_rows,
            state,
            outs,
            ties,
            "soon_slots",
        )

    outs = soon_slots(0, None, [late])
    late = plane_stage(late, *outs)
    outs = soon_slots(1, outs, [late])
    late = line_exchange(late, small_last, outs)
    outs = soon_slots(2, outs, [late])
    late = net.gather(late, net.stages[1], *outs)
    late = (late, net.swap(late, net.stages[0], 1))
    rows_last = small_rows(late, late_rows)
    group = []
    for g in range(net.n_own):
        group.append(
            sum(1 << k for k, (axis, bit) in enumerate(net.digits()) if axis == "own" and g & bit)
        )

    bias_outs = finish(
        table,
        rows_soon,
        rows_last,
        own_ada,
        bias,
        moment_one,
        moment_two,
        seqs,
        group,
        soon_rows,
        last_rows,
    )
    *bias_outs, cond_parts = bias_outs
    bias_grad, moment_one_new, moment_two_new, bias_new = bias_outs
    weight_grads, left_new, right_new, master_new = slots_call(
        6,
        0,
        steps_last,
        table,
        (rows_soon, rows_last, soon_rows, last_rows, 2, seqs),
        late,
        late_rows,
        state,
        outs,
        [bias_grad],
        "last_slots",
    )

    cond_parts = tie(cond_parts, weight_grads).reshape(net.n_own, seqs, D)
    back_cond = cond_parts[0]
    for g in range(1, net.n_own):
        back_cond = back_cond + net.swap(cond_parts[g], own_all, g)
    condition_grad = silu_pull(back_cond)[0]
    return (
        block_out,
        latents_grad,
        condition_grad,
        weight_grads,
        left_new,
        right_new,
        master_new,
        bias_grad,
        moment_one_new,
        moment_two_new,
        bias_new,
    )


def solution(mesh):
    net = Net(mesh.shape["dp"], mesh.shape["own"])
    token = P(("dp", "own"), None, None)
    slot = P("own", None, None)
    return jax.shard_map(
        functools.partial(per_device, net),
        mesh=mesh,
        in_specs=(token, P(("dp", "own"), None), token, P()) + (slot,) * 5 + (P(),) * 3,
        out_specs=(token, token, P(("dp", "own"), None)) + (slot,) * 4 + (P(),) * 4,
        check_vma=False,
    )
```

```python
import functools

import jax
import jax.numpy as jnp
from jax import lax
from jax.experimental import pallas as pl
from jax.experimental.pallas import tpu as pltpu
from jax.sharding import PartitionSpec as P

D = 384
H = 6
HD = 64
FF = 1536
FB = FF // D
STEP = 10
HALF = D // 2
LATE = 4
EARLY = 2 * FB

SHRINK = 2.5

norm_eps = 1e-06
shampoo_rate = 1.0
shampoo_decay = 0.01
adam_rate = 0.2
adam_decay = 0.01
f32 = jnp.float32
bf16 = jnp.bfloat16
VMEM = 60 * 1024 * 1024
LIMIT = 60.0

NN = (((1,), (0,)), ((), ()))
NT = (((1,), (1,)), ((), ()))
TN = (((0,), (0,)), ((), ()))


def dot(left, right, dims=NN):
    return lax.dot_general(left, right, dims, preferred_element_type=f32)


def cost(flops, moved, trans=0):
    return pl.CostEstimate(
        flops=int(flops / SHRINK),
        bytes_accessed=int(moved / SHRINK),
        transcendentals=int(trans / SHRINK),
    )


def params(**more):
    return pltpu.CompilerParams(vmem_limit_bytes=VMEM, **more)


def shape(dims, dtype=f32):
    return jax.ShapeDtypeStruct(dims, dtype)


def tie(value, *others):
    return lax.optimization_barrier((value,) + others)[0] if others else value


class Net:
    def __init__(self, n_dp, n_own):
        self.n_dp, self.n_own = n_dp, n_own
        self.dp_bits = [1 << i for i in range(n_dp.bit_length() - 1)]
        self.own_bits = [1 << i for i in range(n_own.bit_length() - 1)]
        core = [("dp", self.dp_bits[0])]
        plane = [("dp", self.dp_bits[1]), ("own", self.own_bits[0])]
        line = [("dp", self.dp_bits[2]), ("dp", self.dp_bits[3])]
        self.stages = [core, plane, line]
        self.rest = [[("dp", b)] for b in self.dp_bits[4:]] + [
            [("own", b)] for b in self.own_bits[1:]
        ]

    def place(self, bits):
        at = {"dp": lax.axis_index("dp"), "own": lax.axis_index("own")}
        total = 0
        for i, (axis, bit) in enumerate(bits):
            total = total + jnp.where((at[axis] & bit) != 0, 1 << i, 0)
        return total.astype(jnp.int32)

    def swap(self, value, bits, which):
        dp_mask = own_mask = 0
        for i, (axis, bit) in enumerate(bits):
            if which >> i & 1:
                if axis == "dp":
                    dp_mask |= bit
                else:
                    own_mask |= bit
        pairs = []
        for d in range(self.n_dp):
            for o in range(self.n_own):
                source = d * self.n_own + o
                pairs.append((source, (d ^ dp_mask) * self.n_own + (o ^ own_mask)))
        return lax.ppermute(value, ("dp", "own"), pairs)

    def scatter_sum(self, parts, bits, link, *others):
        me = self.place(bits)
        got = []
        for g in range(1 << len(bits)):
            piece = lax.dynamic_index_in_dim(parts, me ^ g, 0, keepdims=False)
            if g > 0:
                piece = tie(self.swap(piece.astype(link), bits, g), *others).astype(parts.dtype)
            got.append(piece)
        while len(got) > 1:
            got = [got[i] + got[i + 1] for i in range(0, len(got), 2)]
        return got[0]

    def gather(self, value, bits, *others):
        got = [self.swap(value, bits, g) for g in range(1, 1 << len(bits))]
        return jnp.stack([value] + tie(got, *others))

    def add_up(self, value, bits):
        got = [value] + [self.swap(value, bits, g) for g in range(1, 1 << len(bits))]
        while len(got) > 1:
            got = [got[i] + got[i + 1] for i in range(0, len(got), 2)]
        return got[0]

    def digits(self):
        found = []
        for bits in (self.stages + self.rest)[::-1]:
            found = found + bits
        return found

    def own_list(self):
        return [("own", b) for b in self.own_bits]


def plan_kernel(cuts_soon, steps_last, slots, owner, seat, table):
    blocks = owner.shape[0]
    for i in range(4):
        table[2, i] = seat[i]
    count = jnp.int32(0)
    mine = []
    for b in range(blocks):
        here = (owner[b] == seat[4]).astype(jnp.int32)
        table[0, b] = count * here
        table[1, b] = here
        mine.append((here, count))
        count = count + here

    def fill(row, cuts, entries):
        left = jnp.int32(0)
        for here, *_ in entries:
            left = left + here
        steps = cuts[-1]
        for i in range(steps):
            for k in range(3):
                table[row + k, i] = 0
        ends = []
        for c in range(len(cuts) - 1):
            room, calls = cuts[c + 1] - cuts[c], len(cuts) - 1 - c
            part = jnp.minimum(room, (left + calls - 1) // calls)
            part = jnp.maximum(part, left - (steps - cuts[c + 1]))
            ends.append(cuts[c] + part)
            left = left - part
        at = jnp.int32(0)
        for c in range(len(ends) - 1):
            at = jnp.where(at == ends[c], cuts[c + 1], at)
        for here, slot, kind, block in entries:
            @pl.when(here > 0)
            def _(at=at, slot=slot, kind=kind, block=block):
                table[row, at] = slot
                table[row + 1, at] = kind
                table[row + 2, at] = block

            at = at + here
            for c in range(len(ends) - 1):
                at = jnp.where(at == ends[c], cuts[c + 1], at)
        for i in range(1, steps):
            @pl.when(table[row + 1, i] == 0)
            def _(i=i):
                table[row, i] = table[row, i - 1]
                table[row + 2, i] = table[row + 2, i - 1]

    first_ada = LATE + EARLY
    soon = [(*mine[LATE + n], 1, n) for n in range(EARLY)]
    soon += [(*mine[first_ada + n], 2, n - 2) for n in range(2, blocks - first_ada)]
    for i in range(slots):
        soon.append(((i >= count).astype(jnp.int32), i, 3, 0))
    fill(3, cuts_soon, soon)
    last = [(*mine[first_ada + n], 2, n) for n in range(2)]
    last += [(*mine[n], 1, n) for n in range(LATE)]
    fill(6, [0, steps_last], last)


def make_plan(owner, seat, slots, cuts_soon, steps_last):
    smem = pl.BlockSpec(memory_space=pltpu.SMEM)
    return pl.pallas_call(
        functools.partial(plan_kernel, cuts_soon, steps_last, slots),
        in_specs=[smem, smem],
        out_specs=smem,
        out_shape=shape((9, max(32, slots)), jnp.int32),
        name="plan",
    )(owner, seat)


def pick_kernel(groups, table, *refs):
    refs = list(refs)
    outs = refs[-len(groups) :]
    for out, (blocks, _) in zip(outs, groups):
        for i, b in enumerate(blocks):
            kept = jnp.where(table[1, b] > 0, 1.0, 0.0)
            out[i] = (refs.pop(0)[0] * kept).astype(bf16)


def pick_blocks(table, master, *groups):
    dims = [(len(blocks), rows, D) for blocks, rows in groups]
    specs = [
        pl.BlockSpec((1, rows, D), lambda i, t, b=b, rows=rows: (t[0, b], t[2, 0] if rows < D else 0, 0))
        for blocks, rows in groups
        for b in blocks
    ]
    return pl.pallas_call(
        functools.partial(pick_kernel, groups),
        grid_spec=pltpu.PrefetchScalarGridSpec(
            num_scalar_prefetch=1,
            grid=(1,),
            in_specs=specs,
            out_specs=[pl.BlockSpec(d, lambda i, t: (0, 0, 0)) for d in dims],
        ),
        out_shape=[shape(d, bf16) for d in dims],
        compiler_params=params(),
        cost_estimate=cost(0, 6 * sum(d[0] * d[1] * D for d in dims)),
        name="pick_blocks",
    )(table, *([master] * len(specs)))


def join_halves(core, near, far, out):
    out[:, pl.ds(pl.multiple_of(core * HALF, HALF), HALF), :] = near[...]
    out[:, pl.ds(pl.multiple_of((1 - core) * HALF, HALF), HALF), :] = far[...]


def normed(value):
    centered = value - jnp.mean(value, axis=-1, keepdims=True)
    inverse = lax.rsqrt(jnp.mean(centered * centered, axis=-1, keepdims=True) + norm_eps)
    return centered * inverse, inverse


def norm_back(gradient, norm, inverse):
    return inverse * (
        gradient
        - jnp.mean(gradient, axis=-1, keepdims=True)
        - norm * jnp.mean(gradient * norm, axis=-1, keepdims=True)
    )


def attend_kernel(core, latents, mod, near, far, bias, qkv, mixed, total, first_in, weight):
    @pl.when(pl.program_id(0) == 0)
    def _():
        join_halves(core[2, 0], near, far, weight)

    norm, _ = normed(latents[0].astype(f32))
    first = (norm * (1.0 + mod[0, 1:2]) + mod[0, 0:1]).astype(bf16)
    first_in[0] = first.T
    for b in range(3):
        qkv[0, :, b * D : (b + 1) * D] = (dot(first, weight[b]) + bias[:, b * D : (b + 1) * D]).astype(bf16)
    total[0] = jnp.zeros_like(total[0])

    head_of = lax.broadcasted_iota(jnp.int32, (D, 2 * HD), 0) // HD
    marks = jnp.where(
        head_of == lax.broadcasted_iota(jnp.int32, (D, 2 * HD), 1), 1.0, 0.0
    ).astype(bf16)

    def longest(block):
        value = qkv[0, :, block * D : (block + 1) * D].astype(f32)
        return jnp.max(dot((value * value).astype(bf16), marks), axis=0, keepdims=True)

    bound = jnp.max(longest(0) * longest(1)) * (1.05 / HD)
    small = bound < LIMIT * LIMIT

    def heads(shifted):
        lane = lax.broadcasted_iota(jnp.int32, (1, 2 * HD), 1)
        values_t = qkv[0, :, 2 * D : 3 * D].T
        for p in range(H // 2):
            keys = qkv[0, :, D + 2 * HD * p : D + 2 * HD * (p + 1)]
            pair = qkv[0, :, 2 * HD * p : 2 * HD * (p + 1)]
            for h in range(2):
                j = 2 * p + h
                mask = jnp.where((lane < HD) == (h == 0), HD**-0.5, 0.0).astype(bf16)
                scores = dot(keys, pair * mask, NT)
                peak = 0.0
                if shifted:
                    peak = jnp.max(scores, axis=0, keepdims=True)
                    scores = scores - peak
                expo = jnp.exp(scores)
                sums = jnp.sum(expo, axis=0, keepdims=True)
                prob = (expo * (1.0 / sums)).astype(bf16)
                out = dot(values_t[HD * j : HD * (j + 1)], prob)
                mixed[0, HD * j : HD * (j + 1), :] = out.astype(bf16)
                total[0, j : j + 1, :] = peak + jnp.log(sums)

    @pl.when(small)
    def _():
        heads(False)

    @pl.when(jnp.logical_not(small))
    def _():
        heads(True)


def middle_kernel(
    seqs,
    core,
    latents,
    upstream,
    mixed,
    mod,
    near,
    near_come,
    far,
    far_come,
    bias,
    cond,
    block_out,
    residual_back,
    mixed_back,
    keep,
    send,
    grad_late,
    small,
    proj,
    up,
    down,
    total,
    sums,
    bias_sums,
    second_s,
    act_s,
    pre_s,
    sems,
):
    seq, step = pl.program_id(0), pl.program_id(1)

    @pl.when((seq == 0) & (step == 0))
    def _():
        for half, ref, come in ((core[2, 0], near, near_come), (1 - core[2, 0], far, far_come)):
            at = pl.multiple_of(half * HALF, HALF)
            proj[pl.ds(at, HALF), :] = ref[0] + come[0]
            for n in range(FB):
                up[pl.ds(at, HALF), n * D : (n + 1) * D] = ref[1 + n] + come[1 + n]
                down[pl.ds(n * D + at, HALF), :] = ref[1 + FB + n] + come[1 + FB + n]
        total[...] = jnp.zeros_like(total)
        grad_late[...] = jnp.zeros_like(grad_late)
        bias_sums[...] = jnp.zeros_like(bias_sums)

    gate_one, shift_two, scale_two, gate_two = (mod[0, i : i + 1] for i in (2, 3, 4, 5))
    bias_up = bias[:, 4 * D : 4 * D + FF]

    def column(value):
        return jnp.sum(value, axis=0, keepdims=True)

    attn_out = dot(mixed[0], proj[...], TN) + bias[:, 3 * D : 4 * D]
    residual = latents[0].astype(f32) + gate_one * attn_out
    norm, inverse = normed(residual)
    second = (norm * (1.0 + scale_two) + shift_two).astype(bf16)
    second_s[...] = second
    ct = upstream[0].astype(f32)
    ffn_back = (ct * gate_two).astype(bf16)
    pre = dot(second, up[...]) + bias_up
    square = pre * pre
    k0 = 0.7978845608028654
    tanh = jnp.tanh(pre * (k0 + (k0 * 0.044715) * square))
    half = 0.5 + 0.5 * tanh
    act_s[...] = (pre * half).astype(bf16)
    slope = half + pre * (0.5 - 0.5 * tanh * tanh) * (k0 + (3.0 * k0 * 0.044715) * square)
    ffn_out = dot(act_s[...], down[...]) + bias[:, 4 * D + FF : 5 * D + FF]
    pre_back = (dot(ffn_back, down[...], NT) * slope).astype(bf16)
    pre_s[...] = pre_back
    low_pre = column(pre_back.astype(f32))
    second_back = dot(pre_back, up[...], NT)
    block_out[0] = (residual + gate_two * ffn_out).astype(bf16)
    res_back = ct + norm_back(second_back * (1.0 + scale_two), norm, inverse)
    residual_back[0] = res_back
    attn_back = (res_back * gate_one).astype(bf16)
    mixed_back[0] = dot(attn_back, proj[...], NT).astype(bf16)
    both = jnp.concatenate(
        [
            column(res_back * attn_out),
            column(second_back),
            column(second_back * norm),
            column(ct * ffn_out),
        ],
        axis=0,
    )
    bias_sums[...] += jnp.concatenate(
        [column(attn_back.astype(f32))]
        + [low_pre[:, n * D : (n + 1) * D] for n in range(FB)]
        + [column(ffn_back.astype(f32))],
        axis=0,
    )

    for n in range(seqs):
        @pl.when(seq == n)
        def _(n=n):
            sums[n] = jnp.where(step == 0, both, sums[n] + both)

    grad_late[0] += dot(mixed[0], attn_back)
    grad_up = dot(second_s[...], pre_s[...], TN)
    grad_down_t = dot(ffn_back, act_s[...], TN)
    side = core[2, 0] * FB
    for n in range(FB):
        cols = slice(n * D, (n + 1) * D)
        total[side + n] += grad_up[:, cols]
        total[FB - side + n] += grad_down_t[:, cols].T

    @pl.when((seq == pl.num_programs(0) - 1) & (step == pl.num_programs(1) - 1))
    def _():
        copies = [
            pltpu.make_async_copy(total.at[pl.ds(i * FB, FB)], out, sems.at[i])
            for i, out in enumerate((keep, send))
        ]
        for copy in copies:
            copy.start()
        rows = [jnp.concatenate([sums[n], cond[n : n + 1]], axis=0) for n in range(seqs)]
        rows.append(bias_sums[...])
        filled = seqs * 5 + FB + 2
        if small.shape[0] > filled:
            rows.append(jnp.zeros((small.shape[0] - filled, D), f32))
        small[...] = jnp.concatenate(rows, axis=0).astype(bf16)
        for copy in copies:
            copy.wait()


def attend_back_kernel(begin, first_pair, query, keys, values, back, total, first, *rest):
    grads_in, biases_in = rest[:2]
    back_query, back_keys, back_values, grads, biases = rest[-5:]
    pair = first_pair + pl.program_id(0)
    lane = lax.broadcasted_iota(jnp.int32, (1, 2 * HD), 1)
    keys_t = keys[0].T
    key_sum = value_sum = 0.0
    query_parts = []
    for h in range(2):
        one = jnp.where((lane < HD) == (h == 0), 1.0, 0.0).astype(bf16)
        q = query[0] * (one * HD**-0.5)
        g = back[0] * one
        prob = jnp.exp(dot(keys[0], q, NT) - total[0, pl.ds(2 * pair + h, 1)])
        prob_back = dot(values[0], g, NT)
        row_delta = jnp.sum(prob * prob_back, axis=0, keepdims=True)
        score_back = (prob * (prob_back - row_delta)).astype(bf16)
        value_sum = value_sum + dot(prob.astype(bf16), g)
        key_sum = key_sum + dot(score_back, q)
        query_parts.append(dot(keys_t[HD * h : HD * (h + 1)], score_back))
    low = (
        (jnp.concatenate(query_parts, axis=0) * HD**-0.5).T.astype(bf16),
        key_sum.astype(bf16),
        value_sum.astype(bf16),
    )
    for out, value in zip((back_query, back_keys, back_values), low):
        out[0] = value
    joined = jnp.concatenate(low, axis=1)
    new = dot(first[0], joined)
    sums = jnp.sum(joined.astype(f32), axis=0, keepdims=True)
    width = 2 * HD
    for i in range(3):
        cols = slice(i * width, (i + 1) * width)
        grads[i] = new[:, cols] if begin else grads_in[i] + new[:, cols]
        biases[i : i + 1] = sums[:, cols] if begin else biases_in[i : i + 1] + sums[:, cols]


def first_back_kernel(
    n, final, table, latents, residual_back, mod, back_query, back_keys, back_values, near, far, biases, *rest
):
    latents_grad, small, weight, sums = rest[-4:]

    @pl.when(pl.program_id(0) == 0)
    def _():
        join_halves(table[2, 0], near, far, weight)
        sums[...] = jnp.zeros_like(sums)

    norm, inverse = normed(latents[0].astype(f32))
    first_back = (
        dot(back_query[0], weight[0], NT)
        + dot(back_keys[0], weight[1], NT)
        + dot(back_values[0], weight[2], NT)
    )
    sums[0:1] += jnp.sum(first_back, axis=0, keepdims=True)
    sums[1:2] += jnp.sum(first_back * norm, axis=0, keepdims=True)
    latents_grad[0] = residual_back[0] + norm_back(
        first_back * (1.0 + mod[0, 1:2]), norm, inverse
    )

    @pl.when(pl.program_id(0) == pl.num_programs(0) - 1)
    def _():
        rows = [rest[0][: 2 * n]] if n else []
        rows.append(sums[0:2])
        if final:
            rows += [part.astype(f32) for part in split_two(biases[0:3])]
        filled = 2 * n + 2 + (6 if final else 0)
        rows.append(jnp.zeros((small.shape[0] - filled, D), f32))
        small[...] = jnp.concatenate(rows, axis=0).astype(small.dtype)


def split_two(value):
    high = value.astype(bf16)
    return high, (value - high.astype(f32)).astype(bf16)


def small_spec(half, rows):
    dims = (*half.shape[:-2], half.shape[-2] - rows, D)
    return whole(*dims)


def joined(near, far):
    return jnp.concatenate([near[...].reshape(-1, D), far[...].reshape(-1, D)], axis=0)


def chosen_rows(rows, count, seqs, me, group, per, kind):
    latent = lax.broadcasted_iota(jnp.int32, (count, rows.shape[0]), 0)
    wanted = (latent // seqs ^ me) * group + latent % seqs * per + kind
    hit = wanted == lax.broadcasted_iota(jnp.int32, (count, rows.shape[0]), 1)
    return dot(jnp.where(hit, 1.0, 0.0).astype(bf16), rows)


def slots_kernel(
    row, begin, room, pieces, stages, line, small, table, *refs
):
    cond_halves, mod_halves, (near, far) = refs[:2], refs[2:4], refs[4:6]
    state, outs = refs[6:11], refs[-9:-5]
    held, gradient_in, made, in_sems, out_sems = refs[-5:]
    cond_group, mod_group, per, seqs = small
    rows = D // pieces
    count = jnp.int32(0)
    for i in range(room):
        count = count + (table[row + 1, begin + i] > 0).astype(jnp.int32)

    def piece(half, i, p, buf):
        shard = table[row + 2, begin + i] * pieces + p
        at = ((shard // line & 3) ^ table[2, 1], (shard & 3) ^ table[2, 2])[:stages]
        return pltpu.make_async_copy(
            half.at[(*at, pl.ds(half.shape[-2] - rows, rows))],
            gradient_in.at[buf, pl.ds(p * rows, rows)],
            in_sems.at[buf, 5 + p],
        )

    def arriving(i, k, buf):
        return pltpu.make_async_copy(
            state[k].at[table[row, begin + i]], held.at[buf, k], in_sems.at[buf, k]
        )

    def leaving(i, k, buf):
        return pltpu.make_async_copy(
            made.at[buf, k], outs[k].at[table[row, begin + i]], out_sems.at[buf, k]
        )

    def fetch(i, buf):
        side = (table[row + 2, begin + i] * pieces // (4 * line)) ^ table[2, 0]
        for number, half in enumerate((near, far)):
            @pl.when((table[row + 1, begin + i] == 1) & (side == number))
            def _(half=half):
                for p in range(pieces):
                    piece(half, i, p, buf).start()

        for k in (2, 3, 4, 0, 1):
            arriving(i, k, buf).start()

    @pl.when(count > 0)
    def _():
        fetch(0, 0)

    def one(i, carry):
        buf = i & 1
        kind = table[row + 1, begin + i]

        @pl.when(i + 1 < count)
        def _():
            fetch(i + 1, 1 - buf)

        @pl.when(i >= 2)
        def _():
            for k in range(4):
                leaving(i - 2, k, buf).wait()

        @pl.when(kind == 1)
        def _():
            for p in range(pieces):
                piece(near, i, p, buf).wait()
            made[buf, 0] = gradient_in[buf].astype(f32)

        @pl.when(kind == 2)
        def _():
            conds, mods = joined(*cond_halves), joined(*mod_halves)
            total = conds.shape[0] // cond_group * seqs
            me, block = table[2, 3], table[row + 2, begin + i]
            cond = chosen_rows(conds, total, seqs, me, cond_group, 5, 4).astype(bf16)
            mod = chosen_rows(mods, total, seqs, me, mod_group, per, block).astype(bf16)
            made[buf, 0] = dot(cond, mod, TN)

        @pl.when(kind == 3)
        def _():
            made[buf, 0] = jnp.zeros((D, D), f32)

        leaving(i, 0, buf).start()
        low = made[buf, 0].astype(bf16)
        arriving(i, 2, buf).wait()
        turned = low.T
        two = dot(jnp.concatenate([held[buf, 2].astype(bf16), turned], axis=0), low)
        arriving(i, 3, buf).wait()
        direction = dot(two[:D].astype(bf16), held[buf, 3].astype(bf16))
        arriving(i, 4, buf).wait()
        weight = held[buf, 4]
        scale = jnp.sqrt(jnp.mean(weight * weight) + norm_eps) * lax.rsqrt(
            jnp.mean(direction * direction) + norm_eps
        )
        made[buf, 3] = weight - shampoo_rate * (scale * direction + shampoo_decay * weight)
        leaving(i, 3, buf).start()
        arriving(i, 0, buf).wait()
        made[buf, 1] = 0.5 * held[buf, 0] + 0.5 * dot(low, turned)
        leaving(i, 1, buf).start()
        arriving(i, 1, buf).wait()
        made[buf, 2] = 0.5 * held[buf, 1] + 0.5 * two[D:]
        leaving(i, 2, buf).start()
        return carry

    lax.fori_loop(0, count, one, 0)
    for back in (2, 1):
        @pl.when(count >= back)
        def _(back=back):
            for k in range(4):
                leaving(count - back, k, (count - back) & 1).wait()


def slots_call(row, begin, steps, table, small, gathered, rows, state, outs, ties, name):
    slots = state[0].shape[0]
    pieces = D // rows
    stages = gathered[0].ndim - 2
    line = gathered[0].shape[1] if stages > 1 else 1
    conds, mods, cond_rows, *small = small
    given = [] if outs is None else list(outs)
    anyplace = pl.BlockSpec(memory_space=pl.ANY)
    more = given + list(ties)
    return pl.pallas_call(
        functools.partial(slots_kernel, row, begin, steps, pieces, stages, line, small),
        grid=(1,),
        in_specs=[pl.BlockSpec(memory_space=pltpu.SMEM)]
        + [small_spec(half, cond_rows) for half in conds]
        + [small_spec(half, rows) for half in mods]
        + [anyplace] * (7 + len(more)),
        out_specs=[anyplace] * 4,
        out_shape=[shape((slots, D, D))] * 4,
        scratch_shapes=[
            pltpu.VMEM((2, 5, D, D), f32),
            pltpu.VMEM((2, D, D), bf16),
            pltpu.VMEM((2, 4, D, D), f32),
            pltpu.SemaphoreType.DMA((2, 5 + pieces)),
            pltpu.SemaphoreType.DMA((2, 4)),
        ],
        input_output_aliases={12 + i: i for i in range(len(given))},
        compiler_params=params(),
        cost_estimate=cost(steps * 7 * 2 * D**3, steps * 10 * D * D * 4),
        name=name,
    )(table, *conds, *mods, *gathered, *state, *more)


def finish_kernel(
    seqs,
    group,
    soon_group,
    last_group,
    table,
    soon_near,
    soon_far,
    last_near,
    last_far,
    ada,
    bias,
    one,
    two,
    grad_out,
    one_out,
    two_out,
    bias_out,
    cond_out,
):
    me = table[2, 3]
    soon, last = joined(soon_near, soon_far), joined(last_near, last_far)
    devices = soon.shape[0] // soon_group

    def totals(rows, each_group, kinds):
        count = len(kinds) * devices
        at = lax.broadcasted_iota(jnp.int32, (count, rows.shape[0]), 0)
        first = kinds[0]
        assert list(kinds) == list(range(first, first + len(kinds)))
        wanted = (at % devices ^ me) * each_group + at // devices + first
        hit = wanted == lax.broadcasted_iota(jnp.int32, (count, rows.shape[0]), 1)
        found = dot(jnp.where(hit, 1.0, 0.0).astype(bf16), rows)
        return [
            jnp.sum(found[k * devices : (k + 1) * devices], axis=0, keepdims=True)
            for k in range(len(kinds))
        ]

    of_soon = totals(soon, soon_group, range(0, seqs * 5 + FB + 2))
    of_last = totals(last, last_group, range(0, seqs * 2 + 6))
    qkv = [of_last[seqs * 2 + i] + of_last[seqs * 2 + 3 + i] for i in range(3)]
    mods = [sum(of_last[n * 2 + i] for n in range(seqs)) for i in range(2)]
    mods += [sum(of_soon[n * 5 + i] for n in range(seqs)) for i in range(4)]
    grad = jnp.concatenate(qkv + of_soon[seqs * 5 : seqs * 5 + FB + 2] + mods, axis=1)
    grad = grad.reshape(-1)
    grad_out[...] = grad
    one_new = 0.9 * one[...] + 0.1 * grad
    two_new = 0.95 * two[...] + 0.05 * grad * grad
    one_out[...] = one_new
    two_out[...] = two_new
    corrected = (
        one_new / (1.0 - 0.9**STEP) / (jnp.sqrt(two_new / (1.0 - 0.95**STEP)) + 1e-08)
    )
    bias_out[...] = bias[...] - adam_rate * (corrected + adam_decay * bias[...])
    for g, device in enumerate(group):
        total = 0.0
        for b in range(ada.shape[0]):
            rows, each_group, per, kind = (
                (last, last_group, 2, b) if b < 2 else (soon, soon_group, 5, b - 2)
            )
            base = device * each_group
            mine = jnp.concatenate(
                [rows[base + n * per + kind : base + n * per + kind + 1] for n in range(seqs)]
                + [jnp.zeros((8 - seqs, D), bf16)],
                axis=0,
            )
            total = total + dot(mine, ada[b], NT)
        cond_out[g * seqs : (g + 1) * seqs] = total[:seqs]


def finish(
    table, soon, last, soon_after, last_after, ada, bias, one, two, seqs, group, soon_group, last_group
):
    inputs = (ada, bias, one, two)
    outs = [shape(bias.shape)] * 4 + [shape((len(group) * seqs, D))]
    return pl.pallas_call(
        functools.partial(finish_kernel, seqs, group, soon_group, last_group),
        grid=(1,),
        in_specs=[pl.BlockSpec(memory_space=pltpu.SMEM)]
        + [small_spec(half, soon_after) for half in soon]
        + [small_spec(half, last_after) for half in last]
        + [whole(*v.shape) for v in inputs],
        out_specs=[whole(*v.shape) for v in outs],
        out_shape=outs,
        compiler_params=params(),
        cost_estimate=cost(1e8, 2e6),
        name="finish",
    )(table, *soon, *last, *inputs)


def whole(*dims):
    return pl.BlockSpec(dims, lambda *_: (0,) * len(dims))


def each(*dims):
    return pl.BlockSpec((1,) + dims, lambda i, *_: (i,) + (0,) * len(dims))


def middle(rows, table, latents, cotangent, mixed, modulation, rest, bias_row, cond, small_rows):
    seqs, length, _ = latents.shape
    tok = pl.BlockSpec((1, rows, D), lambda i, j: (i, j, 0))
    anyplace = pl.BlockSpec(memory_space=pl.ANY)
    return pl.pallas_call(
        functools.partial(middle_kernel, seqs),
        grid=(seqs, length // rows),
        in_specs=[
            pl.BlockSpec(memory_space=pltpu.SMEM),
            tok,
            tok,
            pl.BlockSpec((1, D, rows), lambda i, j: (i, 0, j)),
            each(6, D),
            *[whole(1 + EARLY, HALF, D)] * 4,
            whole(*bias_row.shape),
            whole(*cond.shape),
        ],
        out_specs=[
            tok,
            tok,
            tok,
            anyplace,
            anyplace,
            pl.BlockSpec((1, D, D), lambda *_: (LATE - 1, 0, 0)),
            whole(small_rows, D),
        ],
        out_shape=[
            shape((seqs, length, D), bf16),
            shape((seqs, length, D)),
            shape((seqs, length, D), bf16),
            shape((FB, D, D)),
            shape((FB, D, D)),
            shape((LATE, D, D)),
            shape((small_rows, D), bf16),
        ],
        scratch_shapes=[
            pltpu.VMEM((D, D), bf16),
            pltpu.VMEM((D, FF), bf16),
            pltpu.VMEM((FF, D), bf16),
            pltpu.VMEM((2 * FB, D, D), f32),
            pltpu.VMEM((seqs, 4, D), f32),
            pltpu.VMEM((FB + 2, D), f32),
            pltpu.VMEM((rows, D), bf16),
            pltpu.VMEM((rows, FF), bf16),
            pltpu.VMEM((rows, FF), bf16),
            pltpu.SemaphoreType.DMA((2,)),
        ],
        compiler_params=params(),
        cost_estimate=cost(22e9, 25e6, 3e6),
        name="middle",
    )(table, latents, cotangent, mixed, modulation, *rest, bias_row, cond)


def per_device(
    net,
    latents,
    condition,
    cotangent,
    owner,
    master,
    stat_left,
    stat_right,
    root_left,
    root_right,
    bias,
    moment_one,
    moment_two,
):
    slots = master.shape[0]
    seqs, length, _ = latents.shape
    blocks = owner.shape[0]
    first_ada = LATE + EARLY
    ada = blocks - first_ada
    own_all = net.own_list()
    steps_last = min(slots, 2 + LATE)
    anyplace = pl.BlockSpec(memory_space=pl.ANY)
    smem = pl.BlockSpec(memory_space=pltpu.SMEM)
    tok = each(length, D)
    soon_rows = -(-(seqs * 5 + FB + 2) // 16) * 16
    last_rows = -(-(seqs * 2 + 2 * 3) // 16) * 16

    seat = jnp.stack(
        [net.place(bits) for bits in net.stages]
        + [net.place(net.digits()), lax.axis_index("own").astype(jnp.int32)]
    )
    cuts = [0, max(1, slots // 5), max(2, slots // 2), slots]
    table = make_plan(owner, seat, slots, cuts, steps_last)

    (near_qkv,) = pick_blocks(table, master, (list(range(3)), HALF))
    (own_ada,) = pick_blocks(table, master, (list(range(first_ada, blocks)), D))
    (near_rest,) = pick_blocks(table, master, (list(range(3, first_ada)), HALF))
    for bit in own_all:
        near_qkv = near_qkv + tie(net.swap(near_qkv, [bit], 1), near_rest)
    far_qkv = net.swap(near_qkv, net.stages[0], 1)

    bias_row = bias.reshape(1, -1)
    cond_float = condition.astype(f32)
    silu_cond, silu_pull = jax.vjp(jax.nn.silu, cond_float)
    cond_low = silu_cond.astype(bf16)
    cond_group = net.gather(cond_low, own_all)
    mod_parts = jnp.einsum("gld,bde->glbe", cond_group, own_ada, preferred_element_type=f32)
    modulation = mod_parts[0]
    for g in range(1, net.n_own):
        modulation = modulation + net.swap(mod_parts[g], own_all, g)
    modulation = modulation + bias[5 * D + FF :].reshape(ada, D)

    near_rest = tie(near_rest, near_qkv, modulation)
    for bit in own_all[:-1]:
        near_rest = near_rest + net.swap(near_rest, [bit], 1)
    far_rest = net.swap(near_rest, net.stages[0], 1)
    near_come = net.swap(near_rest, own_all[-1:], 1)

    qkv, mixed, totals, first_in = pl.pallas_call(
        attend_kernel,
        grid=(seqs,),
        in_specs=[
            smem,
            tok,
            each(6, D),
            whole(3, HALF, D),
            whole(3, HALF, D),
            whole(*bias_row.shape),
        ],
        out_specs=[each(length, 3 * D), each(D, length), each(8, length), each(D, length)],
        out_shape=[
            shape((seqs, length, 3 * D), bf16),
            shape((seqs, D, length), bf16),
            shape((seqs, 8, length)),
            shape((seqs, D, length), bf16),
        ],
        scratch_shapes=[pltpu.VMEM((3, D, D), bf16)],
        compiler_params=params(),
        cost_estimate=cost(16e9, 12e6, 12e6),
        name="attend",
    )(table, latents, modulation, near_qkv, far_qkv, bias_row)

    near_come = tie(near_come, qkv)
    rest = (near_rest, near_come, far_rest, net.swap(near_come, net.stages[0], 1))

    (
        block_out,
        residual_back,
        mixed_back,
        early_keep,
        early_send,
        grad_late,
        small_soon,
    ) = middle(
        length,
        table,
        latents,
        cotangent,
        mixed,
        modulation,
        rest,
        bias_row,
        cond_low.astype(f32),
        soon_rows,
    )

    def core_stage(grads, *others):
        return net.scatter_sum(grads.reshape(2, -1, D), net.stages[0], f32, *others)

    def plane_stage(value, *others):
        return net.scatter_sum(value.reshape(4, -1, D), net.stages[1], bf16, *others)

    def line_stage(value, *others):
        value = net.scatter_sum(value.reshape(4, -1, D), net.stages[2], bf16, *others)
        for bits in net.rest:
            value = net.add_up(value, bits)
        return value.astype(bf16)

    def with_small(value, small):
        for bits in net.rest[::-1]:
            small = net.gather(small, bits)
        return jnp.concatenate([small.reshape(-1, D), value], axis=0)

    def line_exchange(value, small, others):
        sent = with_small(value.astype(bf16), small)
        rows = sent.shape[0] - value.shape[0]
        got = net.gather(sent, net.stages[2], *others)
        value = (got[0, rows:].astype(f32) + got[1, rows:]) + (got[2, rows:].astype(f32) + got[3, rows:])
        for bits in net.rest:
            value = net.add_up(value, bits)
        return jnp.concatenate([got[:, :rows].reshape(-1, D), value.astype(bf16)], axis=0)

    def back_pairs(n, first_pair, count, carried, ties):
        def head(offset):
            return pl.BlockSpec((1, length, 2 * HD), lambda i: (n, 0, offset + first_pair + i))

        def latent(*dims):
            return pl.BlockSpec((1,) + dims, lambda i: (n, 0, 0))

        begin = n == 0
        grad_spec = pl.BlockSpec((3, D, 2 * HD), lambda i: (0, 0, first_pair + i))
        bias_spec = pl.BlockSpec((8, 2 * HD), lambda i: (0, first_pair + i))
        return pl.pallas_call(
            functools.partial(attend_back_kernel, begin, first_pair),
            grid=(count,),
            in_specs=[head(0), head(3), head(6), head(0), latent(8, length), latent(D, length)]
            + ([anyplace] * 2 if begin else [grad_spec, bias_spec])[: len(carried)]
            + [anyplace] * (len(carried[2:]) + len(ties)),
            out_specs=[head(0)] * 3 + [grad_spec, bias_spec],
            out_shape=[shape((seqs, length, D), bf16)] * 3 + [shape((LATE, D, D)), shape((8, D))],
            input_output_aliases={6 + i: at for i, at in enumerate((3, 4, 0, 1, 2)[: len(carried)])},
            compiler_params=params(),
            cost_estimate=cost(count * 7e9, count * 3e6, count * 2e6),
            name="attend_back",
        )(qkv, qkv, qkv, mixed_back, totals, first_in, *carried, *ties)

    def first_back(n, backs, carried, ties):
        rows = length // 2
        final = n == seqs - 1
        part = pl.BlockSpec((1, rows, D), lambda i: (n, i, 0))
        grad, small = carried if carried else (None, None)
        more = ([small, grad] if n else []) + ties
        specs = ([whole(*small.shape), anyplace] if n else []) + [anyplace] * len(ties)
        return pl.pallas_call(
            functools.partial(first_back_kernel, n, final),
            grid=(2,),
            in_specs=[smem, part, part, pl.BlockSpec((1, 6, D), lambda i: (n, 0, 0))]
            + [part] * 3
            + [whole(3, HALF, D)] * 2
            + [whole(8, D)]
            + specs,
            out_specs=[part, whole(last_rows, D)],
            out_shape=[
                shape((seqs, length, D)),
                shape((last_rows, D), bf16 if final else f32),
            ],
            input_output_aliases={11: 0} if n else {},
            scratch_shapes=[pltpu.VMEM((3, D, D), bf16), pltpu.VMEM((8, D), f32)],
            compiler_params=params(),
            cost_estimate=cost(3.5e9, 9e6),
            name="first_back",
        )(
            table,
            latents,
            residual_back,
            modulation,
            *backs[:3],
            near_qkv,
            far_qkv,
            backs[4],
            *more,
        )

    def swapped(backs):
        return [backs[3], backs[4], *backs[:3]]

    early = early_keep
    stages = [
        lambda value: value + net.swap(early_send, net.stages[0], 1),
        plane_stage,
        lambda value: with_small(line_stage(value), small_soon),
        lambda value: net.gather(value, net.stages[2]),
    ]
    def after_stage(*others):
        nonlocal early
        if stages:
            early = stages.pop(0)(early)
            return [early, *others]
        return list(others)

    backs = [None] * 3 + [grad_late]
    firsts = []
    for n in range(seqs):
        for first_pair, count in ((0, 1), (1, 2)) if n == 0 else ((0, 1), (1, 1), (2, 1)):
            if n + first_pair == 0:
                carried, ties = [grad_late], []
            else:
                carried = swapped(backs)
                last = n > 0 and first_pair == 2
                ties = [] if last else after_stage(*(firsts[:1] if first_pair == 0 else []))
            backs = back_pairs(n, first_pair, count, carried, ties)
        if n < seqs - 1:
            firsts = first_back(n, backs, firsts, after_stage())
    for stage in stages:
        early = stage(early)
    pieces = [net.swap(early, net.stages[1], g) for g in range(1, 4)]
    pieces, grad_late = tie((pieces, backs[3]), backs[0])
    early = jnp.stack([early] + pieces)
    latents_grad, small_last = first_back(seqs - 1, backs, firsts, [])
    late = core_stage(grad_late, latents_grad)
    early = (early, net.swap(early, net.stages[0], 1))
    early_rows = EARLY * D // 32
    late_rows = LATE * D // 8
    state = (stat_left, stat_right, root_left, root_right, master)
    def soon_slots(i, outs, ties):
        return slots_call(
            3,
            cuts[i],
            cuts[i + 1] - cuts[i],
            table,
            (early, early, early_rows, soon_rows, soon_rows, 5, seqs),
            early,
            early_rows,
            state,
            outs,
            ties,
            "soon_slots",
        )

    outs = soon_slots(0, None, [late])
    late = plane_stage(late, *outs)
    outs = soon_slots(1, outs, [late])
    late = line_exchange(late, small_last, outs)
    outs = soon_slots(2, outs, [late])
    late = net.gather(late, net.stages[1], *outs)
    late = (late, net.swap(late, net.stages[0], 1))
    group = []
    for g in range(net.n_own):
        group.append(
            sum(1 << k for k, (axis, bit) in enumerate(net.digits()) if axis == "own" and g & bit)
        )

    bias_outs = finish(
        table,
        early,
        late,
        early_rows,
        late_rows,
        own_ada,
        bias,
        moment_one,
        moment_two,
        seqs,
        group,
        soon_rows,
        last_rows,
    )
    *bias_outs, cond_parts = bias_outs
    bias_grad, moment_one_new, moment_two_new, bias_new = bias_outs
    weight_grads, left_new, right_new, master_new = slots_call(
        6,
        0,
        steps_last,
        table,
        (early, late, early_rows, soon_rows, last_rows, 2, seqs),
        late,
        late_rows,
        state,
        outs,
        [bias_grad],
        "last_slots",
    )

    cond_parts = tie(cond_parts, weight_grads).reshape(net.n_own, seqs, D)
    back_cond = cond_parts[0]
    for g in range(1, net.n_own):
        back_cond = back_cond + net.swap(cond_parts[g], own_all, g)
    condition_grad = silu_pull(back_cond)[0]
    return (
        block_out,
        latents_grad,
        condition_grad,
        weight_grads,
        left_new,
        right_new,
        master_new,
        bias_grad,
        moment_one_new,
        moment_two_new,
        bias_new,
    )


def solution(mesh):
    net = Net(mesh.shape["dp"], mesh.shape["own"])
    token = P(("dp", "own"), None, None)
    slot = P("own", None, None)
    return jax.shard_map(
        functools.partial(per_device, net),
        mesh=mesh,
        in_specs=(token, P(("dp", "own"), None), token, P()) + (slot,) * 5 + (P(),) * 3,
        out_specs=(token, token, P(("dp", "own"), None)) + (slot,) * 4 + (P(),) * 4,
        check_vma=False,
    )
```

```python
import functools

import jax
import jax.numpy as jnp
from jax import lax
from jax.experimental import pallas as pl
from jax.experimental.pallas import tpu as pltpu
from jax.sharding import PartitionSpec as P

D = 384
H = 6
HD = 64
FF = 1536
FB = FF // D
STEP = 10
HALF = D // 2
LATE = 4
EARLY = 2 * FB

SHRINK = 2.5

norm_eps = 1e-06
shampoo_rate = 1.0
shampoo_decay = 0.01
adam_rate = 0.2
adam_decay = 0.01
f32 = jnp.float32
bf16 = jnp.bfloat16
VMEM = 60 * 1024 * 1024
LIMIT = 60.0

NN = (((1,), (0,)), ((), ()))
NT = (((1,), (1,)), ((), ()))
TN = (((0,), (0,)), ((), ()))


def dot(left, right, dims=NN):
    return lax.dot_general(left, right, dims, preferred_element_type=f32)


def cost(flops, moved, trans=0):
    return pl.CostEstimate(
        flops=int(flops / SHRINK),
        bytes_accessed=int(moved / SHRINK),
        transcendentals=int(trans / SHRINK),
    )


def params(**more):
    return pltpu.CompilerParams(vmem_limit_bytes=VMEM, **more)


def shape(dims, dtype=f32):
    return jax.ShapeDtypeStruct(dims, dtype)


def tie(value, *others):
    return lax.optimization_barrier((value,) + others)[0] if others else value


class Net:
    def __init__(self, n_dp, n_own):
        self.n_dp, self.n_own = n_dp, n_own
        self.dp_bits = [1 << i for i in range(n_dp.bit_length() - 1)]
        self.own_bits = [1 << i for i in range(n_own.bit_length() - 1)]
        core = [("dp", self.dp_bits[0])]
        plane = [("dp", self.dp_bits[1]), ("own", self.own_bits[0])]
        line = [("dp", self.dp_bits[2]), ("dp", self.dp_bits[3])]
        self.stages = [core, plane, line]
        self.rest = [[("dp", b)] for b in self.dp_bits[4:]] + [
            [("own", b)] for b in self.own_bits[1:]
        ]

    def place(self, bits):
        at = {"dp": lax.axis_index("dp"), "own": lax.axis_index("own")}
        total = 0
        for i, (axis, bit) in enumerate(bits):
            total = total + jnp.where((at[axis] & bit) != 0, 1 << i, 0)
        return total.astype(jnp.int32)

    def swap(self, value, bits, which):
        dp_mask = own_mask = 0
        for i, (axis, bit) in enumerate(bits):
            if which >> i & 1:
                if axis == "dp":
                    dp_mask |= bit
                else:
                    own_mask |= bit
        pairs = []
        for d in range(self.n_dp):
            for o in range(self.n_own):
                source = d * self.n_own + o
                pairs.append((source, (d ^ dp_mask) * self.n_own + (o ^ own_mask)))
        return lax.ppermute(value, ("dp", "own"), pairs)

    def scatter_sum(self, parts, bits, link, *others):
        me = self.place(bits)
        got = []
        for g in range(1 << len(bits)):
            piece = lax.dynamic_index_in_dim(parts, me ^ g, 0, keepdims=False)
            if g > 0:
                piece = tie(self.swap(piece.astype(link), bits, g), *others).astype(parts.dtype)
            got.append(piece)
        while len(got) > 1:
            got = [got[i] + got[i + 1] for i in range(0, len(got), 2)]
        return got[0]

    def gather(self, value, bits, *others):
        got = [self.swap(value, bits, g) for g in range(1, 1 << len(bits))]
        return jnp.stack([value] + tie(got, *others))

    def add_up(self, value, bits):
        got = [value] + [self.swap(value, bits, g) for g in range(1, 1 << len(bits))]
        while len(got) > 1:
            got = [got[i] + got[i + 1] for i in range(0, len(got), 2)]
        return got[0]

    def digits(self):
        found = []
        for bits in (self.stages + self.rest)[::-1]:
            found = found + bits
        return found

    def own_list(self):
        return [("own", b) for b in self.own_bits]


def plan_kernel(cuts_soon, steps_last, slots, owner, seat, table):
    blocks = owner.shape[0]
    for i in range(4):
        table[2, i] = seat[i]
    count = jnp.int32(0)
    mine = []
    for b in range(blocks):
        here = (owner[b] == seat[4]).astype(jnp.int32)
        table[0, b] = count * here
        table[1, b] = here
        mine.append((here, count))
        count = count + here

    def fill(row, cuts, entries):
        left = jnp.int32(0)
        for here, *_ in entries:
            left = left + here
        steps = cuts[-1]
        for i in range(steps):
            for k in range(3):
                table[row + k, i] = 0
        ends = []
        for c in range(len(cuts) - 1):
            room, calls = cuts[c + 1] - cuts[c], len(cuts) - 1 - c
            part = jnp.minimum(room, (left + calls - 1) // calls)
            part = jnp.maximum(part, left - (steps - cuts[c + 1]))
            ends.append(cuts[c] + part)
            left = left - part
        at = jnp.int32(0)
        for c in range(len(ends) - 1):
            at = jnp.where(at == ends[c], cuts[c + 1], at)
        for here, slot, kind, block in entries:
            @pl.when(here > 0)
            def _(at=at, slot=slot, kind=kind, block=block):
                table[row, at] = slot
                table[row + 1, at] = kind
                table[row + 2, at] = block

            at = at + here
            for c in range(len(ends) - 1):
                at = jnp.where(at == ends[c], cuts[c + 1], at)
        for i in range(1, steps):
            @pl.when(table[row + 1, i] == 0)
            def _(i=i):
                table[row, i] = table[row, i - 1]
                table[row + 2, i] = table[row + 2, i - 1]

    first_ada = LATE + EARLY
    soon = [(*mine[LATE + n], 1, n) for n in range(EARLY)]
    soon += [(*mine[first_ada + n], 2, n - 2) for n in range(2, blocks - first_ada)]
    for i in range(slots):
        soon.append(((i >= count).astype(jnp.int32), i, 3, 0))
    fill(3, cuts_soon, soon)
    last = [(*mine[first_ada + n], 2, n) for n in range(2)]
    last += [(*mine[n], 1, n) for n in range(LATE)]
    fill(6, [0, steps_last], last)


def make_plan(owner, seat, slots, cuts_soon, steps_last):
    smem = pl.BlockSpec(memory_space=pltpu.SMEM)
    return pl.pallas_call(
        functools.partial(plan_kernel, cuts_soon, steps_last, slots),
        in_specs=[smem, smem],
        out_specs=smem,
        out_shape=shape((9, max(32, slots)), jnp.int32),
        name="plan",
    )(owner, seat)


def pick_kernel(blocks, table, master, out, buffer, sems):
    rows = out.shape[1]
    at = pl.multiple_of(table[2, 0] * HALF, HALF) if rows < D else 0
    for i, b in enumerate(blocks):
        copy = pltpu.make_async_copy(
            master.at[table[0, b], pl.ds(at, rows)], buffer.at[i], sems.at[i]
        )

        @pl.when(table[1, b] > 0)
        def _(copy=copy):
            copy.start()

    for i, b in enumerate(blocks):
        copy = pltpu.make_async_copy(
            master.at[table[0, b], pl.ds(at, rows)], buffer.at[i], sems.at[i]
        )

        @pl.when(table[1, b] > 0)
        def _(copy=copy, i=i):
            copy.wait()
            out[i] = buffer[i].astype(bf16)

        @pl.when(table[1, b] == 0)
        def _(i=i):
            out[i] = jnp.zeros(out.shape[1:], bf16)


def pick_blocks(table, master, blocks, rows):
    dims = (len(blocks), rows, D)
    return pl.pallas_call(
        functools.partial(pick_kernel, blocks),
        in_specs=[pl.BlockSpec(memory_space=pltpu.SMEM), pl.BlockSpec(memory_space=pl.ANY)],
        out_shape=shape(dims, bf16),
        scratch_shapes=[pltpu.VMEM(dims, f32), pltpu.SemaphoreType.DMA((len(blocks),))],
        compiler_params=params(),
        cost_estimate=cost(0, 6 * dims[0] * rows * D),
        name="pick_blocks",
    )(table, master)


def join_halves(core, near, far, out):
    out[:, pl.ds(pl.multiple_of(core * HALF, HALF), HALF), :] = near[...]
    out[:, pl.ds(pl.multiple_of((1 - core) * HALF, HALF), HALF), :] = far[...]


def normed(value):
    centered = value - jnp.mean(value, axis=-1, keepdims=True)
    inverse = lax.rsqrt(jnp.mean(centered * centered, axis=-1, keepdims=True) + norm_eps)
    return centered * inverse, inverse


def norm_back(gradient, norm, inverse):
    return inverse * (
        gradient
        - jnp.mean(gradient, axis=-1, keepdims=True)
        - norm * jnp.mean(gradient * norm, axis=-1, keepdims=True)
    )


def attend_kernel(core, latents, mod, near, far, bias, qkv, mixed, total, first_in, weight):
    @pl.when(pl.program_id(0) == 0)
    def _():
        join_halves(core[2, 0], near, far, weight)

    norm, _ = normed(latents[0].astype(f32))
    first = (norm * (1.0 + mod[0, 1:2]) + mod[0, 0:1]).astype(bf16)
    first_in[0] = first.T
    for b in range(3):
        qkv[0, :, b * D : (b + 1) * D] = (dot(first, weight[b]) + bias[:, b * D : (b + 1) * D]).astype(bf16)
    total[0] = jnp.zeros_like(total[0])

    head_of = lax.broadcasted_iota(jnp.int32, (D, 2 * HD), 0) // HD
    marks = jnp.where(
        head_of == lax.broadcasted_iota(jnp.int32, (D, 2 * HD), 1), 1.0, 0.0
    ).astype(bf16)

    def longest(block):
        value = qkv[0, :, block * D : (block + 1) * D].astype(f32)
        return jnp.max(dot((value * value).astype(bf16), marks), axis=0, keepdims=True)

    bound = jnp.max(longest(0) * longest(1)) * (1.05 / HD)
    small = bound < LIMIT * LIMIT

    def heads(shifted):
        lane = lax.broadcasted_iota(jnp.int32, (1, 2 * HD), 1)
        values_t = qkv[0, :, 2 * D : 3 * D].T
        for p in range(H // 2):
            keys = qkv[0, :, D + 2 * HD * p : D + 2 * HD * (p + 1)]
            pair = qkv[0, :, 2 * HD * p : 2 * HD * (p + 1)]
            for h in range(2):
                j = 2 * p + h
                mask = jnp.where((lane < HD) == (h == 0), HD**-0.5, 0.0).astype(bf16)
                scores = dot(keys, pair * mask, NT)
                peak = 0.0
                if shifted:
                    peak = jnp.max(scores, axis=0, keepdims=True)
                    scores = scores - peak
                expo = jnp.exp(scores)
                sums = jnp.sum(expo, axis=0, keepdims=True)
                prob = (expo * (1.0 / sums)).astype(bf16)
                out = dot(values_t[HD * j : HD * (j + 1)], prob)
                mixed[0, HD * j : HD * (j + 1), :] = out.astype(bf16)
                total[0, j : j + 1, :] = peak + jnp.log(sums)

    @pl.when(small)
    def _():
        heads(False)

    @pl.when(jnp.logical_not(small))
    def _():
        heads(True)


def middle_kernel(
    seqs,
    core,
    latents,
    upstream,
    mixed,
    mod,
    near,
    near_come,
    far,
    far_come,
    bias,
    cond,
    block_out,
    residual_back,
    mixed_back,
    keep,
    send,
    grad_late,
    small,
    proj,
    up,
    down,
    total,
    sums,
    bias_sums,
    second_s,
    act_s,
    pre_s,
    sems,
):
    seq, step = pl.program_id(0), pl.program_id(1)

    @pl.when((seq == 0) & (step == 0))
    def _():
        for half, ref, come in ((core[2, 0], near, near_come), (1 - core[2, 0], far, far_come)):
            at = pl.multiple_of(half * HALF, HALF)
            proj[pl.ds(at, HALF), :] = ref[0] + come[0]
            for n in range(FB):
                up[pl.ds(at, HALF), n * D : (n + 1) * D] = ref[1 + n] + come[1 + n]
                down[pl.ds(n * D + at, HALF), :] = ref[1 + FB + n] + come[1 + FB + n]
        total[...] = jnp.zeros_like(total)
        grad_late[...] = jnp.zeros_like(grad_late)
        bias_sums[...] = jnp.zeros_like(bias_sums)

    gate_one, shift_two, scale_two, gate_two = (mod[0, i : i + 1] for i in (2, 3, 4, 5))
    bias_up = bias[:, 4 * D : 4 * D + FF]

    def column(value):
        return jnp.sum(value, axis=0, keepdims=True)

    attn_out = dot(mixed[0], proj[...], TN) + bias[:, 3 * D : 4 * D]
    residual = latents[0].astype(f32) + gate_one * attn_out
    norm, inverse = normed(residual)
    second = (norm * (1.0 + scale_two) + shift_two).astype(bf16)
    second_s[...] = second
    ct = upstream[0].astype(f32)
    ffn_back = (ct * gate_two).astype(bf16)
    pre = dot(second, up[...]) + bias_up
    square = pre * pre
    k0 = 0.7978845608028654
    tanh = jnp.tanh(pre * (k0 + (k0 * 0.044715) * square))
    half = 0.5 + 0.5 * tanh
    act_s[...] = (pre * half).astype(bf16)
    slope = half + pre * (0.5 - 0.5 * tanh * tanh) * (k0 + (3.0 * k0 * 0.044715) * square)
    ffn_out = dot(act_s[...], down[...]) + bias[:, 4 * D + FF : 5 * D + FF]
    pre_back = (dot(ffn_back, down[...], NT) * slope).astype(bf16)
    pre_s[...] = pre_back
    low_pre = column(pre_back.astype(f32))
    second_back = dot(pre_back, up[...], NT)
    block_out[0] = (residual + gate_two * ffn_out).astype(bf16)
    res_back = ct + norm_back(second_back * (1.0 + scale_two), norm, inverse)
    residual_back[0] = res_back
    attn_back = (res_back * gate_one).astype(bf16)
    mixed_back[0] = dot(attn_back, proj[...], NT).astype(bf16)
    both = jnp.concatenate(
        [
            column(res_back * attn_out),
            column(second_back),
            column(second_back * norm),
            column(ct * ffn_out),
        ],
        axis=0,
    )
    bias_sums[...] += jnp.concatenate(
        [column(attn_back.astype(f32))]
        + [low_pre[:, n * D : (n + 1) * D] for n in range(FB)]
        + [column(ffn_back.astype(f32))],
        axis=0,
    )

    for n in range(seqs):
        @pl.when(seq == n)
        def _(n=n):
            sums[n] = jnp.where(step == 0, both, sums[n] + both)

    grad_late[0] += dot(mixed[0], attn_back)
    grad_up = dot(second_s[...], pre_s[...], TN)
    grad_down_t = dot(ffn_back, act_s[...], TN)
    side = core[2, 0] * FB
    for n in range(FB):
        cols = slice(n * D, (n + 1) * D)
        total[side + n] += grad_up[:, cols]
        total[FB - side + n] += grad_down_t[:, cols].T

    @pl.when((seq == pl.num_programs(0) - 1) & (step == pl.num_programs(1) - 1))
    def _():
        copies = [
            pltpu.make_async_copy(total.at[pl.ds(i * FB, FB)], out, sems.at[i])
            for i, out in enumerate((keep, send))
        ]
        for copy in copies:
            copy.start()
        rows = [jnp.concatenate([sums[n], cond[n : n + 1]], axis=0) for n in range(seqs)]
        rows.append(bias_sums[...])
        filled = seqs * 5 + FB + 2
        if small.shape[0] > filled:
            rows.append(jnp.zeros((small.shape[0] - filled, D), f32))
        small[...] = jnp.concatenate(rows, axis=0).astype(bf16)
        for copy in copies:
            copy.wait()


def attend_back_kernel(begin, first_pair, query, keys, values, back, total, first, *rest):
    grads_in, biases_in = rest[:2]
    back_query, back_keys, back_values, grads, biases = rest[-5:]
    pair = first_pair + pl.program_id(0)
    lane = lax.broadcasted_iota(jnp.int32, (1, 2 * HD), 1)
    keys_t = keys[0].T
    key_sum = value_sum = 0.0
    query_parts = []
    for h in range(2):
        one = jnp.where((lane < HD) == (h == 0), 1.0, 0.0).astype(bf16)
        q = query[0] * (one * HD**-0.5)
        g = back[0] * one
        prob = jnp.exp(dot(keys[0], q, NT) - total[0, pl.ds(2 * pair + h, 1)])
        prob_back = dot(values[0], g, NT)
        row_delta = jnp.sum(prob * prob_back, axis=0, keepdims=True)
        score_back = (prob * (prob_back - row_delta)).astype(bf16)
        value_sum = value_sum + dot(prob.astype(bf16), g)
        key_sum = key_sum + dot(score_back, q)
        query_parts.append(dot(keys_t[HD * h : HD * (h + 1)], score_back))
    low = (
        (jnp.concatenate(query_parts, axis=0) * HD**-0.5).T.astype(bf16),
        key_sum.astype(bf16),
        value_sum.astype(bf16),
    )
    for out, value in zip((back_query, back_keys, back_values), low):
        out[0] = value
    joined = jnp.concatenate(low, axis=1)
    new = dot(first[0], joined)
    sums = jnp.sum(joined.astype(f32), axis=0, keepdims=True)
    width = 2 * HD
    for i in range(3):
        cols = slice(i * width, (i + 1) * width)
        grads[i] = new[:, cols] if begin else grads_in[i] + new[:, cols]
        biases[i : i + 1] = sums[:, cols] if begin else biases_in[i : i + 1] + sums[:, cols]


def first_back_kernel(
    n, final, table, latents, residual_back, mod, back_query, back_keys, back_values, near, far, biases, *rest
):
    latents_grad, small, weight, sums = rest[-4:]

    @pl.when(pl.program_id(0) == 0)
    def _():
        join_halves(table[2, 0], near, far, weight)
        sums[...] = jnp.zeros_like(sums)

    norm, inverse = normed(latents[0].astype(f32))
    first_back = (
        dot(back_query[0], weight[0], NT)
        + dot(back_keys[0], weight[1], NT)
        + dot(back_values[0], weight[2], NT)
    )
    sums[0:1] += jnp.sum(first_back, axis=0, keepdims=True)
    sums[1:2] += jnp.sum(first_back * norm, axis=0, keepdims=True)
    latents_grad[0] = residual_back[0] + norm_back(
        first_back * (1.0 + mod[0, 1:2]), norm, inverse
    )

    @pl.when(pl.program_id(0) == pl.num_programs(0) - 1)
    def _():
        rows = [rest[0][: 2 * n]] if n else []
        rows.append(sums[0:2])
        if final:
            rows += [part.astype(f32) for part in split_two(biases[0:3])]
        filled = 2 * n + 2 + (6 if final else 0)
        rows.append(jnp.zeros((small.shape[0] - filled, D), f32))
        small[...] = jnp.concatenate(rows, axis=0).astype(small.dtype)


def split_two(value):
    high = value.astype(bf16)
    return high, (value - high.astype(f32)).astype(bf16)


def small_spec(half, rows):
    dims = (*half.shape[:-2], half.shape[-2] - rows, D)
    return whole(*dims)


def joined(near, far):
    return jnp.concatenate([near[...].reshape(-1, D), far[...].reshape(-1, D)], axis=0)


def chosen_rows(rows, count, seqs, me, group, per, kind):
    latent = lax.broadcasted_iota(jnp.int32, (count, rows.shape[0]), 0)
    wanted = (latent // seqs ^ me) * group + latent % seqs * per + kind
    hit = wanted == lax.broadcasted_iota(jnp.int32, (count, rows.shape[0]), 1)
    return dot(jnp.where(hit, 1.0, 0.0).astype(bf16), rows)


def finish(seqs, group, soon_group, last_group, me, soon, last, inputs, outs):
    ada, bias, one, two = inputs
    grad_out, one_out, two_out, bias_out, cond_out = outs
    devices = soon.shape[0] // soon_group

    def totals(rows, each_group, kinds):
        count = len(kinds) * devices
        at = lax.broadcasted_iota(jnp.int32, (count, rows.shape[0]), 0)
        first = kinds[0]
        assert list(kinds) == list(range(first, first + len(kinds)))
        wanted = (at % devices ^ me) * each_group + at // devices + first
        hit = wanted == lax.broadcasted_iota(jnp.int32, (count, rows.shape[0]), 1)
        found = dot(jnp.where(hit, 1.0, 0.0).astype(bf16), rows)
        return [
            jnp.sum(found[k * devices : (k + 1) * devices], axis=0, keepdims=True)
            for k in range(len(kinds))
        ]

    of_soon = totals(soon, soon_group, range(0, seqs * 5 + FB + 2))
    of_last = totals(last, last_group, range(0, seqs * 2 + 6))
    qkv = [of_last[seqs * 2 + i] + of_last[seqs * 2 + 3 + i] for i in range(3)]
    mods = [sum(of_last[n * 2 + i] for n in range(seqs)) for i in range(2)]
    mods += [sum(of_soon[n * 5 + i] for n in range(seqs)) for i in range(4)]
    grad = jnp.concatenate(qkv + of_soon[seqs * 5 : seqs * 5 + FB + 2] + mods, axis=1)
    grad = grad.reshape(-1)
    grad_out[...] = grad
    one_new = 0.9 * one[...] + 0.1 * grad
    two_new = 0.95 * two[...] + 0.05 * grad * grad
    one_out[...] = one_new
    two_out[...] = two_new
    corrected = (
        one_new / (1.0 - 0.9**STEP) / (jnp.sqrt(two_new / (1.0 - 0.95**STEP)) + 1e-08)
    )
    bias_out[...] = bias[...] - adam_rate * (corrected + adam_decay * bias[...])
    for g, device in enumerate(group):
        total = 0.0
        for b in range(ada.shape[0]):
            rows, each_group, per, kind = (
                (last, last_group, 2, b) if b < 2 else (soon, soon_group, 5, b - 2)
            )
            base = device * each_group
            mine = jnp.concatenate(
                [rows[base + n * per + kind : base + n * per + kind + 1] for n in range(seqs)]
                + [jnp.zeros((8 - seqs, D), bf16)],
                axis=0,
            )
            total = total + dot(mine, ada[b], NT)
        cond_out[g] = total[:seqs]


def slots_kernel(
    row, begin, room, pieces, stages, line, small, extra, table, *refs
):
    cond_halves, mod_halves, (near, far) = refs[:2], refs[2:4], refs[4:6]
    state, refs = refs[6:11], refs[11:]
    more_in, refs = refs[: 4 if extra else 0], refs[4 if extra else 0 :]
    more_out, refs = (refs[-10:-5], refs[:-10] + refs[-5:]) if extra else ((), refs)
    outs = refs[-9:-5]
    held, gradient_in, made, in_sems, out_sems = refs[-5:]
    cond_group, mod_group, per, seqs = small
    rows = D // pieces
    count = jnp.int32(0)
    for i in range(room):
        count = count + (table[row + 1, begin + i] > 0).astype(jnp.int32)

    def piece(half, i, p, buf):
        shard = table[row + 2, begin + i] * pieces + p
        at = ((shard // line & 3) ^ table[2, 1], (shard & 3) ^ table[2, 2])[:stages]
        return pltpu.make_async_copy(
            half.at[(*at, pl.ds(half.shape[-2] - rows, rows))],
            gradient_in.at[buf, pl.ds(p * rows, rows)],
            in_sems.at[buf, 5 + p],
        )

    def arriving(i, k, buf):
        return pltpu.make_async_copy(
            state[k].at[table[row, begin + i]], held.at[buf, k], in_sems.at[buf, k]
        )

    def leaving(i, k, buf):
        return pltpu.make_async_copy(
            made.at[buf, k], outs[k].at[table[row, begin + i]], out_sems.at[buf, k]
        )

    def fetch(i, buf):
        side = (table[row + 2, begin + i] * pieces // (4 * line)) ^ table[2, 0]
        for number, half in enumerate((near, far)):
            @pl.when((table[row + 1, begin + i] == 1) & (side == number))
            def _(half=half):
                for p in range(pieces):
                    piece(half, i, p, buf).start()

        for k in (2, 3, 4, 0, 1):
            arriving(i, k, buf).start()

    @pl.when(count > 0)
    def _():
        fetch(0, 0)

    if extra:
        finish(
            seqs,
            extra,
            cond_group,
            mod_group,
            table[2, 3],
            joined(*cond_halves),
            joined(*mod_halves),
            more_in,
            more_out,
        )

    def one(i, carry):
        buf = i & 1
        kind = table[row + 1, begin + i]

        @pl.when(i + 1 < count)
        def _():
            fetch(i + 1, 1 - buf)

        @pl.when(i >= 2)
        def _():
            for k in range(4):
                leaving(i - 2, k, buf).wait()

        @pl.when(kind == 1)
        def _():
            for p in range(pieces):
                piece(near, i, p, buf).wait()
            made[buf, 0] = gradient_in[buf].astype(f32)

        @pl.when(kind == 2)
        def _():
            conds, mods = joined(*cond_halves), joined(*mod_halves)
            total = conds.shape[0] // cond_group * seqs
            me, block = table[2, 3], table[row + 2, begin + i]
            cond = chosen_rows(conds, total, seqs, me, cond_group, 5, 4).astype(bf16)
            mod = chosen_rows(mods, total, seqs, me, mod_group, per, block).astype(bf16)
            made[buf, 0] = dot(cond, mod, TN)

        @pl.when(kind == 3)
        def _():
            made[buf, 0] = jnp.zeros((D, D), f32)

        leaving(i, 0, buf).start()
        low = made[buf, 0].astype(bf16)
        arriving(i, 2, buf).wait()
        turned = low.T
        two = dot(jnp.concatenate([held[buf, 2].astype(bf16), turned], axis=0), low)
        arriving(i, 3, buf).wait()
        direction = dot(two[:D].astype(bf16), held[buf, 3].astype(bf16))
        arriving(i, 4, buf).wait()
        weight = held[buf, 4]
        scale = jnp.sqrt(jnp.mean(weight * weight) + norm_eps) * lax.rsqrt(
            jnp.mean(direction * direction) + norm_eps
        )
        made[buf, 3] = weight - shampoo_rate * (scale * direction + shampoo_decay * weight)
        leaving(i, 3, buf).start()
        arriving(i, 0, buf).wait()
        made[buf, 1] = 0.5 * held[buf, 0] + 0.5 * dot(low, turned)
        leaving(i, 1, buf).start()
        arriving(i, 1, buf).wait()
        made[buf, 2] = 0.5 * held[buf, 1] + 0.5 * two[D:]
        leaving(i, 2, buf).start()
        return carry

    lax.fori_loop(0, count, one, 0)
    for back in (2, 1):
        @pl.when(count >= back)
        def _(back=back):
            for k in range(4):
                leaving(count - back, k, (count - back) & 1).wait()


def slots_call(row, begin, steps, table, small, gathered, rows, state, outs, ties, name, finishing=None):
    slots = state[0].shape[0]
    pieces = D // rows
    stages = gathered[0].ndim - 2
    line = gathered[0].shape[1] if stages > 1 else 1
    conds, mods, cond_rows, *small = small
    given = [] if outs is None else list(outs)
    anyplace = pl.BlockSpec(memory_space=pl.ANY)
    group, more_in = finishing or (None, ())
    more = given + list(ties)
    more_out = [shape(v.shape) for v in more_in[1:2] * 4]
    if finishing:
        more_out.append(shape((len(group), small[-1], D)))
    return pl.pallas_call(
        functools.partial(slots_kernel, row, begin, steps, pieces, stages, line, small, group),
        grid=(1,),
        in_specs=[pl.BlockSpec(memory_space=pltpu.SMEM)]
        + [small_spec(half, cond_rows) for half in conds]
        + [small_spec(half, rows) for half in mods]
        + [anyplace] * 7
        + [whole(*v.shape) for v in more_in]
        + [anyplace] * len(more),
        out_specs=[anyplace] * 4 + [whole(*v.shape) for v in more_out],
        out_shape=[shape((slots, D, D))] * 4 + more_out,
        scratch_shapes=[
            pltpu.VMEM((2, 5, D, D), f32),
            pltpu.VMEM((2, D, D), bf16),
            pltpu.VMEM((2, 4, D, D), f32),
            pltpu.SemaphoreType.DMA((2, 5 + pieces)),
            pltpu.SemaphoreType.DMA((2, 4)),
        ],
        input_output_aliases={12 + len(more_in) + i: i for i in range(len(given))},
        compiler_params=params(),
        cost_estimate=cost(steps * 7 * 2 * D**3, steps * 10 * D * D * 4),
        name=name,
    )(table, *conds, *mods, *gathered, *state, *more_in, *more)


def whole(*dims):
    return pl.BlockSpec(dims, lambda *_: (0,) * len(dims))


def each(*dims):
    return pl.BlockSpec((1,) + dims, lambda i, *_: (i,) + (0,) * len(dims))


def middle(rows, table, latents, cotangent, mixed, modulation, rest, bias_row, cond, small_rows):
    seqs, length, _ = latents.shape
    tok = pl.BlockSpec((1, rows, D), lambda i, j: (i, j, 0))
    anyplace = pl.BlockSpec(memory_space=pl.ANY)
    return pl.pallas_call(
        functools.partial(middle_kernel, seqs),
        grid=(seqs, length // rows),
        in_specs=[
            pl.BlockSpec(memory_space=pltpu.SMEM),
            tok,
            tok,
            pl.BlockSpec((1, D, rows), lambda i, j: (i, 0, j)),
            each(6, D),
            *[whole(1 + EARLY, HALF, D)] * 4,
            whole(*bias_row.shape),
            whole(*cond.shape),
        ],
        out_specs=[
            tok,
            tok,
            tok,
            anyplace,
            anyplace,
            pl.BlockSpec((1, D, D), lambda *_: (LATE - 1, 0, 0)),
            whole(small_rows, D),
        ],
        out_shape=[
            shape((seqs, length, D), bf16),
            shape((seqs, length, D)),
            shape((seqs, length, D), bf16),
            shape((FB, D, D)),
            shape((FB, D, D)),
            shape((LATE, D, D)),
            shape((small_rows, D), bf16),
        ],
        scratch_shapes=[
            pltpu.VMEM((D, D), bf16),
            pltpu.VMEM((D, FF), bf16),
            pltpu.VMEM((FF, D), bf16),
            pltpu.VMEM((2 * FB, D, D), f32),
            pltpu.VMEM((seqs, 4, D), f32),
            pltpu.VMEM((FB + 2, D), f32),
            pltpu.VMEM((rows, D), bf16),
            pltpu.VMEM((rows, FF), bf16),
            pltpu.VMEM((rows, FF), bf16),
            pltpu.SemaphoreType.DMA((2,)),
        ],
        compiler_params=params(),
        cost_estimate=cost(22e9, 25e6, 3e6),
        name="middle",
    )(table, latents, cotangent, mixed, modulation, *rest, bias_row, cond)


def per_device(
    net,
    latents,
    condition,
    cotangent,
    owner,
    master,
    stat_left,
    stat_right,
    root_left,
    root_right,
    bias,
    moment_one,
    moment_two,
):
    slots = master.shape[0]
    seqs, length, _ = latents.shape
    blocks = owner.shape[0]
    first_ada = LATE + EARLY
    ada = blocks - first_ada
    own_all = net.own_list()
    steps_last = min(slots, 2 + LATE)
    anyplace = pl.BlockSpec(memory_space=pl.ANY)
    smem = pl.BlockSpec(memory_space=pltpu.SMEM)
    tok = each(length, D)
    soon_rows = -(-(seqs * 5 + FB + 2) // 16) * 16
    last_rows = -(-(seqs * 2 + 2 * 3) // 16) * 16

    seat = jnp.stack(
        [net.place(bits) for bits in net.stages]
        + [net.place(net.digits()), lax.axis_index("own").astype(jnp.int32)]
    )
    cuts = [0, max(1, slots // 5), max(2, slots // 2), slots]
    table = make_plan(owner, seat, slots, cuts, steps_last)

    near_qkv = pick_blocks(table, master, list(range(3)), HALF)
    own_ada = pick_blocks(table, master, list(range(first_ada, blocks)), D)
    near_rest = pick_blocks(table, master, list(range(3, first_ada)), HALF)
    for bit in own_all:
        near_qkv = near_qkv + tie(net.swap(near_qkv, [bit], 1), near_rest)
    far_qkv = net.swap(near_qkv, net.stages[0], 1)

    bias_row = bias.reshape(1, -1)
    cond_float = condition.astype(f32)
    silu_cond, silu_pull = jax.vjp(jax.nn.silu, cond_float)
    cond_low = silu_cond.astype(bf16)
    cond_group = net.gather(cond_low, own_all)
    mod_parts = jnp.einsum("gld,bde->glbe", cond_group, own_ada, preferred_element_type=f32)
    modulation = mod_parts[0]
    for g in range(1, net.n_own):
        modulation = modulation + net.swap(mod_parts[g], own_all, g)
    modulation = modulation + bias[5 * D + FF :].reshape(ada, D)

    near_rest = tie(near_rest, near_qkv, modulation)
    for bit in own_all[:-1]:
        near_rest = near_rest + net.swap(near_rest, [bit], 1)
    far_rest = net.swap(near_rest, net.stages[0], 1)
    near_come = net.swap(near_rest, own_all[-1:], 1)

    qkv, mixed, totals, first_in = pl.pallas_call(
        attend_kernel,
        grid=(seqs,),
        in_specs=[
            smem,
            tok,
            each(6, D),
            whole(3, HALF, D),
            whole(3, HALF, D),
            whole(*bias_row.shape),
        ],
        out_specs=[each(length, 3 * D), each(D, length), each(8, length), each(D, length)],
        out_shape=[
            shape((seqs, length, 3 * D), bf16),
            shape((seqs, D, length), bf16),
            shape((seqs, 8, length)),
            shape((seqs, D, length), bf16),
        ],
        scratch_shapes=[pltpu.VMEM((3, D, D), bf16)],
        compiler_params=params(),
        cost_estimate=cost(16e9, 12e6, 12e6),
        name="attend",
    )(table, latents, modulation, near_qkv, far_qkv, bias_row)

    near_come = tie(near_come, qkv)
    rest = (near_rest, near_come, far_rest, net.swap(near_come, net.stages[0], 1))

    (
        block_out,
        residual_back,
        mixed_back,
        early_keep,
        early_send,
        grad_late,
        small_soon,
    ) = middle(
        length,
        table,
        latents,
        cotangent,
        mixed,
        modulation,
        rest,
        bias_row,
        cond_low.astype(f32),
        soon_rows,
    )

    def core_stage(grads, *others):
        return net.scatter_sum(grads.reshape(2, -1, D), net.stages[0], f32, *others)

    def plane_stage(value, *others):
        return net.scatter_sum(value.reshape(4, -1, D), net.stages[1], bf16, *others)

    def line_stage(value, *others):
        value = net.scatter_sum(value.reshape(4, -1, D), net.stages[2], bf16, *others)
        for bits in net.rest:
            value = net.add_up(value, bits)
        return value.astype(bf16)

    def with_small(value, small):
        for bits in net.rest[::-1]:
            small = net.gather(small, bits)
        return jnp.concatenate([small.reshape(-1, D), value], axis=0)

    def line_exchange(value, small, others):
        sent = with_small(value.astype(bf16), small)
        rows = sent.shape[0] - value.shape[0]
        got = net.gather(sent, net.stages[2], *others)
        value = (got[0, rows:].astype(f32) + got[1, rows:]) + (got[2, rows:].astype(f32) + got[3, rows:])
        for bits in net.rest:
            value = net.add_up(value, bits)
        return jnp.concatenate([got[:, :rows].reshape(-1, D), value.astype(bf16)], axis=0)

    def back_pairs(n, first_pair, count, carried, ties):
        def head(offset):
            return pl.BlockSpec((1, length, 2 * HD), lambda i: (n, 0, offset + first_pair + i))

        def latent(*dims):
            return pl.BlockSpec((1,) + dims, lambda i: (n, 0, 0))

        begin = n == 0
        grad_spec = pl.BlockSpec((3, D, 2 * HD), lambda i: (0, 0, first_pair + i))
        bias_spec = pl.BlockSpec((8, 2 * HD), lambda i: (0, first_pair + i))
        return pl.pallas_call(
            functools.partial(attend_back_kernel, begin, first_pair),
            grid=(count,),
            in_specs=[head(0), head(3), head(6), head(0), latent(8, length), latent(D, length)]
            + ([anyplace] * 2 if begin else [grad_spec, bias_spec])[: len(carried)]
            + [anyplace] * (len(carried[2:]) + len(ties)),
            out_specs=[head(0)] * 3 + [grad_spec, bias_spec],
            out_shape=[shape((seqs, length, D), bf16)] * 3 + [shape((LATE, D, D)), shape((8, D))],
            input_output_aliases={6 + i: at for i, at in enumerate((3, 4, 0, 1, 2)[: len(carried)])},
            compiler_params=params(),
            cost_estimate=cost(count * 7e9, count * 3e6, count * 2e6),
            name="attend_back",
        )(qkv, qkv, qkv, mixed_back, totals, first_in, *carried, *ties)

    def first_back(n, backs, carried, ties):
        rows = length // 2
        final = n == seqs - 1
        part = pl.BlockSpec((1, rows, D), lambda i: (n, i, 0))
        grad, small = carried if carried else (None, None)
        more = ([small, grad] if n else []) + ties
        specs = ([whole(*small.shape), anyplace] if n else []) + [anyplace] * len(ties)
        return pl.pallas_call(
            functools.partial(first_back_kernel, n, final),
            grid=(2,),
            in_specs=[smem, part, part, pl.BlockSpec((1, 6, D), lambda i: (n, 0, 0))]
            + [part] * 3
            + [whole(3, HALF, D)] * 2
            + [whole(8, D)]
            + specs,
            out_specs=[part, whole(last_rows, D)],
            out_shape=[
                shape((seqs, length, D)),
                shape((last_rows, D), bf16 if final else f32),
            ],
            input_output_aliases={11: 0} if n else {},
            scratch_shapes=[pltpu.VMEM((3, D, D), bf16), pltpu.VMEM((8, D), f32)],
            compiler_params=params(),
            cost_estimate=cost(3.5e9, 9e6),
            name="first_back",
        )(
            table,
            latents,
            residual_back,
            modulation,
            *backs[:3],
            near_qkv,
            far_qkv,
            backs[4],
            *more,
        )

    def swapped(backs):
        return [backs[3], backs[4], *backs[:3]]

    early = early_keep
    stages = [
        lambda value: value + net.swap(early_send, net.stages[0], 1),
        plane_stage,
        lambda value: with_small(line_stage(value), small_soon),
        lambda value: net.gather(value, net.stages[2]),
    ]
    def after_stage(*others):
        nonlocal early
        if stages:
            early = stages.pop(0)(early)
            return [early, *others]
        return list(others)

    backs = [None] * 3 + [grad_late]
    firsts = []
    for n in range(seqs):
        for first_pair, count in ((0, 1), (1, 2)):
            if n + first_pair == 0:
                carried, ties = [grad_late], []
            else:
                carried = swapped(backs)
                ties = after_stage(*(firsts[:1] if first_pair == 0 else []))
            backs = back_pairs(n, first_pair, count, carried, ties)
        if n < seqs - 1:
            firsts = first_back(n, backs, firsts, after_stage())
    for stage in stages:
        early = stage(early)
    pieces = [net.swap(early, net.stages[1], g) for g in range(1, 4)]
    pieces, grad_late = tie((pieces, backs[3]), backs[0])
    early = jnp.stack([early] + pieces)
    latents_grad, small_last = first_back(seqs - 1, backs, firsts, [])
    late = core_stage(grad_late, latents_grad)
    early = (early, net.swap(early, net.stages[0], 1))
    early_rows = EARLY * D // 32
    late_rows = LATE * D // 8
    state = (stat_left, stat_right, root_left, root_right, master)
    def soon_slots(i, outs, ties):
        return slots_call(
            3,
            cuts[i],
            cuts[i + 1] - cuts[i],
            table,
            (early, early, early_rows, soon_rows, soon_rows, 5, seqs),
            early,
            early_rows,
            state,
            outs,
            ties,
            "soon_slots",
        )

    outs = soon_slots(0, None, [late])
    late = plane_stage(late, *outs)
    outs = soon_slots(1, outs, [late])
    late = line_exchange(late, small_last, outs)
    outs = soon_slots(2, outs, [late])
    late = net.gather(late, net.stages[1], *outs)
    late = (late, net.swap(late, net.stages[0], 1))
    group = []
    for g in range(net.n_own):
        group.append(
            sum(1 << k for k, (axis, bit) in enumerate(net.digits()) if axis == "own" and g & bit)
        )

    weight_grads, left_new, right_new, master_new, *bias_outs, cond_parts = slots_call(
        6,
        0,
        steps_last,
        table,
        (early, late, early_rows, soon_rows, last_rows, 2, seqs),
        late,
        late_rows,
        state,
        outs,
        [],
        "last_slots",
        (group, (own_ada, bias, moment_one, moment_two)),
    )
    bias_grad, moment_one_new, moment_two_new, bias_new = bias_outs

    back_cond = cond_parts[0]
    for g in range(1, net.n_own):
        back_cond = back_cond + net.swap(cond_parts[g], own_all, g)
    condition_grad = silu_pull(back_cond)[0]
    return (
        block_out,
        latents_grad,
        condition_grad,
        weight_grads,
        left_new,
        right_new,
        master_new,
        bias_grad,
        moment_one_new,
        moment_two_new,
        bias_new,
    )


def solution(mesh):
    net = Net(mesh.shape["dp"], mesh.shape["own"])
    token = P(("dp", "own"), None, None)
    slot = P("own", None, None)
    return jax.shard_map(
        functools.partial(per_device, net),
        mesh=mesh,
        in_specs=(token, P(("dp", "own"), None), token, P()) + (slot,) * 5 + (P(),) * 3,
        out_specs=(token, token, P(("dp", "own"), None)) + (slot,) * 4 + (P(),) * 4,
        check_vma=False,
    )
```

```python
import functools

import jax
import jax.numpy as jnp
from jax import lax
from jax.experimental import pallas as pl
from jax.experimental.pallas import tpu as pltpu
from jax.sharding import PartitionSpec as P

D = 384
H = 6
HD = 64
FF = 1536
FB = FF // D
STEP = 10
HALF = D // 2
LATE = 4
EARLY = 2 * FB

SHRINK = 2.5

norm_eps = 1e-06
shampoo_rate = 1.0
shampoo_decay = 0.01
adam_rate = 0.2
adam_decay = 0.01
f32 = jnp.float32
bf16 = jnp.bfloat16
VMEM = 60 * 1024 * 1024
LIMIT = 60.0

NN = (((1,), (0,)), ((), ()))
NT = (((1,), (1,)), ((), ()))
TN = (((0,), (0,)), ((), ()))


def dot(left, right, dims=NN):
    return lax.dot_general(left, right, dims, preferred_element_type=f32)


def cost(flops, moved, trans=0):
    return pl.CostEstimate(
        flops=int(flops / SHRINK),
        bytes_accessed=int(moved / SHRINK),
        transcendentals=int(trans / SHRINK),
    )


def params(**more):
    return pltpu.CompilerParams(vmem_limit_bytes=VMEM, **more)


def shape(dims, dtype=f32):
    return jax.ShapeDtypeStruct(dims, dtype)


def tie(value, *others):
    return lax.optimization_barrier((value,) + others)[0] if others else value


class Net:
    def __init__(self, n_dp, n_own):
        self.n_dp, self.n_own = n_dp, n_own
        self.dp_bits = [1 << i for i in range(n_dp.bit_length() - 1)]
        self.own_bits = [1 << i for i in range(n_own.bit_length() - 1)]
        core = [("dp", self.dp_bits[0])]
        plane = [("dp", self.dp_bits[1]), ("own", self.own_bits[0])]
        line = [("dp", self.dp_bits[2]), ("dp", self.dp_bits[3])]
        self.stages = [core, plane, line]
        self.rest = [[("dp", b)] for b in self.dp_bits[4:]] + [
            [("own", b)] for b in self.own_bits[1:]
        ]

    def place(self, bits):
        at = {"dp": lax.axis_index("dp"), "own": lax.axis_index("own")}
        total = 0
        for i, (axis, bit) in enumerate(bits):
            total = total + jnp.where((at[axis] & bit) != 0, 1 << i, 0)
        return total.astype(jnp.int32)

    def swap(self, value, bits, which):
        dp_mask = own_mask = 0
        for i, (axis, bit) in enumerate(bits):
            if which >> i & 1:
                if axis == "dp":
                    dp_mask |= bit
                else:
                    own_mask |= bit
        pairs = []
        for d in range(self.n_dp):
            for o in range(self.n_own):
                source = d * self.n_own + o
                pairs.append((source, (d ^ dp_mask) * self.n_own + (o ^ own_mask)))
        return lax.ppermute(value, ("dp", "own"), pairs)

    def scatter_sum(self, parts, bits, link, *others):
        me = self.place(bits)
        got = []
        for g in range(1 << len(bits)):
            piece = lax.dynamic_index_in_dim(parts, me ^ g, 0, keepdims=False)
            if g > 0:
                piece = tie(self.swap(piece.astype(link), bits, g), *others).astype(parts.dtype)
            got.append(piece)
        while len(got) > 1:
            got = [got[i] + got[i + 1] for i in range(0, len(got), 2)]
        return got[0]

    def gather(self, value, bits, *others):
        got = [self.swap(value, bits, g) for g in range(1, 1 << len(bits))]
        return jnp.stack([value] + tie(got, *others))

    def add_up(self, value, bits):
        got = [value] + [self.swap(value, bits, g) for g in range(1, 1 << len(bits))]
        while len(got) > 1:
            got = [got[i] + got[i + 1] for i in range(0, len(got), 2)]
        return got[0]

    def digits(self):
        found = []
        for bits in (self.stages + self.rest)[::-1]:
            found = found + bits
        return found

    def own_list(self):
        return [("own", b) for b in self.own_bits]


def plan_kernel(cuts_soon, steps_last, slots, owner, seat, table):
    blocks = owner.shape[0]
    for i in range(4):
        table[2, i] = seat[i]
    count = jnp.int32(0)
    mine = []
    for b in range(blocks):
        here = (owner[b] == seat[4]).astype(jnp.int32)
        table[0, b] = count * here
        table[1, b] = here
        mine.append((here, count))
        count = count + here

    def fill(row, cuts, entries):
        left = jnp.int32(0)
        for here, *_ in entries:
            left = left + here
        steps = cuts[-1]
        for i in range(steps):
            for k in range(3):
                table[row + k, i] = 0
        ends = []
        for c in range(len(cuts) - 1):
            room, calls = cuts[c + 1] - cuts[c], len(cuts) - 1 - c
            part = jnp.minimum(room, (left + calls - 1) // calls)
            part = jnp.maximum(part, left - (steps - cuts[c + 1]))
            ends.append(cuts[c] + part)
            left = left - part
        at = jnp.int32(0)
        for c in range(len(ends) - 1):
            at = jnp.where(at == ends[c], cuts[c + 1], at)
        for here, slot, kind, block in entries:
            @pl.when(here > 0)
            def _(at=at, slot=slot, kind=kind, block=block):
                table[row, at] = slot
                table[row + 1, at] = kind
                table[row + 2, at] = block

            at = at + here
            for c in range(len(ends) - 1):
                at = jnp.where(at == ends[c], cuts[c + 1], at)
        for i in range(1, steps):
            @pl.when(table[row + 1, i] == 0)
            def _(i=i):
                table[row, i] = table[row, i - 1]
                table[row + 2, i] = table[row + 2, i - 1]

    first_ada = LATE + EARLY
    soon = [(*mine[LATE + n], 1, n) for n in range(EARLY)]
    soon += [(*mine[first_ada + n], 2, n - 2) for n in range(2, blocks - first_ada)]
    for i in range(slots):
        soon.append(((i >= count).astype(jnp.int32), i, 3, 0))
    fill(3, cuts_soon, soon)
    last = [(*mine[first_ada + n], 2, n) for n in range(2)]
    last += [(*mine[n], 1, n) for n in range(LATE)]
    fill(6, [0, steps_last], last)


def make_plan(owner, seat, slots, cuts_soon, steps_last):
    smem = pl.BlockSpec(memory_space=pltpu.SMEM)
    return pl.pallas_call(
        functools.partial(plan_kernel, cuts_soon, steps_last, slots),
        in_specs=[smem, smem],
        out_specs=smem,
        out_shape=shape((9, max(32, slots)), jnp.int32),
        name="plan",
    )(owner, seat)


def pick_kernel(blocks, table, master, out, buffer, sems):
    rows = out.shape[1]
    at = pl.multiple_of(table[2, 0] * HALF, HALF) if rows < D else 0
    for i, b in enumerate(blocks):
        copy = pltpu.make_async_copy(
            master.at[table[0, b], pl.ds(at, rows)], buffer.at[i], sems.at[i]
        )

        @pl.when(table[1, b] > 0)
        def _(copy=copy):
            copy.start()

    for i, b in enumerate(blocks):
        copy = pltpu.make_async_copy(
            master.at[table[0, b], pl.ds(at, rows)], buffer.at[i], sems.at[i]
        )

        @pl.when(table[1, b] > 0)
        def _(copy=copy, i=i):
            copy.wait()
            out[i] = buffer[i].astype(bf16)

        @pl.when(table[1, b] == 0)
        def _(i=i):
            out[i] = jnp.zeros(out.shape[1:], bf16)


def pick_blocks(table, master, blocks, rows):
    dims = (len(blocks), rows, D)
    return pl.pallas_call(
        functools.partial(pick_kernel, blocks),
        in_specs=[pl.BlockSpec(memory_space=pltpu.SMEM), pl.BlockSpec(memory_space=pl.ANY)],
        out_shape=shape(dims, bf16),
        scratch_shapes=[pltpu.VMEM(dims, f32), pltpu.SemaphoreType.DMA((len(blocks),))],
        compiler_params=params(),
        cost_estimate=cost(0, 6 * dims[0] * rows * D),
        name="pick_blocks",
    )(table, master)


def join_halves(core, near, far, out):
    out[:, pl.ds(pl.multiple_of(core * HALF, HALF), HALF), :] = near[...]
    out[:, pl.ds(pl.multiple_of((1 - core) * HALF, HALF), HALF), :] = far[...]


def normed(value):
    centered = value - jnp.mean(value, axis=-1, keepdims=True)
    inverse = lax.rsqrt(jnp.mean(centered * centered, axis=-1, keepdims=True) + norm_eps)
    return centered * inverse, inverse


def norm_back(gradient, norm, inverse):
    return inverse * (
        gradient
        - jnp.mean(gradient, axis=-1, keepdims=True)
        - norm * jnp.mean(gradient * norm, axis=-1, keepdims=True)
    )


def attend_kernel(core, latents, mod, near, far, bias, qkv, mixed, total, first_in, weight):
    @pl.when(pl.program_id(0) == 0)
    def _():
        join_halves(core[2, 0], near, far, weight)

    norm, _ = normed(latents[0].astype(f32))
    first = (norm * (1.0 + mod[0, 1:2]) + mod[0, 0:1]).astype(bf16)
    first_in[0] = first.T
    for b in range(3):
        qkv[0, :, b * D : (b + 1) * D] = (dot(first, weight[b]) + bias[:, b * D : (b + 1) * D]).astype(bf16)
    total[0] = jnp.zeros_like(total[0])

    head_of = lax.broadcasted_iota(jnp.int32, (D, 2 * HD), 0) // HD
    marks = jnp.where(
        head_of == lax.broadcasted_iota(jnp.int32, (D, 2 * HD), 1), 1.0, 0.0
    ).astype(bf16)

    def longest(block):
        value = qkv[0, :, block * D : (block + 1) * D].astype(f32)
        return jnp.max(dot((value * value).astype(bf16), marks), axis=0, keepdims=True)

    bound = jnp.max(longest(0) * longest(1)) * (1.05 / HD)
    small = bound < LIMIT * LIMIT

    def heads(shifted):
        lane = lax.broadcasted_iota(jnp.int32, (1, 2 * HD), 1)
        values_t = qkv[0, :, 2 * D : 3 * D].T
        for p in range(H // 2):
            keys = qkv[0, :, D + 2 * HD * p : D + 2 * HD * (p + 1)]
            pair = qkv[0, :, 2 * HD * p : 2 * HD * (p + 1)]
            for h in range(2):
                j = 2 * p + h
                mask = jnp.where((lane < HD) == (h == 0), HD**-0.5, 0.0).astype(bf16)
                scores = dot(keys, pair * mask, NT)
                peak = 0.0
                if shifted:
                    peak = jnp.max(scores, axis=0, keepdims=True)
                    scores = scores - peak
                expo = jnp.exp(scores)
                sums = jnp.sum(expo, axis=0, keepdims=True)
                prob = (expo * (1.0 / sums)).astype(bf16)
                out = dot(values_t[HD * j : HD * (j + 1)], prob)
                mixed[0, HD * j : HD * (j + 1), :] = out.astype(bf16)
                total[0, j : j + 1, :] = peak + jnp.log(sums)

    @pl.when(small)
    def _():
        heads(False)

    @pl.when(jnp.logical_not(small))
    def _():
        heads(True)


def middle_kernel(
    seqs,
    core,
    latents,
    upstream,
    mixed,
    mod,
    near,
    near_come,
    far,
    far_come,
    bias,
    cond,
    block_out,
    residual_back,
    mixed_back,
    keep,
    send,
    grad_late,
    small,
    proj,
    up,
    down,
    total,
    sums,
    bias_sums,
    second_s,
    act_s,
    pre_s,
    sems,
):
    seq, step = pl.program_id(0), pl.program_id(1)

    @pl.when((seq == 0) & (step == 0))
    def _():
        for half, ref, come in ((core[2, 0], near, near_come), (1 - core[2, 0], far, far_come)):
            at = pl.multiple_of(half * HALF, HALF)
            proj[pl.ds(at, HALF), :] = ref[0] + come[0]
            for n in range(FB):
                up[pl.ds(at, HALF), n * D : (n + 1) * D] = ref[1 + n] + come[1 + n]
                down[pl.ds(n * D + at, HALF), :] = ref[1 + FB + n] + come[1 + FB + n]
        total[...] = jnp.zeros_like(total)
        grad_late[...] = jnp.zeros_like(grad_late)
        bias_sums[...] = jnp.zeros_like(bias_sums)

    gate_one, shift_two, scale_two, gate_two = (mod[0, i : i + 1] for i in (2, 3, 4, 5))
    bias_up = bias[:, 4 * D : 4 * D + FF]

    def column(value):
        return jnp.sum(value, axis=0, keepdims=True)

    attn_out = dot(mixed[0], proj[...], TN) + bias[:, 3 * D : 4 * D]
    residual = latents[0].astype(f32) + gate_one * attn_out
    norm, inverse = normed(residual)
    second = (norm * (1.0 + scale_two) + shift_two).astype(bf16)
    second_s[...] = second
    ct = upstream[0].astype(f32)
    ffn_back = (ct * gate_two).astype(bf16)
    pre = dot(second, up[...]) + bias_up
    square = pre * pre
    k0 = 0.7978845608028654
    tanh = jnp.tanh(pre * (k0 + (k0 * 0.044715) * square))
    half = 0.5 + 0.5 * tanh
    act_s[...] = (pre * half).astype(bf16)
    slope = half + pre * (0.5 - 0.5 * tanh * tanh) * (k0 + (3.0 * k0 * 0.044715) * square)
    ffn_out = dot(act_s[...], down[...]) + bias[:, 4 * D + FF : 5 * D + FF]
    pre_back = (dot(ffn_back, down[...], NT) * slope).astype(bf16)
    pre_s[...] = pre_back
    low_pre = column(pre_back.astype(f32))
    second_back = dot(pre_back, up[...], NT)
    block_out[0] = (residual + gate_two * ffn_out).astype(bf16)
    res_back = ct + norm_back(second_back * (1.0 + scale_two), norm, inverse)
    residual_back[0] = res_back
    attn_back = (res_back * gate_one).astype(bf16)
    mixed_back[0] = dot(attn_back, proj[...], NT).astype(bf16)
    both = jnp.concatenate(
        [
            column(res_back * attn_out),
            column(second_back),
            column(second_back * norm),
            column(ct * ffn_out),
        ],
        axis=0,
    )
    bias_sums[...] += jnp.concatenate(
        [column(attn_back.astype(f32))]
        + [low_pre[:, n * D : (n + 1) * D] for n in range(FB)]
        + [column(ffn_back.astype(f32))],
        axis=0,
    )

    for n in range(seqs):
        @pl.when(seq == n)
        def _(n=n):
            sums[n] = jnp.where(step == 0, both, sums[n] + both)

    grad_late[0] += dot(mixed[0], attn_back)
    grad_up = dot(second_s[...], pre_s[...], TN)
    grad_down_t = dot(ffn_back, act_s[...], TN)
    side = core[2, 0] * FB
    for n in range(FB):
        cols = slice(n * D, (n + 1) * D)
        total[side + n] += grad_up[:, cols]
        total[FB - side + n] += grad_down_t[:, cols].T

    @pl.when((seq == pl.num_programs(0) - 1) & (step == pl.num_programs(1) - 1))
    def _():
        copies = [
            pltpu.make_async_copy(total.at[pl.ds(i * FB, FB)], out, sems.at[i])
            for i, out in enumerate((keep, send))
        ]
        for copy in copies:
            copy.start()
        rows = [jnp.concatenate([sums[n], cond[n : n + 1]], axis=0) for n in range(seqs)]
        rows.append(bias_sums[...])
        filled = seqs * 5 + FB + 2
        if small.shape[0] > filled:
            rows.append(jnp.zeros((small.shape[0] - filled, D), f32))
        small[...] = jnp.concatenate(rows, axis=0).astype(bf16)
        for copy in copies:
            copy.wait()


def attend_back_kernel(begin, first_pair, query, keys, values, back, total, first, *rest):
    grads_in, biases_in = rest[:2]
    back_query, back_keys, back_values, grads, biases = rest[-5:]
    pair = first_pair + pl.program_id(0)
    lane = lax.broadcasted_iota(jnp.int32, (1, 2 * HD), 1)
    keys_t = keys[0].T
    key_sum = value_sum = 0.0
    query_parts = []
    for h in range(2):
        one = jnp.where((lane < HD) == (h == 0), 1.0, 0.0).astype(bf16)
        q = query[0] * (one * HD**-0.5)
        g = back[0] * one
        prob = jnp.exp(dot(keys[0], q, NT) - total[0, pl.ds(2 * pair + h, 1)])
        prob_back = dot(values[0], g, NT)
        row_delta = jnp.sum(prob * prob_back, axis=0, keepdims=True)
        score_back = (prob * (prob_back - row_delta)).astype(bf16)
        value_sum = value_sum + dot(prob.astype(bf16), g)
        key_sum = key_sum + dot(score_back, q)
        query_parts.append(dot(keys_t[HD * h : HD * (h + 1)], score_back))
    low = (
        (jnp.concatenate(query_parts, axis=0) * HD**-0.5).T.astype(bf16),
        key_sum.astype(bf16),
        value_sum.astype(bf16),
    )
    for out, value in zip((back_query, back_keys, back_values), low):
        out[0] = value
    joined = jnp.concatenate(low, axis=1)
    new = dot(first[0], joined)
    sums = jnp.sum(joined.astype(f32), axis=0, keepdims=True)
    width = 2 * HD
    for i in range(3):
        cols = slice(i * width, (i + 1) * width)
        grads[i] = new[:, cols] if begin else grads_in[i] + new[:, cols]
        biases[i : i + 1] = sums[:, cols] if begin else biases_in[i : i + 1] + sums[:, cols]


def first_back_kernel(
    n, final, table, latents, residual_back, mod, back_query, back_keys, back_values, near, far, biases, *rest
):
    latents_grad, small, weight, sums = rest[-4:]

    @pl.when(pl.program_id(0) == 0)
    def _():
        join_halves(table[2, 0], near, far, weight)
        sums[...] = jnp.zeros_like(sums)

    norm, inverse = normed(latents[0].astype(f32))
    first_back = (
        dot(back_query[0], weight[0], NT)
        + dot(back_keys[0], weight[1], NT)
        + dot(back_values[0], weight[2], NT)
    )
    sums[0:1] += jnp.sum(first_back, axis=0, keepdims=True)
    sums[1:2] += jnp.sum(first_back * norm, axis=0, keepdims=True)
    latents_grad[0] = residual_back[0] + norm_back(
        first_back * (1.0 + mod[0, 1:2]), norm, inverse
    )

    @pl.when(pl.program_id(0) == pl.num_programs(0) - 1)
    def _():
        rows = [rest[0][: 2 * n]] if n else []
        rows.append(sums[0:2])
        if final:
            rows += [part.astype(f32) for part in split_two(biases[0:3])]
        filled = 2 * n + 2 + (6 if final else 0)
        rows.append(jnp.zeros((small.shape[0] - filled, D), f32))
        small[...] = jnp.concatenate(rows, axis=0).astype(small.dtype)


def split_two(value):
    high = value.astype(bf16)
    return high, (value - high.astype(f32)).astype(bf16)


def small_spec(half, rows):
    dims = (*half.shape[:-2], half.shape[-2] - rows, D)
    return whole(*dims)


def joined(near, far):
    return jnp.concatenate([near[...].reshape(-1, D), far[...].reshape(-1, D)], axis=0)


def chosen_rows(rows, count, seqs, me, group, per, kind):
    latent = lax.broadcasted_iota(jnp.int32, (count, rows.shape[0]), 0)
    wanted = (latent // seqs ^ me) * group + latent % seqs * per + kind
    hit = wanted == lax.broadcasted_iota(jnp.int32, (count, rows.shape[0]), 1)
    return dot(jnp.where(hit, 1.0, 0.0).astype(bf16), rows)


def finish(seqs, group, soon_group, last_group, me, soon, last, inputs, outs):
    ada, bias, one, two = inputs
    grad_out, one_out, two_out, bias_out, *cond_outs = outs
    devices = soon.shape[0] // soon_group

    def totals(rows, each_group, kinds):
        count = len(kinds) * devices
        at = lax.broadcasted_iota(jnp.int32, (count, rows.shape[0]), 0)
        first = kinds[0]
        assert list(kinds) == list(range(first, first + len(kinds)))
        wanted = (at % devices ^ me) * each_group + at // devices + first
        hit = wanted == lax.broadcasted_iota(jnp.int32, (count, rows.shape[0]), 1)
        found = dot(jnp.where(hit, 1.0, 0.0).astype(bf16), rows)
        return [
            jnp.sum(found[k * devices : (k + 1) * devices], axis=0, keepdims=True)
            for k in range(len(kinds))
        ]

    of_soon = totals(soon, soon_group, range(0, seqs * 5 + FB + 2))
    of_last = totals(last, last_group, range(0, seqs * 2 + 6))
    qkv = [of_last[seqs * 2 + i] + of_last[seqs * 2 + 3 + i] for i in range(3)]
    mods = [sum(of_last[n * 2 + i] for n in range(seqs)) for i in range(2)]
    mods += [sum(of_soon[n * 5 + i] for n in range(seqs)) for i in range(4)]
    grad = jnp.concatenate(qkv + of_soon[seqs * 5 : seqs * 5 + FB + 2] + mods, axis=1)
    grad = grad.reshape(-1)
    grad_out[...] = grad
    one_new = 0.9 * one[...] + 0.1 * grad
    two_new = 0.95 * two[...] + 0.05 * grad * grad
    one_out[...] = one_new
    two_out[...] = two_new
    corrected = (
        one_new / (1.0 - 0.9**STEP) / (jnp.sqrt(two_new / (1.0 - 0.95**STEP)) + 1e-08)
    )
    bias_out[...] = bias[...] - adam_rate * (corrected + adam_decay * bias[...])
    for g, device in enumerate(group):
        total = 0.0
        for b in range(ada.shape[0]):
            rows, each_group, per, kind = (
                (last, last_group, 2, b) if b < 2 else (soon, soon_group, 5, b - 2)
            )
            base = device * each_group
            mine = jnp.concatenate(
                [rows[base + n * per + kind : base + n * per + kind + 1] for n in range(seqs)]
                + [jnp.zeros((8 - seqs, D), bf16)],
                axis=0,
            )
            total = total + dot(mine, ada[b], NT)
        cond_outs[g][...] = total[:seqs]


def slots_kernel(
    row, begin, room, pieces, stages, line, small, extra, table, *refs
):
    cond_halves, mod_halves, (near, far) = refs[:2], refs[2:4], refs[4:6]
    state, refs = refs[6:11], refs[11:]
    more_in, refs = refs[: 4 if extra else 0], refs[4 if extra else 0 :]
    ends = len(refs) - 5 - (4 + len(extra) if extra else 0)
    more_out, refs = refs[ends:-5], refs[:ends] + refs[-5:]
    outs = refs[-9:-5]
    held, gradient_in, made, in_sems, out_sems = refs[-5:]
    cond_group, mod_group, per, seqs = small
    rows = D // pieces
    count = jnp.int32(0)
    for i in range(room):
        count = count + (table[row + 1, begin + i] > 0).astype(jnp.int32)

    def piece(half, i, p, buf):
        shard = table[row + 2, begin + i] * pieces + p
        at = ((shard // line & 3) ^ table[2, 1], (shard & 3) ^ table[2, 2])[:stages]
        return pltpu.make_async_copy(
            half.at[(*at, pl.ds(half.shape[-2] - rows, rows))],
            gradient_in.at[buf, pl.ds(p * rows, rows)],
            in_sems.at[buf, 5 + p],
        )

    def arriving(i, k, buf):
        return pltpu.make_async_copy(
            state[k].at[table[row, begin + i]], held.at[buf, k], in_sems.at[buf, k]
        )

    def leaving(i, k, buf):
        return pltpu.make_async_copy(
            made.at[buf, k], outs[k].at[table[row, begin + i]], out_sems.at[buf, k]
        )

    def fetch(i, buf):
        side = (table[row + 2, begin + i] * pieces // (4 * line)) ^ table[2, 0]
        for number, half in enumerate((near, far)):
            @pl.when((table[row + 1, begin + i] == 1) & (side == number))
            def _(half=half):
                for p in range(pieces):
                    piece(half, i, p, buf).start()

        for k in (2, 3, 4, 0, 1):
            arriving(i, k, buf).start()

    @pl.when(count > 0)
    def _():
        fetch(0, 0)

    if extra:
        finish(
            seqs,
            extra,
            cond_group,
            mod_group,
            table[2, 3],
            joined(*cond_halves),
            joined(*mod_halves),
            more_in,
            more_out,
        )

    def one(i, carry):
        buf = i & 1
        kind = table[row + 1, begin + i]

        @pl.when(i + 1 < count)
        def _():
            fetch(i + 1, 1 - buf)

        @pl.when(i >= 2)
        def _():
            for k in range(4):
                leaving(i - 2, k, buf).wait()

        @pl.when(kind == 1)
        def _():
            for p in range(pieces):
                piece(near, i, p, buf).wait()
            made[buf, 0] = gradient_in[buf].astype(f32)

        @pl.when(kind == 2)
        def _():
            conds, mods = joined(*cond_halves), joined(*mod_halves)
            total = conds.shape[0] // cond_group * seqs
            me, block = table[2, 3], table[row + 2, begin + i]
            cond = chosen_rows(conds, total, seqs, me, cond_group, 5, 4).astype(bf16)
            mod = chosen_rows(mods, total, seqs, me, mod_group, per, block).astype(bf16)
            made[buf, 0] = dot(cond, mod, TN)

        @pl.when(kind == 3)
        def _():
            made[buf, 0] = jnp.zeros((D, D), f32)

        leaving(i, 0, buf).start()
        low = made[buf, 0].astype(bf16)
        arriving(i, 2, buf).wait()
        turned = low.T
        two = dot(jnp.concatenate([held[buf, 2].astype(bf16), turned], axis=0), low)
        arriving(i, 3, buf).wait()
        direction = dot(two[:D].astype(bf16), held[buf, 3].astype(bf16))
        arriving(i, 4, buf).wait()
        weight = held[buf, 4]
        scale = jnp.sqrt(jnp.mean(weight * weight) + norm_eps) * lax.rsqrt(
            jnp.mean(direction * direction) + norm_eps
        )
        made[buf, 3] = weight - shampoo_rate * (scale * direction + shampoo_decay * weight)
        leaving(i, 3, buf).start()
        arriving(i, 0, buf).wait()
        made[buf, 1] = 0.5 * held[buf, 0] + 0.5 * dot(low, turned)
        leaving(i, 1, buf).start()
        arriving(i, 1, buf).wait()
        made[buf, 2] = 0.5 * held[buf, 1] + 0.5 * two[D:]
        leaving(i, 2, buf).start()
        return carry

    lax.fori_loop(0, count, one, 0)
    for back in (2, 1):
        @pl.when(count >= back)
        def _(back=back):
            for k in range(4):
                leaving(count - back, k, (count - back) & 1).wait()


def slots_call(row, begin, steps, table, small, gathered, rows, state, outs, ties, name, finishing=None):
    slots = state[0].shape[0]
    pieces = D // rows
    stages = gathered[0].ndim - 2
    line = gathered[0].shape[1] if stages > 1 else 1
    conds, mods, cond_rows, *small = small
    given = [] if outs is None else list(outs)
    anyplace = pl.BlockSpec(memory_space=pl.ANY)
    group, more_in = finishing or (None, ())
    more = given + list(ties)
    more_out = [shape(v.shape) for v in more_in[1:2] * 4]
    if finishing:
        more_out += [shape((small[-1], D))] * len(group)
    return pl.pallas_call(
        functools.partial(slots_kernel, row, begin, steps, pieces, stages, line, small, group),
        grid=(1,),
        in_specs=[pl.BlockSpec(memory_space=pltpu.SMEM)]
        + [small_spec(half, cond_rows) for half in conds]
        + [small_spec(half, rows) for half in mods]
        + [anyplace] * 7
        + [whole(*v.shape) for v in more_in]
        + [anyplace] * len(more),
        out_specs=[anyplace] * 4 + [whole(*v.shape) for v in more_out],
        out_shape=[shape((slots, D, D))] * 4 + more_out,
        scratch_shapes=[
            pltpu.VMEM((2, 5, D, D), f32),
            pltpu.VMEM((2, D, D), bf16),
            pltpu.VMEM((2, 4, D, D), f32),
            pltpu.SemaphoreType.DMA((2, 5 + pieces)),
            pltpu.SemaphoreType.DMA((2, 4)),
        ],
        input_output_aliases={12 + len(more_in) + i: i for i in range(len(given))},
        compiler_params=params(),
        cost_estimate=cost(steps * 7 * 2 * D**3, steps * 10 * D * D * 4),
        name=name,
    )(table, *conds, *mods, *gathered, *state, *more_in, *more)


def whole(*dims):
    return pl.BlockSpec(dims, lambda *_: (0,) * len(dims))


def each(*dims):
    return pl.BlockSpec((1,) + dims, lambda i, *_: (i,) + (0,) * len(dims))


def middle(rows, table, latents, cotangent, mixed, modulation, rest, bias_row, cond, small_rows):
    seqs, length, _ = latents.shape
    tok = pl.BlockSpec((1, rows, D), lambda i, j: (i, j, 0))
    anyplace = pl.BlockSpec(memory_space=pl.ANY)
    return pl.pallas_call(
        functools.partial(middle_kernel, seqs),
        grid=(seqs, length // rows),
        in_specs=[
            pl.BlockSpec(memory_space=pltpu.SMEM),
            tok,
            tok,
            pl.BlockSpec((1, D, rows), lambda i, j: (i, 0, j)),
            each(6, D),
            *[whole(1 + EARLY, HALF, D)] * 4,
            whole(*bias_row.shape),
            whole(*cond.shape),
        ],
        out_specs=[
            tok,
            tok,
            tok,
            anyplace,
            anyplace,
            pl.BlockSpec((1, D, D), lambda *_: (LATE - 1, 0, 0)),
            whole(small_rows, D),
        ],
        out_shape=[
            shape((seqs, length, D), bf16),
            shape((seqs, length, D)),
            shape((seqs, length, D), bf16),
            shape((FB, D, D)),
            shape((FB, D, D)),
            shape((LATE, D, D)),
            shape((small_rows, D), bf16),
        ],
        scratch_shapes=[
            pltpu.VMEM((D, D), bf16),
            pltpu.VMEM((D, FF), bf16),
            pltpu.VMEM((FF, D), bf16),
            pltpu.VMEM((2 * FB, D, D), f32),
            pltpu.VMEM((seqs, 4, D), f32),
            pltpu.VMEM((FB + 2, D), f32),
            pltpu.VMEM((rows, D), bf16),
            pltpu.VMEM((rows, FF), bf16),
            pltpu.VMEM((rows, FF), bf16),
            pltpu.SemaphoreType.DMA((2,)),
        ],
        compiler_params=params(),
        cost_estimate=cost(22e9, 25e6, 3e6),
        name="middle",
    )(table, latents, cotangent, mixed, modulation, *rest, bias_row, cond)


def per_device(
    net,
    latents,
    condition,
    cotangent,
    owner,
    master,
    stat_left,
    stat_right,
    root_left,
    root_right,
    bias,
    moment_one,
    moment_two,
):
    slots = master.shape[0]
    seqs, length, _ = latents.shape
    blocks = owner.shape[0]
    first_ada = LATE + EARLY
    ada = blocks - first_ada
    own_all = net.own_list()
    steps_last = min(slots, 2 + LATE)
    anyplace = pl.BlockSpec(memory_space=pl.ANY)
    smem = pl.BlockSpec(memory_space=pltpu.SMEM)
    tok = each(length, D)
    soon_rows = -(-(seqs * 5 + FB + 2) // 16) * 16
    last_rows = -(-(seqs * 2 + 2 * 3) // 16) * 16

    seat = jnp.stack(
        [net.place(bits) for bits in net.stages]
        + [net.place(net.digits()), lax.axis_index("own").astype(jnp.int32)]
    )
    cuts = [0, max(1, slots // 5), max(2, slots // 2), slots]
    table = make_plan(owner, seat, slots, cuts, steps_last)

    near_qkv = pick_blocks(table, master, list(range(3)), HALF)
    own_ada = pick_blocks(table, master, list(range(first_ada, blocks)), D)
    near_rest = pick_blocks(table, master, list(range(3, first_ada)), HALF)
    for bit in own_all:
        near_qkv = near_qkv + tie(net.swap(near_qkv, [bit], 1), near_rest)
    far_qkv = net.swap(near_qkv, net.stages[0], 1)

    bias_row = bias.reshape(1, -1)
    cond_float = condition.astype(f32)
    silu_cond, silu_pull = jax.vjp(jax.nn.silu, cond_float)
    cond_low = silu_cond.astype(bf16)
    cond_group = net.gather(cond_low, own_all)
    mod_parts = jnp.einsum("gld,bde->glbe", cond_group, own_ada, preferred_element_type=f32)
    modulation = mod_parts[0]
    mods_come = [net.swap(mod_parts[g], own_all, g) for g in range(1, net.n_own)]
    for come in mods_come:
        modulation = modulation + come
    modulation = modulation + bias[5 * D + FF :].reshape(ada, D)

    near_rest = tie(near_rest, near_qkv, *mods_come)
    for bit in own_all[:-1]:
        near_rest = near_rest + net.swap(near_rest, [bit], 1)
    far_rest = net.swap(near_rest, net.stages[0], 1)
    near_come = net.swap(near_rest, own_all[-1:], 1)

    qkv, mixed, totals, first_in = pl.pallas_call(
        attend_kernel,
        grid=(seqs,),
        in_specs=[
            smem,
            tok,
            each(6, D),
            whole(3, HALF, D),
            whole(3, HALF, D),
            whole(*bias_row.shape),
        ],
        out_specs=[each(length, 3 * D), each(D, length), each(8, length), each(D, length)],
        out_shape=[
            shape((seqs, length, 3 * D), bf16),
            shape((seqs, D, length), bf16),
            shape((seqs, 8, length)),
            shape((seqs, D, length), bf16),
        ],
        scratch_shapes=[pltpu.VMEM((3, D, D), bf16)],
        compiler_params=params(),
        cost_estimate=cost(16e9, 12e6, 12e6),
        name="attend",
    )(table, latents, modulation, near_qkv, far_qkv, bias_row)

    near_come = tie(near_come, qkv)
    rest = (near_rest, near_come, far_rest, net.swap(near_come, net.stages[0], 1))

    (
        block_out,
        residual_back,
        mixed_back,
        early_keep,
        early_send,
        grad_late,
        small_soon,
    ) = middle(
        length,
        table,
        latents,
        cotangent,
        mixed,
        modulation,
        rest,
        bias_row,
        cond_low.astype(f32),
        soon_rows,
    )

    def core_stage(grads, *others):
        return net.scatter_sum(grads.reshape(2, -1, D), net.stages[0], f32, *others)

    def plane_stage(value, *others):
        return net.scatter_sum(value.reshape(4, -1, D), net.stages[1], bf16, *others)

    def line_stage(value, *others):
        value = net.scatter_sum(value.reshape(4, -1, D), net.stages[2], bf16, *others)
        for bits in net.rest:
            value = net.add_up(value, bits)
        return value.astype(bf16)

    def with_small(value, small):
        for bits in net.rest[::-1]:
            small = net.gather(small, bits)
        return jnp.concatenate([small.reshape(-1, D), value], axis=0)

    def line_exchange(value, small, others):
        sent = with_small(value.astype(bf16), small)
        rows = sent.shape[0] - value.shape[0]
        got = net.gather(sent, net.stages[2], *others)
        value = (got[0, rows:].astype(f32) + got[1, rows:]) + (got[2, rows:].astype(f32) + got[3, rows:])
        for bits in net.rest:
            value = net.add_up(value, bits)
        return jnp.concatenate([got[:, :rows].reshape(-1, D), value.astype(bf16)], axis=0)

    def back_pairs(n, first_pair, count, carried, ties):
        def head(offset):
            return pl.BlockSpec((1, length, 2 * HD), lambda i: (n, 0, offset + first_pair + i))

        def latent(*dims):
            return pl.BlockSpec((1,) + dims, lambda i: (n, 0, 0))

        begin = n == 0
        grad_spec = pl.BlockSpec((3, D, 2 * HD), lambda i: (0, 0, first_pair + i))
        bias_spec = pl.BlockSpec((8, 2 * HD), lambda i: (0, first_pair + i))
        return pl.pallas_call(
            functools.partial(attend_back_kernel, begin, first_pair),
            grid=(count,),
            in_specs=[head(0), head(3), head(6), head(0), latent(8, length), latent(D, length)]
            + ([anyplace] * 2 if begin else [grad_spec, bias_spec])[: len(carried)]
            + [anyplace] * (len(carried[2:]) + len(ties)),
            out_specs=[head(0)] * 3 + [grad_spec, bias_spec],
            out_shape=[shape((seqs, length, D), bf16)] * 3 + [shape((LATE, D, D)), shape((8, D))],
            input_output_aliases={6 + i: at for i, at in enumerate((3, 4, 0, 1, 2)[: len(carried)])},
            compiler_params=params(),
            cost_estimate=cost(count * 7e9, count * 3e6, count * 2e6),
            name="attend_back",
        )(qkv, qkv, qkv, mixed_back, totals, first_in, *carried, *ties)

    def first_back(n, backs, carried, ties):
        rows = length // 2
        final = n == seqs - 1
        part = pl.BlockSpec((1, rows, D), lambda i: (n, i, 0))
        grad, small = carried if carried else (None, None)
        more = ([small, grad] if n else []) + ties
        specs = ([whole(*small.shape), anyplace] if n else []) + [anyplace] * len(ties)
        return pl.pallas_call(
            functools.partial(first_back_kernel, n, final),
            grid=(2,),
            in_specs=[smem, part, part, pl.BlockSpec((1, 6, D), lambda i: (n, 0, 0))]
            + [part] * 3
            + [whole(3, HALF, D)] * 2
            + [whole(8, D)]
            + specs,
            out_specs=[part, whole(last_rows, D)],
            out_shape=[
                shape((seqs, length, D)),
                shape((last_rows, D), bf16 if final else f32),
            ],
            input_output_aliases={11: 0} if n else {},
            scratch_shapes=[pltpu.VMEM((3, D, D), bf16), pltpu.VMEM((8, D), f32)],
            compiler_params=params(),
            cost_estimate=cost(3.5e9, 9e6),
            name="first_back",
        )(
            table,
            latents,
            residual_back,
            modulation,
            *backs[:3],
            near_qkv,
            far_qkv,
            backs[4],
            *more,
        )

    def swapped(backs):
        return [backs[3], backs[4], *backs[:3]]

    early = early_keep
    stages = [
        lambda value: value + net.swap(early_send, net.stages[0], 1),
        plane_stage,
        lambda value: with_small(line_stage(value), small_soon),
        lambda value: net.gather(value, net.stages[2]),
    ]
    def after_stage(*others):
        nonlocal early
        if stages:
            early = stages.pop(0)(early)
            return [early, *others]
        return list(others)

    backs = [None] * 3 + [grad_late]
    firsts = []
    for n in range(seqs):
        for first_pair, count in ((0, 1), (1, 2)):
            if n + first_pair == 0:
                carried, ties = [grad_late], []
            else:
                carried = swapped(backs)
                ties = after_stage(*(firsts[:1] if first_pair == 0 else []))
            backs = back_pairs(n, first_pair, count, carried, ties)
        if n < seqs - 1:
            firsts = first_back(n, backs, firsts, after_stage())
    for stage in stages:
        early = stage(early)
    pieces = [net.swap(early, net.stages[1], g) for g in range(1, 4)]
    pieces, grad_late = tie((pieces, backs[3]), backs[0])
    early = jnp.stack([early] + pieces)
    latents_grad, small_last = first_back(seqs - 1, backs, firsts, [])
    late = core_stage(grad_late, latents_grad)
    early = (early, net.swap(early, net.stages[0], 1))
    early_rows = EARLY * D // 32
    late_rows = LATE * D // 8
    state = (stat_left, stat_right, root_left, root_right, master)
    def soon_slots(i, outs, ties):
        return slots_call(
            3,
            cuts[i],
            cuts[i + 1] - cuts[i],
            table,
            (early, early, early_rows, soon_rows, soon_rows, 5, seqs),
            early,
            early_rows,
            state,
            outs,
            ties,
            "soon_slots",
        )

    outs = soon_slots(0, None, [late])
    late = plane_stage(late, *outs)
    outs = soon_slots(1, outs, [late])
    late = line_exchange(late, small_last, outs)
    outs = soon_slots(2, outs, [late])
    late = net.gather(late, net.stages[1], *outs)
    late = (late, net.swap(late, net.stages[0], 1))
    group = []
    for g in range(net.n_own):
        group.append(
            sum(1 << k for k, (axis, bit) in enumerate(net.digits()) if axis == "own" and g & bit)
        )

    weight_grads, left_new, right_new, master_new, *others = slots_call(
        6,
        0,
        steps_last,
        table,
        (early, late, early_rows, soon_rows, last_rows, 2, seqs),
        late,
        late_rows,
        state,
        outs,
        [],
        "last_slots",
        (group, (own_ada, bias, moment_one, moment_two)),
    )
    bias_grad, moment_one_new, moment_two_new, bias_new, *cond_parts = others

    back_cond = cond_parts[0]
    for g in range(1, net.n_own):
        back_cond = back_cond + net.swap(cond_parts[g], own_all, g)
    condition_grad = silu_pull(back_cond)[0]
    return (
        block_out,
        latents_grad,
        condition_grad,
        weight_grads,
        left_new,
        right_new,
        master_new,
        bias_grad,
        moment_one_new,
        moment_two_new,
        bias_new,
    )


def solution(mesh):
    net = Net(mesh.shape["dp"], mesh.shape["own"])
    token = P(("dp", "own"), None, None)
    slot = P("own", None, None)
    return jax.shard_map(
        functools.partial(per_device, net),
        mesh=mesh,
        in_specs=(token, P(("dp", "own"), None), token, P()) + (slot,) * 5 + (P(),) * 3,
        out_specs=(token, token, P(("dp", "own"), None)) + (slot,) * 4 + (P(),) * 4,
        check_vma=False,
    )
```
